128 devices in a mesh: dp: 16 (over z_hi, y, core), ctx: 8 (over z_lo, x).
Axes of the slice: x: 4, y: 4, z: 4 (z_hi: 2, z_lo: 2; z = z_hi * 2 + z_lo), core: 2. Of those that a mesh axis runs over, the one named last changes fastest.
Arguments:
- inputs: bfloat16 [16, 2048, 960], P('dp', 'ctx'), may hold values from -6 to 6
- cotangent: bfloat16 [16, 2048, 960], P('dp', 'ctx'), may hold values from -6 to 6
- span_order: int32 [16], replicated, may hold values from 0 to 15, each once
- w_qkv: float32 [960, 1600], P('ctx'), may hold values from -0.1875 to 0.1875
- qkv_first: float32 [960, 1600], P('ctx'), may hold values from -128 to 128
- qkv_second: float32 [960, 1600], P('ctx'), may hold values from 983.04 to 9830.4
- w_proj: float32 [960, 960], P('ctx'), may hold values from -0.5 to 0.5
- proj_first: float32 [960, 960], P('ctx'), may hold values from -48 to 48
- proj_second: float32 [960, 960], P('ctx'), may hold values from 157.2864 to 1572.864
- w_expand: float32 [960, 5120], P('ctx'), may hold values from -0.1875 to 0.1875
- expand_first: float32 [960, 5120], P('ctx'), may hold values from -48 to 48
- expand_second: float32 [960, 5120], P('ctx'), may hold values from 157.2864 to 1572.864
- w_down: float32 [2560, 960], P('ctx'), may hold values from -0.125 to 0.125
- down_first: float32 [2560, 960], P('ctx'), may hold values from -64 to 64
- down_second: float32 [2560, 960], P('ctx'), may hold values from 353.8944 to 3538.944
- gains: float32 [2, 960], P(None, 'ctx'), may hold values from 0.5 to 1.5
- gains_first: float32 [2, 960], P(None, 'ctx'), may hold values from -128 to 128
- gains_second: float32 [2, 960], P(None, 'ctx'), may hold values from 983.04 to 9830.4
Outputs:
- output: bfloat16 [16, 2048, 960], P('dp', 'ctx')
- input_grad: bfloat16 [16, 2048, 960], P('dp', 'ctx')
- new_qkv: float32 [960, 1600], P('ctx')
- qkv_mean: float32 [960, 1600], P('ctx')
- qkv_square: float32 [960, 1600], P('ctx')
- new_proj: float32 [960, 960], P('ctx')
- proj_mean: float32 [960, 960], P('ctx')
- proj_square: float32 [960, 960], P('ctx')
- new_expand: float32 [960, 5120], P('ctx')
- expand_mean: float32 [960, 5120], P('ctx')
- expand_square: float32 [960, 5120], P('ctx')
- new_down: float32 [2560, 960], P('ctx')
- down_mean: float32 [2560, 960], P('ctx')
- down_square: float32 [2560, 960], P('ctx')
- new_gains: float32 [2, 960], P(None, 'ctx')
- gains_mean: float32 [2, 960], P(None, 'ctx')
- gains_square: float32 [2, 960], P(None, 'ctx')
The draws below stay inside these ranges and needn't reach their ends.
Inputs may be any that keep to these rules, and one draw needn't show every extreme that they name: Layout block r of every sequence is sequence block span_order[r] of 128 tokens; each number appears once.
All inputs are finite; a program needn't handle non-finite values.
Results may differ from the reference program's by a relative error of at most 0.015.
Values may be sent and summed in bfloat16 or wider, within the bound.
No kernel may reach another device: no remote copies, remote signals or barrier semaphores. Data moves between devices by JAX's collectives and lax.ppermute only.
A program may use at most 320 MiB of HBM per device.

```python
import math
from functools import partial
import jax
import jax.numpy as jnp
from jax import lax

D = 960
HEADS = 15
KV_HEADS = 5
HEAD_DIM = 64
FF = 2560
STEP = 10
LENGTH = 2048
SEQS = 16
TOKENS = 32768
SPANS = 16
SPAN = 128
QKVW = 1600


def levels(own_key, dims, split, least, largest):
    level = 1.0
    for axis_at, shards_of in split:
        draws = jax.random.uniform(jax.random.fold_in(jax.random.fold_in(own_key, 6), axis_at), (shards_of,), jnp.float32, least / len(split), largest / len(split))
        level = level * jnp.repeat(jnp.exp(draws), dims[axis_at] // shards_of).reshape((-1,) + (1,) * (len(dims) - 1 - axis_at))
    return level


def scatter_about(stream_key, shape, width, bound, split=(), held_as=jnp.bfloat16):
    entries = jax.random.normal(stream_key, shape, jnp.float32) * width
    if len(split) > 0:
        entries = levels(stream_key, shape, split, -0.22, 0.18) * entries
    return jnp.clip(entries, min=-bound, max=bound).astype(held_as)


def setup_inputs(seed: int = 0) -> dict:
    seeds = jax.random.split(jax.random.key(seed), 19)
    inputs = scatter_about(seeds[0], (SEQS, LENGTH, D), 1.0, 6.0, ((0, 16), (1, 8)))
    cotangent = scatter_about(seeds[1], (SEQS, LENGTH, D), 1.0, 6.0, ((0, 16), (1, 8)))
    span_order = jax.random.permutation(seeds[2], SPANS).astype(jnp.int32)
    w_qkv = scatter_about(seeds[3], (D, QKVW), D ** -0.5, 0.1875, ((0, 8),), jnp.float32)
    qkv_first = scatter_about(seeds[4], (D, QKVW), (0.11 * TOKENS ** 0.5), 128.0, ((0, 8),), jnp.float32)
    qkv_second = jnp.clip(jnp.exp(math.log(9830.4) - 2.3025852 * jax.random.uniform(seeds[5], (D, QKVW), jnp.float32) ** levels(seeds[5], (D, QKVW), ((0, 8),), -0.2, 0.2)), 983.04, 9830.4)
    w_proj = scatter_about(seeds[6], (D, D), (D // 8) ** -0.5, 0.5, ((0, 8),), jnp.float32)
    proj_first = scatter_about(seeds[7], (D, D), (0.044 * TOKENS ** 0.5), 48.0, ((0, 8),), jnp.float32)
    proj_second = jnp.clip(jnp.exp(math.log(1572.864) - 2.3025851 * jax.random.uniform(seeds[8], (D, D), jnp.float32) ** levels(seeds[8], (D, D), ((0, 8),), -0.2, 0.2)), 157.2864, 1572.864)
    w_expand = scatter_about(seeds[9], (D, 2 * FF), D ** -0.5, 0.1875, ((0, 8),), jnp.float32)
    expand_first = scatter_about(seeds[10], (D, 2 * FF), (0.044 * TOKENS ** 0.5), 48.0, ((0, 8),), jnp.float32)
    expand_second = jnp.clip(jnp.exp(math.log(1572.864) - 2.3025851 * jax.random.uniform(seeds[11], (D, 2 * FF), jnp.float32) ** levels(seeds[11], (D, 2 * FF), ((0, 8),), -0.2, 0.2)), 157.2864, 1572.864)
    w_down = scatter_about(seeds[12], (FF, D), FF ** -0.5, 0.125, ((0, 8),), jnp.float32)
    down_first = scatter_about(seeds[13], (FF, D), (0.066 * TOKENS ** 0.5), 64.0, ((0, 8),), jnp.float32)
    down_second = jnp.clip(jnp.exp(math.log(3538.944) - 2.3025851 * jax.random.uniform(seeds[14], (FF, D), jnp.float32) ** levels(seeds[14], (FF, D), ((0, 8),), -0.2, 0.2)), 353.8944, 3538.944)
    gains = jnp.clip(1.0 + 0.1 * jax.random.normal(seeds[15], (2, D), jnp.float32), 0.5, 1.5)
    gains_first = scatter_about(seeds[16], (2, D), (0.11 * TOKENS ** 0.5), 128.0, ((1, 8),), jnp.float32)
    gains_second = jnp.clip(jnp.exp(math.log(9830.4) - 2.3025852 * jax.random.uniform(seeds[17], (2, D), jnp.float32) ** levels(seeds[17], (2, D), ((1, 8),), -0.2, 0.2)), 983.04, 9830.4)
    return dict(inputs=inputs, cotangent=cotangent, span_order=span_order, w_qkv=w_qkv, qkv_first=qkv_first, qkv_second=qkv_second, w_proj=w_proj, proj_first=proj_first, proj_second=proj_second, w_expand=w_expand, expand_first=expand_first, expand_second=expand_second, w_down=w_down, down_first=down_first, down_second=down_second, gains=gains, gains_first=gains_first, gains_second=gains_second)


@jax.custom_vjp
def low(v):
    return lax.optimization_barrier(v.astype(jnp.bfloat16)).astype(jnp.float32)

@jax.custom_vjp
def low_back(v):
    return v

def low_keep(v):
    return (low(v), None)

def low_pass(kept, grad):
    return (grad,)

def back_keep(v):
    return (v, None)

def back_low(kept, grad):
    return (low(grad),)
low.defvjp(low_keep, low_pass)
low_back.defvjp(back_keep, back_low)
eps = 1e-05
rope_base = 100000.0
beta_first = 0.9
beta_second = 0.95
adam_eps = 1e-08
highest = lax.Precision.HIGHEST

def rope_tables(positions):
    halfway = HEAD_DIM // 2
    freqs = rope_base ** (-(jnp.arange(halfway, dtype=jnp.float32) * 2.0) / HEAD_DIM)
    angles = positions.astype(jnp.float32)[:, None] * freqs[None, :]
    return (jnp.cos(angles), jnp.sin(angles))

def rotate(field, cosine, sine):
    halfway = field.shape[-1] // 2
    first = field[..., :halfway]
    second = field[..., halfway:]
    cosine = cosine[:, None, :]
    sine = sine[:, None, :]
    return jnp.concatenate([first * cosine - second * sine, second * cosine + first * sine], axis=-1)

def attend_block(keys, values, key_pos, block):
    queries, query_pos = block
    scores = jnp.einsum('qkgd,skd->kgqs', queries, keys, precision=highest) * HEAD_DIM ** (-0.5)
    scores = low_back(scores)
    visible = key_pos[None, :] <= query_pos[:, None]
    masked = jnp.where(visible, scores, -1e+30)
    probs = low(jax.nn.softmax(masked, axis=-1))
    return jnp.einsum('kgqs,skd->qkgd', probs, values, precision=highest)

def rms_scale(rows):
    return lax.rsqrt(lax.optimization_barrier(jnp.mean(rows * rows, axis=-1, keepdims=True)) + eps)

def forward(inputs, w_qkv, w_proj, w_expand, w_down, gains, positions):
    cosine, sine = rope_tables(positions)
    kv_width = KV_HEADS * HEAD_DIM
    group = HEADS // KV_HEADS
    normed = low(inputs * rms_scale(inputs) * gains[0])
    mixed = low_back(jnp.dot(normed, w_qkv, precision=highest))
    queries = mixed[:, :D].reshape(LENGTH, HEADS, HEAD_DIM)
    keys = mixed[:, D:D + kv_width].reshape(LENGTH, KV_HEADS, HEAD_DIM)
    values = mixed[:, D + kv_width:].reshape(LENGTH, KV_HEADS, HEAD_DIM)
    queries = low(rotate(queries, cosine, sine))
    keys = low(rotate(keys, cosine, sine))
    values = low(values)
    block = min(512, LENGTH)
    grouped = queries.reshape(LENGTH // block, block, KV_HEADS, group, HEAD_DIM)
    pos_blocks = positions.reshape(LENGTH // block, block)
    attended = lax.map(jax.checkpoint(partial(attend_block, keys, values, positions)), (grouped, pos_blocks))
    attended = low_back(low(attended.reshape(LENGTH, D)))
    branch = low_back(jnp.dot(attended, w_proj, precision=highest))
    middle = inputs + branch
    normed_two = low(middle * rms_scale(middle) * gains[1])
    expanded = low_back(jnp.dot(normed_two, w_expand, precision=highest))
    hidden = low(jax.nn.silu(expanded[:, :FF]) * expanded[:, FF:])
    return middle + jnp.dot(hidden, w_down, precision=highest)

def adam_step(master, first, second, grad, rate, decay):
    new_first = beta_first * first + (1.0 - beta_first) * grad
    new_second = beta_second * second + (1.0 - beta_second) * grad * grad
    fix_one = 1.0 - beta_first ** STEP
    fix_two = 1.0 - beta_second ** STEP
    update = new_first / fix_one / (jnp.sqrt(new_second / fix_two) + adam_eps) + decay * master
    return (master - rate * update, new_first, new_second)

def reference(inputs, cotangent, span_order, w_qkv, qkv_first, qkv_second, w_proj, proj_first, proj_second, w_expand, expand_first, expand_second, w_down, down_first, down_second, gains, gains_first, gains_second):
    rows = jnp.arange(LENGTH, dtype=jnp.int32)
    positions = (jnp.take(span_order, rows // SPAN) * SPAN + rows % SPAN).astype(jnp.int32)
    weights = (low(w_qkv), low(w_proj), low(w_expand), low(w_down), low(gains))

    def one_sequence(carry, pair):
        seq_in, seq_back = pair

        def layer(layer_in, mat_qkv, mat_proj, mat_expand, mat_down, gain_rows):
            return forward(layer_in, mat_qkv, mat_proj, mat_expand, mat_down, gain_rows, positions)
        result, pullback = jax.vjp(layer, seq_in.astype(jnp.float32), *weights)
        grads = pullback(seq_back.astype(jnp.float32))
        summed = tuple((total + piece for total, piece in zip(carry, grads[1:])))
        return (summed, (result.astype(jnp.bfloat16), grads[0].astype(jnp.bfloat16)))
    zeros = tuple((jnp.zeros(weight.shape, jnp.float32) for weight in weights))
    totals, (output, input_grad) = lax.scan(one_sequence, zeros, (inputs, cotangent))
    new_qkv, qkv_mean, qkv_square = adam_step(w_qkv, qkv_first, qkv_second, totals[0], 2.0 * D ** (-0.5), 0.1)
    new_proj, proj_mean, proj_square = adam_step(w_proj, proj_first, proj_second, totals[1], 2.0 * (D // 8) ** (-0.5), 0.1)
    new_expand, expand_mean, expand_square = adam_step(w_expand, expand_first, expand_second, totals[2], 2.0 * D ** (-0.5), 0.1)
    new_down, down_mean, down_square = adam_step(w_down, down_first, down_second, totals[3], 2.0 * FF ** (-0.5), 0.1)
    new_gains, gains_mean, gains_square = adam_step(gains, gains_first, gains_second, totals[4], 1.0, 0.0)
    return (output, input_grad, new_qkv, qkv_mean, qkv_square, new_proj, proj_mean, proj_square, new_expand, expand_mean, expand_square, new_down, down_mean, down_square, new_gains, gains_mean, gains_square)
```

```python
import itertools

import jax
import jax.numpy as jnp
from jax import lax
from jax.experimental import pallas as pl
from jax.experimental.pallas import tpu as pltpu
from jax.sharding import PartitionSpec as P

D = 960
HEADS = 15
KV_HEADS = 5
GROUP = HEADS // KV_HEADS
HEAD_DIM = 64
FF = 2560
STEP = 10
HALF = FF // 2
QKVW = D + 2 * KV_HEADS * HEAD_DIM
PART = 896


eps = 1e-05
rope_base = 100000.0
beta_first = 0.9
beta_second = 0.95
adam_eps = 1e-08
masked_score = -1e30
low = jnp.bfloat16


def linear(zh, y, core, zl, x):
    return (zh * 8 + y * 2 + core) * 8 + zl * 4 + x


def send(value, target):
    pairs = []
    for place in itertools.product(range(2), range(4), range(2), range(2), range(4)):
        to = target(*place)
        if to is not None:
            pairs.append((linear(*place), linear(*to)))
    return lax.ppermute(value, ("dp", "ctx"), pairs)


def to_x(k):
    return lambda zh, y, core, zl, x: (zh, y, core, zl, x ^ k)


def to_x_owner(k):
    return lambda zh, y, core, zl, x: (zh, y, core, zl, x ^ k) if core == zl else None


def to_core(zh, y, core, zl, x):
    return (zh, y, 1 - core, zl, x)


def to_z(step):
    def target(zh, y, core, zl, x):
        z = (zh * 2 + zl + step) % 4
        return (z // 2, y, core, z % 2, x)

    return target


def to_z_from(step, owner):
    def target(zh, y, core, zl, x):
        if (core == zl) != owner:
            return None
        z = (zh * 2 + zl + step) % 4
        return (z // 2, y, core, z % 2, x)

    return target


def to_chip(k):
    return lambda zh, y, core, zl, x: (zh ^ (k >> 2), y ^ (k & 3), core, zl, x)


def to_chip_owner(k):
    return lambda zh, y, core, zl, x: (
        (zh ^ (k >> 2), y ^ (k & 3), core, zl, x) if core == zl else None
    )


def pick(stack, index):
    return lax.dynamic_index_in_dim(stack, index, 0, keepdims=False)


def reduce_direct(stack, me, targets):
    total = pick(stack, me).astype(jnp.float32)
    for k, target in targets:
        total = total + send(pick(stack, me ^ k), target).astype(jnp.float32)
    return total.astype(low)


def gather_direct(piece, me, targets):
    count = len(targets) + 1
    whole = jnp.zeros((count,) + piece.shape, piece.dtype)
    whole = lax.dynamic_update_index_in_dim(whole, piece, me, 0)
    for k, target in targets:
        whole = lax.dynamic_update_index_in_dim(whole, send(piece, target), me ^ k, 0)
    return whole


def rope_tables(positions):
    halfway = HEAD_DIM // 2
    freqs = rope_base ** (-(jnp.arange(halfway, dtype=jnp.float32) * 2.0) / HEAD_DIM)
    angles = freqs[:, None] * positions.astype(jnp.float32)[None, :]
    return (jnp.cos(angles), jnp.sin(angles))


def rotate(field, cosine, sine):
    halfway = HEAD_DIM // 2
    first = field[:, :halfway]
    second = field[:, halfway:]
    return jnp.concatenate(
        [first * cosine - second * sine, second * cosine + first * sine], axis=1
    )


def rotate_back(field, cosine, sine):
    halfway = HEAD_DIM // 2
    first = field[:, :halfway]
    second = field[:, halfway:]
    return jnp.concatenate(
        [first * cosine + second * sine, second * cosine - first * sine], axis=1
    )


def positions_of(order, count, span):
    rows = jnp.arange(count, dtype=jnp.int32)
    slots = rows // span
    labels = jnp.arange(order.shape[0], dtype=jnp.int32)
    picked = jnp.sum(jnp.where(slots[:, None] == labels[None, :], order[None, :], 0), axis=1)
    return picked * span + rows % span


def rms_scale(rows):
    return lax.rsqrt(jnp.mean(rows * rows, axis=-1, keepdims=True) + eps)


def contract(left, right, left_axis, right_axis):
    return lax.dot_general(
        left,
        right,
        (((left_axis,), (right_axis,)), ((), ())),
        preferred_element_type=jnp.float32,
    )


def norm_back(grad_normed, rows, inverse, gain):
    scaled = grad_normed * gain
    inner = jnp.mean(scaled * rows, axis=-1, keepdims=True)
    rows_grad = inverse * (scaled - rows * inverse * inverse * inner)
    gain_grad = jnp.sum(grad_normed * rows * inverse, axis=0)
    return (rows_grad, gain_grad)


def load_keys(kv_ref):
    columns = jnp.concatenate([kv_ref[j, 0] for j in range(kv_ref.shape[0])], axis=1)
    return columns, columns.T


def attend_kernel(q_ref, kv_ref, bias_ref, o_ref, lse_ref):
    columns, rows = load_keys(kv_ref)
    bias = bias_ref[...]
    blank = jnp.zeros((HEAD_DIM, q_ref.shape[1]), low)
    for h in range(GROUP):
        part = pl.ds(h * HEAD_DIM, HEAD_DIM)
        query = jnp.concatenate([q_ref[part, :], blank], axis=0)
        scores = contract(rows, query, 1, 0) + bias
        top = jnp.max(scores, axis=0, keepdims=True)
        weights = jnp.exp(scores - top)
        total = jnp.sum(weights, axis=0, keepdims=True)
        mixed = contract(columns[HEAD_DIM:], weights.astype(low), 1, 0)
        o_ref[part, :] = (mixed / total).astype(low)
        lse_ref[h] = top + jnp.log(total)


def attend_back_kernel(q_ref, kv_ref, bias_ref, do_ref, o_ref, lse_ref, dq_ref, dkv_ref):
    columns, rows = load_keys(kv_ref)
    bias = bias_ref[...]
    local = q_ref.shape[1]
    blank = jnp.zeros((HEAD_DIM, local), low)
    terms = None
    for h in range(GROUP):
        part = pl.ds(h * HEAD_DIM, HEAD_DIM)
        query = jnp.concatenate([q_ref[part, :], blank], axis=0)
        back = jnp.concatenate([blank, do_ref[part, :]], axis=0)
        delta = jnp.sum(
            do_ref[part, :].astype(jnp.float32) * o_ref[part, :].astype(jnp.float32),
            axis=0,
            keepdims=True,
        )
        weights = jnp.exp(contract(rows, query, 1, 0) + bias - lse_ref[h])
        grad = contract(rows, back, 1, 0)
        scores = (weights * (grad - delta)).astype(low)
        dq_ref[part, :] = contract(columns[:HEAD_DIM], scores, 1, 0) * HEAD_DIM ** (-0.5)
        term = contract(scores, query, 1, 1) + contract(weights.astype(low), back, 1, 1)
        terms = term if terms is None else terms + term
    for j in range(dkv_ref.shape[0]):
        dkv_ref[j, 0] = terms[j * local : (j + 1) * local].astype(low)


def attention_specs(chunks, local):
    wide = GROUP * HEAD_DIM
    heads = pl.BlockSpec((wide, local), lambda g: (g, 0))
    keys = pl.BlockSpec((chunks, 1, 2 * HEAD_DIM, local), lambda g: (0, g, 0, 0))
    bias = pl.BlockSpec((chunks * local, local), lambda g: (0, 0))
    sums = pl.BlockSpec((GROUP, 1, local), lambda g: (g, 0, 0))
    return heads, keys, bias, sums


def attend(query, keys, bias):
    chunks, _, _, local = keys.shape
    heads, kv, mask, sums = attention_specs(chunks, local)
    flops = 4 * HEADS * local * chunks * local * HEAD_DIM
    return pl.pallas_call(
        attend_kernel,
        grid=(KV_HEADS,),
        out_shape=(
            jax.ShapeDtypeStruct((D, local), low),
            jax.ShapeDtypeStruct((HEADS, 1, local), jnp.float32),
        ),
        in_specs=[heads, kv, mask],
        out_specs=(heads, sums),
        compiler_params=pltpu.CompilerParams(vmem_limit_bytes=48 * 1024 * 1024),
        cost_estimate=pl.CostEstimate(
            flops=4 * flops, bytes_accessed=8 * 1024 * 1024, transcendentals=0
        ),
        name="attend",
    )(query, keys, bias)


def attend_back(query, keys, bias, back, out, lse):
    chunks, _, _, local = keys.shape
    heads, kv, mask, sums = attention_specs(chunks, local)
    grads = pl.BlockSpec((chunks, 1, local, 2 * HEAD_DIM), lambda g: (0, g, 0, 0))
    flops = 10 * HEADS * local * chunks * local * HEAD_DIM
    return pl.pallas_call(
        attend_back_kernel,
        grid=(KV_HEADS,),
        out_shape=(
            jax.ShapeDtypeStruct((D, local), jnp.float32),
            jax.ShapeDtypeStruct((chunks, KV_HEADS, local, 2 * HEAD_DIM), low),
        ),
        in_specs=[heads, kv, mask, heads, heads, sums],
        out_specs=(heads, grads),
        compiler_params=pltpu.CompilerParams(vmem_limit_bytes=48 * 1024 * 1024),
        cost_estimate=pl.CostEstimate(
            flops=4 * flops, bytes_accessed=8 * 1024 * 1024, transcendentals=0
        ),
        name="attend_back",
    )(query, keys, bias, back, out, lse)


def adam_step(master, first, second, grad, rate, decay):
    new_first = beta_first * first + (1.0 - beta_first) * grad
    new_second = beta_second * second + (1.0 - beta_second) * grad * grad
    fix_one = 1.0 - beta_first**STEP
    fix_two = 1.0 - beta_second**STEP
    update = new_first / fix_one / (jnp.sqrt(new_second / fix_two) + adam_eps) + decay * master
    return (master - rate * update, new_first, new_second)


def on_device(
    inputs,
    cotangent,
    span_order,
    w_qkv,
    qkv_first,
    qkv_second,
    w_proj,
    proj_first,
    proj_second,
    w_expand,
    expand_first,
    expand_second,
    w_down,
    down_first,
    down_second,
    gains,
    gains_first,
    gains_second,
):
    dp = lax.axis_index("dp")
    rank = lax.axis_index("ctx")
    core = dp % 2
    chip = dp // 2
    zl = rank // 4
    x = rank % 4
    owner = core == zl
    first_core = core == 0
    groups = lax.axis_size("ctx")
    batch, local, width = inputs.shape
    shard = w_qkv.shape[0]
    length = local * groups

    qkv_low = jnp.pad(w_qkv.astype(low), ((0, 0), (0, 2 * PART - QKVW)))
    qkv_half = lax.dynamic_slice_in_dim(qkv_low, PART * core, PART, 1)
    qkv_mine = lax.all_to_all(
        jnp.broadcast_to(qkv_half[None], (groups, shard, PART)), "ctx", 0, 0, tiled=True
    ).reshape(width, PART)
    qkv_theirs = send(qkv_mine, to_core)
    full_proj = lax.all_gather(w_proj.astype(low), "ctx", axis=0, tiled=True)
    full_gains = lax.all_gather(gains.astype(low), "ctx", axis=1, tiled=True)
    gain_one = full_gains[0].astype(jnp.float32)
    gain_two = full_gains[1].astype(jnp.float32)

    gate_low = lax.dynamic_slice_in_dim(w_expand, HALF * core, HALF, 1).astype(low)
    up_low = lax.dynamic_slice_in_dim(w_expand, FF + HALF * core, HALF, 1).astype(low)
    expand_low = jnp.concatenate([gate_low, up_low], axis=1)
    down_low = w_down.astype(low)
    expand_low, down_low, qkv_mine = lax.optimization_barrier((expand_low, down_low, qkv_mine))
    near = [expand_low] + [send(expand_low, to_x(k)) for k in (1, 2, 3)]
    far = [send(near[k], to_z(1 if k % 2 else -1)) for k in range(4)]
    half_expand = jnp.zeros((width, FF), low)
    for k in range(4):
        half_expand = lax.dynamic_update_slice(
            half_expand, near[k], (shard * (zl * 4 + (x ^ k)), 0)
        )
        half_expand = lax.dynamic_update_slice(
            half_expand, far[k], (shard * ((1 - zl) * 4 + (x ^ k)), 0)
        )
    near = [down_low] + [send(down_low, to_x_owner(k)) for k in (1, 2, 3)]
    far = [send(near[k], to_z_from(1 if k % 2 else -1, True)) for k in range(4)]
    half_down = jnp.zeros((HALF, width), low)
    for k in range(4):
        half_down = lax.dynamic_update_slice(
            half_down, jnp.where(owner, near[k], far[k]), (down_low.shape[0] * (x ^ k), 0)
        )

    every_pos = positions_of(span_order, length, local // 2)
    own_pos = lax.dynamic_slice_in_dim(every_pos, rank * local, local)
    cosine, sine = rope_tables(own_pos)
    bias = jnp.where(every_pos[:, None] <= own_pos[None, :], 0.0, masked_score)
    rows_in = inputs.reshape(local, width).astype(jnp.float32)
    inv_one = rms_scale(rows_in)
    normed_one = (rows_in * inv_one * gain_one).astype(low)
    mixed_mine = contract(normed_one, qkv_mine, 1, 0)
    mixed_theirs = contract(normed_one, qkv_theirs, 1, 0)
    mixed = jnp.concatenate(
        [
            jnp.where(first_core, mixed_mine, mixed_theirs),
            jnp.where(first_core, mixed_theirs, mixed_mine),
        ],
        axis=1,
    ).T
    kv_width = KV_HEADS * HEAD_DIM
    queries = mixed[:width].reshape(HEADS, HEAD_DIM, local)
    keys = mixed[width : width + kv_width].reshape(KV_HEADS, HEAD_DIM, local)
    values = mixed[width + kv_width : QKVW].reshape(KV_HEADS, HEAD_DIM, local)
    key_values = jnp.concatenate(
        [rotate(keys, cosine, sine).astype(low), values.astype(low)], axis=1
    )
    all_keys = lax.all_to_all(
        jnp.broadcast_to(key_values[None], (groups,) + key_values.shape), "ctx", 0, 0, tiled=True
    )
    query = (rotate(queries, cosine, sine).astype(low) * HEAD_DIM ** (-0.5)).reshape(width, local)
    attended, lse = attend(query, all_keys, bias)
    middle = rows_in + contract(attended, full_proj, 0, 0)
    inv_two = rms_scale(middle)
    normed_two = (middle * inv_two * gain_two).astype(low)

    back_rows = cotangent.reshape(local, width)
    both_back = jnp.concatenate([back_rows, send(back_rows, to_core)], axis=0)
    both_normed = jnp.concatenate([normed_two, send(normed_two, to_core)], axis=0)
    expanded = contract(both_normed, half_expand, 1, 0)
    gate = expanded[:, :HALF]
    upward = expanded[:, HALF:]
    hidden = (jax.nn.silu(gate) * upward).astype(low)
    fed = contract(hidden, half_down, 1, 0)
    fed_other = send(fed[local:].astype(low), to_core)
    output = (middle + fed[:local] + fed_other.astype(jnp.float32)).astype(low)
    grad_down = contract(hidden, both_back, 0, 0).astype(low)
    grad_hidden = contract(both_back, half_down, 1, 1)
    sigmoid = jax.nn.sigmoid(gate)
    grad_gate = grad_hidden * upward * sigmoid * (1.0 + gate * (1.0 - sigmoid))
    grad_up = grad_hidden * gate * sigmoid
    grad_expanded = jnp.concatenate([grad_gate, grad_up], axis=1).astype(low)
    grad_normed = contract(grad_expanded, half_expand, 1, 1)
    grad_expand = contract(both_normed, grad_expanded, 0, 0).astype(low)
    grad_other = send(grad_normed[local:].astype(low), to_core)
    grad_normed_two = grad_normed[:local] + grad_other.astype(jnp.float32)
    back_two, gain_grad_two = norm_back(grad_normed_two, middle, inv_two, gain_two)
    grad_middle = back_rows.astype(jnp.float32) + back_two
    middle_low = grad_middle.astype(low)
    grad_proj = contract(attended, middle_low, 1, 0).astype(low)
    grad_att = contract(full_proj, middle_low, 1, 1).astype(low)

    other = lax.dynamic_slice_in_dim(grad_expand, 480 * (1 - zl), 480, 0)
    kept = lax.dynamic_slice_in_dim(grad_expand, 480 * zl, 480, 0)
    came = jnp.concatenate([send(other[:, :HALF], to_z(1)), send(other[:, HALF:], to_z(-1))], axis=1)
    expand_sum = (kept.astype(jnp.float32) + came.astype(jnp.float32)).astype(low)
    expand_sum = reduce_direct(
        expand_sum.reshape(4, shard, FF), x, [(k, to_x(k)) for k in (1, 2, 3)]
    )
    chips = [(k, to_chip(k)) for k in range(1, 8)]
    expand_sum = reduce_direct(expand_sum.reshape(8, shard // 8, FF), chip, chips)
    expand_sum = gather_direct(expand_sum, chip, chips).reshape(shard, FF)
    expand_other = send(expand_sum, to_core)
    expand_one = jnp.where(first_core, expand_sum, expand_other)
    expand_two = jnp.where(first_core, expand_other, expand_sum)
    whole_expand = jnp.concatenate(
        [expand_one[:, :HALF], expand_two[:, :HALF], expand_one[:, HALF:], expand_two[:, HALF:]],
        axis=1,
    ).astype(jnp.float32)

    proj_kept = lax.dynamic_slice_in_dim(grad_proj, 480 * core, 480, 0)
    proj_sent = lax.dynamic_slice_in_dim(grad_proj, 480 * (1 - core), 480, 0)
    proj_sum = proj_kept.astype(jnp.float32) + send(proj_sent, to_core).astype(jnp.float32)
    tall = jnp.concatenate(
        [
            grad_down.reshape(4, 320, width),
            proj_sum.astype(low).reshape(4, shard, width),
            jnp.zeros((4, 8, width), low),
        ],
        axis=1,
    )
    came = jnp.concatenate(
        [send(tall[:2], to_z_from(1, False)), send(tall[2:], to_z_from(-1, False))], axis=0
    )
    tall = (tall.astype(jnp.float32) + came.astype(jnp.float32)).astype(low)
    tall = reduce_direct(tall, x, [(k, to_x_owner(k)) for k in (1, 2, 3)])
    chips_owner = [(k, to_chip_owner(k)) for k in range(1, 8)]
    tall = reduce_direct(tall.reshape(8, 56, width), chip, chips_owner)
    tall = gather_direct(tall, chip, chips_owner).reshape(448, width)
    tall = jnp.where(owner, tall, send(tall, to_core)).astype(jnp.float32)
    whole_down = tall[:320]
    whole_proj = tall[320:440]

    grad_query, key_terms = attend_back(query, all_keys, bias, grad_att, attended, lse)
    grad_keys = jnp.sum(
        lax.all_to_all(key_terms, "ctx", 0, 0, tiled=True).astype(jnp.float32), axis=0
    )
    grad_keys = jnp.transpose(grad_keys, (0, 2, 1))
    grad_mixed = jnp.concatenate(
        [
            rotate_back(grad_query.reshape(HEADS, HEAD_DIM, local), cosine, sine).reshape(
                width, local
            ),
            rotate_back(grad_keys[:, :HEAD_DIM], cosine, sine).reshape(kv_width, local),
            grad_keys[:, HEAD_DIM:].reshape(kv_width, local),
        ],
        axis=0,
    ).astype(low)
    mixed_one = grad_mixed[:PART]
    mixed_two = jnp.pad(grad_mixed[PART:], ((0, 2 * PART - QKVW), (0, 0)))
    grad_normed_one = contract(
        jnp.where(first_core, mixed_one, mixed_two), qkv_mine, 0, 1
    ) + contract(jnp.where(first_core, mixed_two, mixed_one), qkv_theirs, 0, 1)
    back_one, gain_grad_one = norm_back(grad_normed_one, rows_in, inv_one, gain_one)
    input_grad = (grad_middle + back_one).astype(low).reshape(batch, local, width)
    grad_qkv = contract(normed_one, grad_mixed, 0, 1)
    wide = jnp.concatenate(
        [
            grad_qkv,
            gain_grad_one[:, None],
            gain_grad_two[:, None],
            jnp.zeros((width, 2 * PART - QKVW - 2), jnp.float32),
        ],
        axis=1,
    ).astype(low)
    kept = lax.dynamic_slice_in_dim(wide, PART * core, PART, 1)
    sent = lax.dynamic_slice_in_dim(wide, PART * (1 - core), PART, 1)
    wide = (kept.astype(jnp.float32) + send(sent, to_core).astype(jnp.float32)).astype(low)
    wide = jnp.sum(
        lax.all_to_all(wide.reshape(groups, shard, PART), "ctx", 0, 0, tiled=True).astype(
            jnp.float32
        ),
        axis=0,
    ).astype(low)
    same_core = [[2 * c + k for c in range(8)] for k in range(2)]
    wide = jnp.sum(
        lax.all_to_all(
            jnp.broadcast_to(wide[None], (8, shard, PART)),
            "dp",
            0,
            0,
            axis_index_groups=same_core,
            tiled=True,
        ).astype(jnp.float32),
        axis=0,
    ).astype(low)
    wide_other = send(wide, to_core)
    wide = jnp.concatenate(
        [jnp.where(first_core, wide, wide_other), jnp.where(first_core, wide_other, wide)], axis=1
    ).astype(jnp.float32)
    whole_qkv = wide[:, :QKVW]
    whole_gains = wide[:, QKVW : QKVW + 2].T

    new_qkv, qkv_mean, qkv_square = adam_step(
        w_qkv, qkv_first, qkv_second, whole_qkv, 2.0 * D ** (-0.5), 0.1
    )
    new_proj, proj_mean, proj_square = adam_step(
        w_proj, proj_first, proj_second, whole_proj, 2.0 * (D // 8) ** (-0.5), 0.1
    )
    new_expand, expand_mean, expand_square = adam_step(
        w_expand, expand_first, expand_second, whole_expand, 2.0 * D ** (-0.5), 0.1
    )
    new_down, down_mean, down_square = adam_step(
        w_down, down_first, down_second, whole_down, 2.0 * FF ** (-0.5), 0.1
    )
    new_gains, gains_mean, gains_square = adam_step(
        gains, gains_first, gains_second, whole_gains, 1.0, 0.0
    )
    return (
        output.reshape(batch, local, width),
        input_grad,
        new_qkv,
        qkv_mean,
        qkv_square,
        new_proj,
        proj_mean,
        proj_square,
        new_expand,
        expand_mean,
        expand_square,
        new_down,
        down_mean,
        down_square,
        new_gains,
        gains_mean,
        gains_square,
    )


def solution(mesh):
    rows = P("dp", "ctx", None)
    owned = P("ctx", None)
    split = P(None, "ctx")
    return jax.shard_map(
        on_device,
        mesh=mesh,
        in_specs=(rows, rows, P()) + (owned,) * 12 + (split,) * 3,
        out_specs=(rows, rows) + (owned,) * 12 + (split,) * 3,
        check_vma=False,
    )
```

```python
import jax
import jax.numpy as jnp
from jax import lax
from jax.experimental import pallas as pl
from jax.experimental.pallas import tpu as pltpu
from jax.sharding import PartitionSpec as P

D = 960
HEADS = 15
KV_HEADS = 5
GROUP = HEADS // KV_HEADS
HEAD_DIM = 64
FF = 2560
STEP = 10
HALF = FF // 2
QKVW = D + 2 * KV_HEADS * HEAD_DIM


eps = 1e-05
rope_base = 100000.0
beta_first = 0.9
beta_second = 0.95
adam_eps = 1e-08
masked_score = -1e30
low = jnp.bfloat16


AXES = ("zh", "y", "core", "zl", "x")
CHIPS = ("zh", "y")
CTX = ("zl", "x")


def swap_cores(value):
    return lax.ppermute(value, "core", [(0, 1), (1, 0)])


def exchange(stack, axes):
    return lax.all_to_all(stack, axes, 0, 0, tiled=True)


def spread(piece, axes, count):
    return exchange(jnp.broadcast_to(piece[None], (count,) + piece.shape), axes)


def total(stack):
    return jnp.sum(stack.astype(jnp.float32), axis=0).astype(low)


def ordered(core, mine, theirs):
    first = core == 0
    return jnp.where(first, mine, theirs), jnp.where(first, theirs, mine)


def rope_tables(positions):
    halfway = HEAD_DIM // 2
    freqs = rope_base ** (-(jnp.arange(halfway, dtype=jnp.float32) * 2.0) / HEAD_DIM)
    angles = freqs[:, None] * positions.astype(jnp.float32)[None, :]
    return (jnp.cos(angles), jnp.sin(angles))


def rotate(field, cosine, sine):
    halfway = HEAD_DIM // 2
    first = field[:, :halfway]
    second = field[:, halfway:]
    return jnp.concatenate(
        [first * cosine - second * sine, second * cosine + first * sine], axis=1
    )


def rotate_back(field, cosine, sine):
    halfway = HEAD_DIM // 2
    first = field[:, :halfway]
    second = field[:, halfway:]
    return jnp.concatenate(
        [first * cosine + second * sine, second * cosine - first * sine], axis=1
    )


def positions_of(order, count, span):
    rows = jnp.arange(count, dtype=jnp.int32)
    slots = rows // span
    labels = jnp.arange(order.shape[0], dtype=jnp.int32)
    picked = jnp.sum(jnp.where(slots[:, None] == labels[None, :], order[None, :], 0), axis=1)
    return picked * span + rows % span


def rms_scale(rows):
    return lax.rsqrt(jnp.mean(rows * rows, axis=-1, keepdims=True) + eps)


def contract(left, right, left_axis, right_axis):
    return lax.dot_general(
        left,
        right,
        (((left_axis,), (right_axis,)), ((), ())),
        preferred_element_type=jnp.float32,
    )


def norm_back(grad_normed, rows, inverse, gain):
    scaled = grad_normed * gain
    inner = jnp.mean(scaled * rows, axis=-1, keepdims=True)
    rows_grad = inverse * (scaled - rows * inverse * inverse * inner)
    gain_grad = jnp.sum(grad_normed * rows * inverse, axis=0)
    return (rows_grad, gain_grad)


def load_keys(kv_ref):
    columns = jnp.concatenate([kv_ref[j, 0] for j in range(kv_ref.shape[0])], axis=1)
    return columns, columns.T


def attend_kernel(q_ref, kv_ref, bias_ref, o_ref, lse_ref):
    columns, rows = load_keys(kv_ref)
    bias = bias_ref[...]
    blank = jnp.zeros((HEAD_DIM, q_ref.shape[1]), low)
    for h in range(GROUP):
        part = pl.ds(h * HEAD_DIM, HEAD_DIM)
        query = jnp.concatenate([q_ref[part, :], blank], axis=0)
        scores = contract(rows, query, 1, 0) + bias
        top = jnp.max(scores, axis=0, keepdims=True)
        weights = jnp.exp(scores - top)
        total = jnp.sum(weights, axis=0, keepdims=True)
        mixed = contract(columns[HEAD_DIM:], weights.astype(low), 1, 0)
        o_ref[part, :] = (mixed / total).astype(low)
        lse_ref[h] = top + jnp.log(total)


def attend_back_kernel(q_ref, kv_ref, bias_ref, do_ref, o_ref, lse_ref, dq_ref, dkv_ref):
    columns, rows = load_keys(kv_ref)
    bias = bias_ref[...]
    local = q_ref.shape[1]
    blank = jnp.zeros((HEAD_DIM, local), low)
    terms = None
    for h in range(GROUP):
        part = pl.ds(h * HEAD_DIM, HEAD_DIM)
        query = jnp.concatenate([q_ref[part, :], blank], axis=0)
        back = jnp.concatenate([blank, do_ref[part, :]], axis=0)
        delta = jnp.sum(
            do_ref[part, :].astype(jnp.float32) * o_ref[part, :].astype(jnp.float32),
            axis=0,
            keepdims=True,
        )
        weights = jnp.exp(contract(rows, query, 1, 0) + bias - lse_ref[h])
        grad = contract(rows, back, 1, 0)
        scores = (weights * (grad - delta)).astype(low)
        dq_ref[part, :] = contract(columns[:HEAD_DIM], scores, 1, 0) * HEAD_DIM ** (-0.5)
        term = contract(scores, query, 1, 1) + contract(weights.astype(low), back, 1, 1)
        terms = term if terms is None else terms + term
    for j in range(dkv_ref.shape[0]):
        dkv_ref[j, 0] = terms[j * local : (j + 1) * local].astype(low)


def attention_specs(chunks, local):
    wide = GROUP * HEAD_DIM
    heads = pl.BlockSpec((wide, local), lambda g: (g, 0))
    keys = pl.BlockSpec((chunks, 1, 2 * HEAD_DIM, local), lambda g: (0, g, 0, 0))
    bias = pl.BlockSpec((chunks * local, local), lambda g: (0, 0))
    sums = pl.BlockSpec((GROUP, 1, local), lambda g: (g, 0, 0))
    return heads, keys, bias, sums


def attend(query, keys, bias):
    chunks, _, _, local = keys.shape
    heads, kv, mask, sums = attention_specs(chunks, local)
    flops = 4 * HEADS * local * chunks * local * HEAD_DIM
    return pl.pallas_call(
        attend_kernel,
        grid=(KV_HEADS,),
        out_shape=(
            jax.ShapeDtypeStruct((D, local), low),
            jax.ShapeDtypeStruct((HEADS, 1, local), jnp.float32),
        ),
        in_specs=[heads, kv, mask],
        out_specs=(heads, sums),
        compiler_params=pltpu.CompilerParams(vmem_limit_bytes=48 * 1024 * 1024),
        cost_estimate=pl.CostEstimate(
            flops=4 * flops, bytes_accessed=8 * 1024 * 1024, transcendentals=0
        ),
        name="attend",
    )(query, keys, bias)


def attend_back(query, keys, bias, back, out, lse):
    chunks, _, _, local = keys.shape
    heads, kv, mask, sums = attention_specs(chunks, local)
    grads = pl.BlockSpec((chunks, 1, local, 2 * HEAD_DIM), lambda g: (0, g, 0, 0))
    flops = 10 * HEADS * local * chunks * local * HEAD_DIM
    return pl.pallas_call(
        attend_back_kernel,
        grid=(KV_HEADS,),
        out_shape=(
            jax.ShapeDtypeStruct((D, local), jnp.float32),
            jax.ShapeDtypeStruct((chunks, KV_HEADS, local, 2 * HEAD_DIM), low),
        ),
        in_specs=[heads, kv, mask, heads, heads, sums],
        out_specs=(heads, grads),
        compiler_params=pltpu.CompilerParams(vmem_limit_bytes=48 * 1024 * 1024),
        cost_estimate=pl.CostEstimate(
            flops=4 * flops, bytes_accessed=8 * 1024 * 1024, transcendentals=0
        ),
        name="attend_back",
    )(query, keys, bias, back, out, lse)


def adam_step(master, first, second, grad, rate, decay):
    new_first = beta_first * first + (1.0 - beta_first) * grad
    new_second = beta_second * second + (1.0 - beta_second) * grad * grad
    fix_one = 1.0 - beta_first**STEP
    fix_two = 1.0 - beta_second**STEP
    update = new_first / fix_one / (jnp.sqrt(new_second / fix_two) + adam_eps) + decay * master
    return (master - rate * update, new_first, new_second)


def on_device(
    inputs,
    cotangent,
    span_order,
    w_qkv,
    qkv_first,
    qkv_second,
    w_proj,
    proj_first,
    proj_second,
    w_expand,
    expand_first,
    expand_second,
    w_down,
    down_first,
    down_second,
    gains,
    gains_first,
    gains_second,
):
    core = lax.axis_index("core")
    rank = lax.axis_index(CTX)
    first_core = core == 0
    groups = 8
    batch, local, width = inputs.shape
    shard = w_qkv.shape[0]
    hidden_shard = w_down.shape[0] // 2
    length = local * groups
    kv_width = KV_HEADS * HEAD_DIM

    full_gains = spread(gains.astype(low), CTX, groups)
    full_gains = jnp.transpose(full_gains, (1, 0, 2)).reshape(2, width).astype(jnp.float32)
    gain_one = full_gains[0]
    gain_two = full_gains[1]

    qkv_low = w_qkv.astype(low)
    proj_low = w_proj.astype(low)
    half_low = jnp.concatenate(
        [
            jnp.where(first_core, qkv_low[:, : QKVW // 2], qkv_low[:, QKVW // 2 :]),
            jnp.where(first_core, proj_low[:, : D // 2], proj_low[:, D // 2 :]),
        ],
        axis=1,
    )
    mine = spread(half_low, CTX, groups).reshape(width, HALF)
    theirs = swap_cores(mine)

    down_low = lax.dynamic_slice_in_dim(w_down, hidden_shard * core, hidden_shard, 0).astype(low)
    half_down = lax.all_gather(down_low, CTX, axis=0, tiled=True)
    expand_low = w_expand.astype(low)
    expand_low = jnp.concatenate(
        [
            jnp.where(
                first_core,
                expand_low[:, k * hidden_shard : (k + 1) * hidden_shard],
                expand_low[:, (k + 1) * hidden_shard : (k + 2) * hidden_shard],
            )
            for k in range(0, 32, 2)
        ],
        axis=1,
    )
    half_expand = lax.all_gather(expand_low, CTX, axis=0, tiled=True)

    every_pos = positions_of(span_order, length, local // 2)
    own_pos = lax.dynamic_slice_in_dim(every_pos, rank * local, local)
    cosine, sine = rope_tables(own_pos)
    bias = jnp.where(every_pos[:, None] <= own_pos[None, :], 0.0, masked_score)
    rows_in = inputs.reshape(local, width).astype(jnp.float32)
    inv_one = rms_scale(rows_in)
    normed_one = (rows_in * inv_one * gain_one).astype(low)
    mixed = jnp.concatenate(
        ordered(
            core,
            contract(normed_one, mine[:, : QKVW // 2], 1, 0),
            contract(normed_one, theirs[:, : QKVW // 2], 1, 0),
        ),
        axis=1,
    ).T
    queries = mixed[:width].reshape(HEADS, HEAD_DIM, local)
    keys = mixed[width : width + kv_width].reshape(KV_HEADS, HEAD_DIM, local)
    values = mixed[width + kv_width :].reshape(KV_HEADS, HEAD_DIM, local)
    key_values = jnp.concatenate(
        [rotate(keys, cosine, sine).astype(low), values.astype(low)], axis=1
    )
    all_keys = spread(key_values, CTX, groups)
    query = (rotate(queries, cosine, sine).astype(low) * HEAD_DIM ** (-0.5)).reshape(width, local)
    attended, lse = attend(query, all_keys, bias)
    proj_one, proj_two = mine[:, QKVW // 2 :], theirs[:, QKVW // 2 :]
    mixed_out = jnp.concatenate(
        ordered(core, contract(attended, proj_one, 0, 0), contract(attended, proj_two, 0, 0)),
        axis=1,
    )
    middle = rows_in + mixed_out
    inv_two = rms_scale(middle)
    normed_two = (middle * inv_two * gain_two).astype(low)

    back_rows = cotangent.reshape(local, width)
    both_back = jnp.concatenate([back_rows, swap_cores(back_rows)], axis=0)
    both_normed = jnp.concatenate([normed_two, swap_cores(normed_two)], axis=0)
    expanded = contract(both_normed, half_expand, 1, 0)
    gate = expanded[:, :HALF]
    upward = expanded[:, HALF:]
    hidden = (jax.nn.silu(gate) * upward).astype(low)
    fed = contract(hidden, half_down, 1, 0)
    fed_other = swap_cores(fed[local:].astype(low))
    output = (middle + fed[:local] + fed_other.astype(jnp.float32)).astype(low)
    grad_down = contract(hidden, both_back, 0, 0).astype(low)
    grad_hidden = contract(both_back, half_down, 1, 1)
    sigmoid = jax.nn.sigmoid(gate)
    grad_gate = grad_hidden * upward * sigmoid * (1.0 + gate * (1.0 - sigmoid))
    grad_up = grad_hidden * gate * sigmoid
    grad_expanded = jnp.concatenate([grad_gate, grad_up], axis=1).astype(low)
    grad_normed = contract(grad_expanded, half_expand, 1, 1)
    grad_expand = contract(both_normed, grad_expanded, 0, 0).astype(low)
    grad_other = swap_cores(grad_normed[local:].astype(low))
    grad_normed_two = grad_normed[:local] + grad_other.astype(jnp.float32)
    back_two, gain_grad_two = norm_back(grad_normed_two, middle, inv_two, gain_two)
    grad_middle = back_rows.astype(jnp.float32) + back_two
    middle_low = grad_middle.astype(low)
    grad_proj = contract(attended, middle_low, 1, 0).astype(low)
    back_one, back_two = ordered(core, middle_low[:, : D // 2], middle_low[:, D // 2 :])
    grad_att = (contract(proj_one, back_one, 1, 1) + contract(proj_two, back_two, 1, 1)).astype(
        low
    )

    down_sum = lax.psum_scatter(grad_down, CTX, scatter_dimension=0, tiled=True)
    expand_sum = lax.psum_scatter(grad_expand, CTX, scatter_dimension=0, tiled=True)

    grad_query, key_terms = attend_back(query, all_keys, bias, grad_att, attended, lse)
    key_terms = exchange(key_terms, CTX)
    query_mixed = (
        rotate_back(grad_query.reshape(HEADS, HEAD_DIM, local), cosine, sine)
        .reshape(width, local)
        .astype(low)
    )
    grad_q = contract(normed_one, query_mixed, 0, 1).astype(low)
    kept, sent = ordered(core, grad_q, grad_proj)
    early = (kept.astype(jnp.float32) + swap_cores(sent).astype(jnp.float32)).astype(low)
    early = total(exchange(early.reshape(groups, shard, width), CTX))

    grad_keys = jnp.transpose(jnp.sum(key_terms.astype(jnp.float32), axis=0), (0, 2, 1))
    key_mixed = jnp.concatenate(
        [
            rotate_back(grad_keys[:, :HEAD_DIM], cosine, sine).reshape(kv_width, local),
            grad_keys[:, HEAD_DIM:].reshape(kv_width, local),
        ],
        axis=0,
    ).astype(low)
    grad_kv = contract(normed_one, key_mixed, 0, 1)
    grad_mixed = jnp.concatenate([query_mixed, key_mixed], axis=0)
    mixed_one, mixed_two = ordered(core, grad_mixed[: QKVW // 2], grad_mixed[QKVW // 2 :])
    grad_normed_one = contract(mixed_one, mine[:, : QKVW // 2], 0, 1) + contract(
        mixed_two, theirs[:, : QKVW // 2], 0, 1
    )
    back_first, gain_grad_one = norm_back(grad_normed_one, rows_in, inv_one, gain_one)
    input_grad = (grad_middle + back_first).astype(low).reshape(batch, local, width)
    late = jnp.concatenate(
        [
            grad_kv,
            gain_grad_one[:, None],
            gain_grad_two[:, None],
            jnp.zeros((width, 768 - 2 * kv_width - 2), jnp.float32),
        ],
        axis=1,
    ).astype(low)
    kept, sent = ordered(core, late[:, :384], late[:, 384:])
    late = (kept.astype(jnp.float32) + swap_cores(sent).astype(jnp.float32)).astype(low)
    late = total(exchange(late.reshape(groups, shard, 384), CTX))
    late = total(spread(late, CHIPS, 8))
    late = jnp.concatenate(ordered(core, late, swap_cores(late)), axis=1).astype(jnp.float32)

    expand_sum = total(exchange(expand_sum.reshape(8, shard // 8, FF), CHIPS))
    expand_sum = spread(expand_sum, CHIPS, 8).reshape(shard, FF)
    expand_one, expand_two = ordered(core, expand_sum, swap_cores(expand_sum))
    whole_expand = jnp.concatenate(
        [
            part[:, k * hidden_shard : (k + 1) * hidden_shard]
            for k in range(16)
            for part in (expand_one, expand_two)
        ],
        axis=1,
    ).astype(jnp.float32)
    rest = jnp.concatenate(
        [
            down_sum.reshape(8, hidden_shard // 8, width),
            early.reshape(8, shard // 8, width),
        ],
        axis=1,
    )
    rest = spread(total(exchange(rest, CHIPS)), CHIPS, 8)
    rest_one, rest_two = ordered(core, rest, swap_cores(rest))
    piece = hidden_shard // 8
    whole_down = jnp.concatenate(
        [part[:, :piece].reshape(hidden_shard, width) for part in (rest_one, rest_two)], axis=0
    ).astype(jnp.float32)
    whole_qkv = jnp.concatenate(
        [
            rest_one[:, piece:].reshape(shard, width).astype(jnp.float32),
            late[:, : 2 * kv_width],
        ],
        axis=1,
    )
    whole_proj = rest_two[:, piece:].reshape(shard, width).astype(jnp.float32)
    whole_gains = late[:, 2 * kv_width : 2 * kv_width + 2].T

    new_qkv, qkv_mean, qkv_square = adam_step(
        w_qkv, qkv_first, qkv_second, whole_qkv, 2.0 * D ** (-0.5), 0.1
    )
    new_proj, proj_mean, proj_square = adam_step(
        w_proj, proj_first, proj_second, whole_proj, 2.0 * (D // 8) ** (-0.5), 0.1
    )
    new_expand, expand_mean, expand_square = adam_step(
        w_expand, expand_first, expand_second, whole_expand, 2.0 * D ** (-0.5), 0.1
    )
    new_down, down_mean, down_square = adam_step(
        w_down, down_first, down_second, whole_down, 2.0 * FF ** (-0.5), 0.1
    )
    new_gains, gains_mean, gains_square = adam_step(
        gains, gains_first, gains_second, whole_gains, 1.0, 0.0
    )
    return (
        output.reshape(batch, local, width),
        input_grad,
        new_qkv,
        qkv_mean,
        qkv_square,
        new_proj,
        proj_mean,
        proj_square,
        new_expand,
        expand_mean,
        expand_square,
        new_down,
        down_mean,
        down_square,
        new_gains,
        gains_mean,
        gains_square,
    )


def solution(mesh):
    parts = jax.sharding.Mesh(mesh.devices.reshape(2, 4, 2, 2, 4), AXES)
    dp, ctx = ("zh", "y", "core"), CTX
    rows = P(dp, ctx, None)
    owned = P(ctx, None)
    split = P(None, ctx)
    return jax.shard_map(
        on_device,
        mesh=parts,
        in_specs=(rows, rows, P()) + (owned,) * 12 + (split,) * 3,
        out_specs=(rows, rows) + (owned,) * 12 + (split,) * 3,
        check_vma=False,
    )
```

```python
import functools

import jax
import jax.numpy as jnp
from jax import lax
from jax.experimental import pallas as pl
from jax.experimental.pallas import tpu as pltpu
from jax.sharding import PartitionSpec as P

D = 960
HEADS = 15
KV_HEADS = 5
GROUP = HEADS // KV_HEADS
HEAD_DIM = 64
FF = 2560
STEP = 10
HALF = FF // 2
QKVW = D + 2 * KV_HEADS * HEAD_DIM


eps = 1e-05
rope_base = 100000.0
beta_first = 0.9
beta_second = 0.95
adam_eps = 1e-08
masked_score = -1e30
TALL = 56
PADDED = 896
NEAR = 1408
ATTEND_FLOPS = 20 * 10**9
BACK_FLOPS = 25 * 10**9
FEED_FLOPS = 20 * 10**9
low = jnp.bfloat16


AXES = ("zh", "y", "core", "zl", "x")
CHIPS = ("zh", "y")
CTX = ("zl", "x")


def swap_cores(value):
    return lax.ppermute(value, "core", [(0, 1), (1, 0)])


def to_peer(value, axis, k):
    count = lax.axis_size(axis)
    return lax.ppermute(value, axis, [(i, i ^ k) for i in range(count)])


def double(piece, axis, k, side):
    bit = lax.axis_index(axis) // k % 2 == 0
    came = to_peer(piece, axis, k)
    return jnp.concatenate(
        [jnp.where(bit, piece, came), jnp.where(bit, came, piece)], axis=side
    )


def add_peer(piece, axis, k):
    return (piece.astype(jnp.float32) + to_peer(piece, axis, k).astype(jnp.float32)).astype(low)


def exchange(stack, axes):
    return lax.all_to_all(stack, axes, 0, 0, tiled=True)


def spread(piece, axes, count):
    return exchange(jnp.broadcast_to(piece[None], (count,) + piece.shape), axes)


def total(stack):
    return jnp.sum(stack.astype(jnp.float32), axis=0).astype(low)


def ordered(core, mine, theirs):
    first = core == 0
    return jnp.where(first, mine, theirs), jnp.where(first, theirs, mine)


def rope_tables(positions):
    halfway = HEAD_DIM // 2
    freqs = rope_base ** (-(jnp.arange(halfway, dtype=jnp.float32) * 2.0) / HEAD_DIM)
    angles = freqs[:, None] * positions.astype(jnp.float32)[None, :]
    return (jnp.cos(angles), jnp.sin(angles))


def rms_scale(rows):
    return lax.rsqrt(jnp.mean(rows * rows, axis=-1, keepdims=True) + eps)


def contract(left, right, left_axis, right_axis):
    return lax.dot_general(
        left,
        right,
        (((left_axis,), (right_axis,)), ((), ())),
        preferred_element_type=jnp.float32,
    )


def load_keys(kv_ref):
    columns = jnp.concatenate([kv_ref[j, 0] for j in range(kv_ref.shape[0])], axis=1)
    return columns, columns.T


def fill_bias(order_ref, own_ref, bias_ref):
    slots = order_ref.shape[0]
    span = bias_ref.shape[0] // slots
    ahead = lax.broadcasted_iota(jnp.int32, (span, span), 0) - lax.broadcasted_iota(
        jnp.int32, (span, span), 1
    )
    for s in range(slots):
        for t in range(own_ref.shape[0]):
            gap = (order_ref[s] - own_ref[t]) * span
            bias_ref[s * span : (s + 1) * span, t * span : (t + 1) * span] = jnp.where(
                ahead + gap <= 0, 0.0, masked_score
            )


def attend_kernel(order_ref, own_ref, q_ref, kv_ref, o_ref, lse_ref, bias_ref):
    @pl.when(pl.program_id(0) == 0)
    def _():
        fill_bias(order_ref, own_ref, bias_ref)

    columns, rows = load_keys(kv_ref)
    bias = bias_ref[...]
    blank = jnp.zeros((HEAD_DIM, q_ref.shape[1]), low)
    for h in range(GROUP):
        part = pl.ds(h * HEAD_DIM, HEAD_DIM)
        query = jnp.concatenate([q_ref[part, :], blank], axis=0)
        scores = contract(rows, query, 1, 0) + bias
        top = jnp.max(scores, axis=0, keepdims=True)
        weights = jnp.exp(scores - top)
        total = jnp.sum(weights, axis=0, keepdims=True)
        mixed = contract(columns[HEAD_DIM:], weights.astype(low), 1, 0)
        o_ref[part, :] = (mixed / total).astype(low)
        lse_ref[h] = top + jnp.log(total)


def attend_back_kernel(
    order_ref, own_ref, q_ref, kv_ref, do_ref, o_ref, lse_ref, dq_ref, dkv_ref, bias_ref
):
    @pl.when(pl.program_id(0) == 0)
    def _():
        fill_bias(order_ref, own_ref, bias_ref)

    columns, rows = load_keys(kv_ref)
    bias = bias_ref[...]
    local = q_ref.shape[1]
    blank = jnp.zeros((HEAD_DIM, local), low)
    terms = None
    for h in range(GROUP):
        part = pl.ds(h * HEAD_DIM, HEAD_DIM)
        query = jnp.concatenate([q_ref[part, :], blank], axis=0)
        back = jnp.concatenate([blank, do_ref[part, :]], axis=0)
        delta = jnp.sum(
            do_ref[part, :].astype(jnp.float32) * o_ref[part, :].astype(jnp.float32),
            axis=0,
            keepdims=True,
        )
        weights = jnp.exp(contract(rows, query, 1, 0) + bias - lse_ref[h])
        grad = contract(rows, back, 1, 0)
        scores = (weights * (grad - delta)).astype(low)
        dq_ref[part, :] = contract(columns[:HEAD_DIM], scores, 1, 0) * HEAD_DIM ** (-0.5)
        term = contract(scores, query, 1, 1) + contract(weights.astype(low), back, 1, 1)
        terms = term if terms is None else terms + term
    for j in range(dkv_ref.shape[0]):
        dkv_ref[j, 0] = terms[j * local : (j + 1) * local].astype(low)


def attention_specs(chunks, local):
    wide = GROUP * HEAD_DIM
    heads = pl.BlockSpec((wide, local), lambda g: (g, 0))
    keys = pl.BlockSpec((chunks, 1, 2 * HEAD_DIM, local), lambda g: (0, g, 0, 0))
    sums = pl.BlockSpec((GROUP, 1, local), lambda g: (g, 0, 0))
    return heads, keys, sums


def scalars():
    return pl.BlockSpec(memory_space=pltpu.SMEM)


def attend(order, own, query, keys):
    chunks, _, _, local = keys.shape
    heads, kv, sums = attention_specs(chunks, local)
    return pl.pallas_call(
        attend_kernel,
        grid=(KV_HEADS,),
        out_shape=(
            jax.ShapeDtypeStruct((D, local), low),
            jax.ShapeDtypeStruct((HEADS, 1, local), jnp.float32),
        ),
        in_specs=[scalars(), scalars(), heads, kv],
        out_specs=(heads, sums),
        scratch_shapes=[pltpu.VMEM((chunks * local, local), jnp.float32)],
        compiler_params=pltpu.CompilerParams(vmem_limit_bytes=48 * 1024 * 1024),
        cost_estimate=pl.CostEstimate(
            flops=ATTEND_FLOPS, bytes_accessed=1000, transcendentals=0
        ),
        name="attend",
    )(order, own, query, keys)


def attend_back(order, own, query, keys, back, out, lse):
    chunks, _, _, local = keys.shape
    heads, kv, sums = attention_specs(chunks, local)
    grads = pl.BlockSpec((chunks, 1, local, 2 * HEAD_DIM), lambda g: (0, g, 0, 0))
    return pl.pallas_call(
        attend_back_kernel,
        grid=(KV_HEADS,),
        out_shape=(
            jax.ShapeDtypeStruct((D, local), jnp.float32),
            jax.ShapeDtypeStruct((chunks, KV_HEADS, local, 2 * HEAD_DIM), low),
        ),
        in_specs=[scalars(), scalars(), heads, kv, heads, heads, sums],
        out_specs=(heads, grads),
        scratch_shapes=[pltpu.VMEM((chunks * local, local), jnp.float32)],
        compiler_params=pltpu.CompilerParams(vmem_limit_bytes=48 * 1024 * 1024),
        cost_estimate=pl.CostEstimate(
            flops=BACK_FLOPS, bytes_accessed=1000, transcendentals=0
        ),
        name="attend_back",
    )(order, own, query, keys, back, out, lse)


def whole_call(kernel, name, flops, out_shape, *operands):
    whole = pl.BlockSpec(memory_space=pltpu.VMEM)
    return pl.pallas_call(
        kernel,
        out_shape=out_shape,
        in_specs=[scalars() if value.ndim == 1 else whole for value in operands],
        out_specs=jax.tree.map(lambda _: whole, out_shape),
        compiler_params=pltpu.CompilerParams(vmem_limit_bytes=48 * 1024 * 1024),
        cost_estimate=pl.CostEstimate(flops=flops, bytes_accessed=1000, transcendentals=0),
        name=name,
    )(*operands)


def stage_kernel(
    place_ref, qkv_ref, proj_ref, expand_ref, down_ref, gains_ref, near_ref, wide_ref, tall_ref
):
    first = place_ref[0] == 0
    shard = qkv_ref.shape[0]
    step = FF // 16
    gains = jnp.concatenate(
        [gains_ref[...], jnp.zeros((6, gains_ref.shape[1]), jnp.float32)], axis=0
    )
    gains = jnp.concatenate([gains, jnp.zeros((8, 128 - shard), jnp.float32)], axis=1).T
    near = jnp.concatenate(
        [
            jnp.where(first, qkv_ref[:, : QKVW // 2], qkv_ref[:, QKVW // 2 :]),
            gains[:shard, :2],
            jnp.zeros((shard, PADDED - QKVW // 2 - 2), jnp.float32),
            jnp.where(first, proj_ref[:, : D // 2], proj_ref[:, D // 2 :]),
            jnp.zeros((shard, NEAR - PADDED - D // 2), jnp.float32),
        ],
        axis=1,
    ).astype(low)
    parts = []
    for k in range(4):
        left = expand_ref[:, 2 * k * step : (2 * k + 1) * step]
        right = expand_ref[:, (2 * k + 1) * step : (2 * k + 2) * step]
        parts.append(jnp.where(first, left, right))
    wide = jnp.concatenate(parts, axis=1).astype(low)
    tall = down_ref[...].astype(low)
    for j in range(near_ref.shape[0]):
        near_ref[j] = near
        wide_ref[j] = wide
        tall_ref[j] = tall


def stage(place, qkv, proj, expand, down, gains, groups):
    shard = qkv.shape[0]
    half = down.shape[0] // 2

    def whole(value):
        return pl.BlockSpec(value.shape, lambda i, place: (0, 0))

    outs = [(groups, shard, NEAR), (groups, shard, FF // 4), (groups, half, D)]
    return pl.pallas_call(
        stage_kernel,
        grid_spec=pltpu.PrefetchScalarGridSpec(
            num_scalar_prefetch=1,
            grid=(1,),
            in_specs=[
                whole(qkv),
                whole(proj),
                pl.BlockSpec((shard, HALF), lambda i, place: (0, place[1])),
                pl.BlockSpec((half, D), lambda i, place: (place[0], 0)),
                whole(gains),
            ],
            out_specs=[pl.BlockSpec(out, lambda i, place: (0, 0, 0)) for out in outs],
        ),
        out_shape=[jax.ShapeDtypeStruct(out, low) for out in outs],
        compiler_params=pltpu.CompilerParams(vmem_limit_bytes=40 * 1024 * 1024),
        cost_estimate=pl.CostEstimate(flops=1000, bytes_accessed=8 * 10**6, transcendentals=0),
        name="stage",
    )(place, qkv, proj, expand, down, gains)


def rotated(block, cosine, sine):
    first = block[: HEAD_DIM // 2]
    second = block[HEAD_DIM // 2 :]
    return [first * cosine - second * sine, second * cosine + first * sine]


def project_kernel(
    core_ref,
    rows_ref,
    mine_ref,
    theirs_ref,
    cosine_ref,
    sine_ref,
    normed_ref,
    query_ref,
    keys_ref,
    gains_ref,
):
    first_core = core_ref[0] == 0
    cosine = cosine_ref[...]
    sine = sine_ref[...]
    rows = rows_ref[...].astype(jnp.float32).T
    gains = mine_ref[:, PADDED - 128 : PADDED].astype(jnp.float32).T
    at = QKVW // 2 - (PADDED - 128)
    gains_ref[...] = gains[at : at + 2]
    normed = (rows * rms_scale(rows) * gains[at : at + 1]).astype(low)
    normed_ref[...] = normed
    near = contract(normed, mine_ref[:, :PADDED], 1, 0).T
    away = contract(normed, theirs_ref[:, :PADDED], 1, 0).T
    half = QKVW // 2
    one = jnp.where(first_core, near, away)[:half]
    two = jnp.where(first_core, away, near)[:half]
    mixed = jnp.concatenate([one, two], axis=0)
    scale = HEAD_DIM ** (-0.5)
    for h in range(HEADS):
        span = slice(h * HEAD_DIM, (h + 1) * HEAD_DIM)
        turned = jnp.concatenate(rotated(mixed[span], cosine, sine), axis=0)
        query_ref[span] = (turned.astype(low).astype(jnp.float32) * scale).astype(low)
    for g in range(KV_HEADS):
        at = D + g * HEAD_DIM
        to = at + KV_HEADS * HEAD_DIM
        pair = rotated(mixed[at : at + HEAD_DIM], cosine, sine) + [mixed[to : to + HEAD_DIM]]
        pair = jnp.concatenate(pair, axis=0).astype(low)
        for j in range(keys_ref.shape[0]):
            keys_ref[j, g] = pair


def middle_kernel(core_ref, out_ref, mine_ref, theirs_ref, rows_ref, gains_ref, mid_ref, normed_ref):
    first_core = core_ref[0] == 0
    mixed = out_ref[...].T
    near = contract(mixed, mine_ref[:, PADDED : PADDED + D // 2], 1, 0)
    away = contract(mixed, theirs_ref[:, PADDED : PADDED + D // 2], 1, 0)
    near, away = jnp.where(first_core, near, away), jnp.where(first_core, away, near)
    middle = rows_ref[...].astype(jnp.float32).T + jnp.concatenate([near, away], axis=1)
    mid_ref[...] = middle
    normed_ref[...] = (middle * rms_scale(middle) * gains_ref[1:2]).astype(low)


def turn_kernel(
    core_ref,
    own_ref,
    came_ref,
    mid_ref,
    back_ref,
    gains_ref,
    mine_ref,
    theirs_ref,
    out_ref,
    grad_ref,
    grad_out_ref,
    kept_ref,
    sent_ref,
    gain_grad_ref,
):
    first_core = core_ref[0] == 0
    normed = own_ref[...] + came_ref[...].astype(jnp.float32)
    middle = mid_ref[...]
    inverse = rms_scale(middle)
    scaled = normed * gains_ref[1:2]
    inner = jnp.mean(scaled * middle, axis=-1, keepdims=True)
    grad = back_ref[...].astype(jnp.float32) + inverse * (
        scaled - middle * inverse * inverse * inner
    )
    grad_ref[...] = grad
    gain_grad_ref[...] = jnp.sum(normed * middle * inverse, axis=0, keepdims=True)
    one = grad[:, : D // 2]
    two = grad[:, D // 2 :]
    near = jnp.where(first_core, one, two).astype(low)
    away = jnp.where(first_core, two, one).astype(low)
    grad_out = contract(near, mine_ref[:, PADDED : PADDED + D // 2], 1, 1) + contract(
        away, theirs_ref[:, PADDED : PADDED + D // 2], 1, 1
    )
    grad_out_ref[...] = grad_out.T.astype(low)
    product = contract(out_ref[...], grad.astype(low), 1, 0)
    groups, window, _ = kept_ref.shape
    shard = product.shape[0] // groups
    for j in range(groups):
        top = product[j * shard : j * shard + window]
        bottom = product[(j + 1) * shard - window : (j + 1) * shard]
        kept_ref[j] = jnp.where(first_core, top, bottom).astype(low)
        sent_ref[j] = jnp.where(first_core, bottom, top).astype(low)


def emit_kernel(mid_ref, own_ref, came_ref, out_ref):
    value = mid_ref[...] + own_ref[...] + came_ref[...].astype(jnp.float32)
    out_ref[...] = value.T.astype(low)


def feed_kernel(
    rows_one,
    rows_two,
    back_one,
    back_two,
    expand_ref,
    down_ref,
    fed_ref,
    fed_other_ref,
    normed_ref,
    normed_other_ref,
    down_grad_ref,
    expand_grad_ref,
    rows_ref,
    back_ref,
    columns_ref,
    fed_sum,
    normed_sum,
):
    local = rows_one.shape[0]
    h = pl.program_id(0)

    @pl.when(h == 0)
    def _():
        rows_ref[:local] = rows_one[...]
        rows_ref[local:] = rows_two[...]
        back_ref[:local] = back_one[...]
        back_ref[local:] = back_two[...]
        columns_ref[...] = rows_ref[...].T

    rows = rows_ref[...]
    back = back_ref[...]
    columns = columns_ref[...]
    wide_gate = expand_ref[0]
    wide_up = expand_ref[1]
    down = down_ref[...]
    gate = contract(rows, wide_gate, 1, 0)
    upward = contract(rows, wide_up, 1, 0)
    sigmoid = jax.nn.sigmoid(gate)
    active = gate * sigmoid
    hidden = (active * upward).astype(low)
    grad_hidden = contract(back, down, 1, 1)
    grad_up = (grad_hidden * active).astype(low)
    grad_gate = (grad_hidden * upward * sigmoid * (1.0 + gate * (1.0 - sigmoid))).astype(low)
    fed = contract(hidden, down, 1, 0)
    normed = contract(grad_gate, wide_gate, 1, 1) + contract(grad_up, wide_up, 1, 1)
    down_grad_ref[...] = contract(hidden.T, back, 1, 0).astype(low)
    expand_grad_ref[0] = contract(columns, grad_gate, 1, 0).astype(low)
    expand_grad_ref[1] = contract(columns, grad_up, 1, 0).astype(low)

    @pl.when(h == 0)
    def _():
        fed_sum[...] = fed
        normed_sum[...] = normed

    @pl.when(h == 1)
    def _():
        fed_all = fed_sum[...] + fed
        normed_all = normed_sum[...] + normed
        fed_ref[...] = fed_all[:local]
        fed_other_ref[...] = fed_all[local:].astype(low)
        normed_ref[...] = normed_all[:local]
        normed_other_ref[...] = normed_all[local:].astype(low)


def feed(rows, back, expand, down):
    local, width = rows[0].shape
    _, _, step = expand.shape
    held = pl.BlockSpec((local, width), lambda h: (0, 0))
    pair = pl.BlockSpec((2, width, step), lambda h: (h, 0, 0))
    tall = pl.BlockSpec((step, width), lambda h: (h, 0))
    own = jax.ShapeDtypeStruct((local, width), jnp.float32)
    other = jax.ShapeDtypeStruct((local, width), low)
    return pl.pallas_call(
        feed_kernel,
        grid=(2,),
        out_shape=(
            own,
            other,
            own,
            other,
            jax.ShapeDtypeStruct(down.shape, low),
            jax.ShapeDtypeStruct(expand.shape, low),
        ),
        in_specs=[held] * 4 + [pair, tall],
        out_specs=(held,) * 4 + (tall, pair),
        scratch_shapes=[
            pltpu.VMEM((2 * local, width), low),
            pltpu.VMEM((2 * local, width), low),
            pltpu.VMEM((width, 2 * local), low),
            pltpu.VMEM((2 * local, width), jnp.float32),
            pltpu.VMEM((2 * local, width), jnp.float32),
        ],
        compiler_params=pltpu.CompilerParams(vmem_limit_bytes=56 * 1024 * 1024),
        cost_estimate=pl.CostEstimate(flops=FEED_FLOPS, bytes_accessed=1000, transcendentals=0),
        name="feed",
    )(*rows, *back, expand, down)


def stack_tall(down, kept, came):
    groups, window, width = kept.shape
    proj = (kept.astype(jnp.float32) + came.astype(jnp.float32)).astype(low)
    parts = [down.reshape(groups, 4, -1, width), proj.reshape(groups, 4, window // 4, width)]
    tall = jnp.concatenate([jnp.transpose(part, (1, 0, 2, 3)) for part in parts], axis=2)
    return tall.reshape(4, groups * TALL, width)


def adam_step(master, first, second, grad, rate, decay):
    new_first = beta_first * first + (1.0 - beta_first) * grad
    new_second = beta_second * second + (1.0 - beta_second) * grad * grad
    fix_one = 1.0 - beta_first**STEP
    fix_two = 1.0 - beta_second**STEP
    update = new_first / fix_one / (jnp.sqrt(new_second / fix_two) + adam_eps) + decay * master
    return (master - rate * update, new_first, new_second)


def adam_kernel(assemble, rate, core_ref, mine, theirs, master, first, second, *outs):
    core = core_ref[0]
    one = jnp.where(core == 0, mine[...], theirs[...]).astype(jnp.float32)
    two = jnp.where(core == 0, theirs[...], mine[...]).astype(jnp.float32)
    grad = assemble(one, two)
    new = adam_step(master[...], first[...], second[...], grad, rate, 0.1)
    for out, value in zip(outs, new):
        out[...] = value


def adam(assemble, rate, core, mine, theirs, state, grid, grad_spec, state_spec, name):
    return pl.pallas_call(
        functools.partial(adam_kernel, assemble, rate),
        grid=grid,
        out_shape=(jax.ShapeDtypeStruct(state[0].shape, jnp.float32),) * 3,
        in_specs=[pl.BlockSpec(memory_space=pltpu.SMEM)] + [grad_spec] * 2 + [state_spec] * 3,
        out_specs=(state_spec,) * 3,
        compiler_params=pltpu.CompilerParams(vmem_limit_bytes=32 * 1024 * 1024),
        cost_estimate=pl.CostEstimate(
            flops=1000, bytes_accessed=24 * state[0].size, transcendentals=0
        ),
        name=name,
    )(core.reshape(1), mine, theirs, *state)


def back_rotated(block, cosine, sine):
    first = block[: HEAD_DIM // 2]
    second = block[HEAD_DIM // 2 :]
    return [first * cosine + second * sine, second * cosine - first * sine]


def early_kernel(
    core_ref, dq_ref, cosine_ref, sine_ref, normed_ref, mixed_ref, kept_ref, sent_ref
):
    cosine = cosine_ref[...]
    sine = sine_ref[...]
    first_core = core_ref[0] == 0
    parts = []
    for h in range(HEADS):
        parts += back_rotated(dq_ref[h * HEAD_DIM : (h + 1) * HEAD_DIM], cosine, sine)
    mixed = jnp.concatenate(parts, axis=0)
    mixed_ref[...] = mixed.astype(low)
    weight_halves(first_core, mixed, normed_ref[...].T, None, kept_ref, sent_ref)


def weight_halves(first_core, mixed, columns, gains, kept_ref, sent_ref):
    half = mixed.shape[0] // 2
    blank = jnp.zeros((kept_ref.shape[2] - half, mixed.shape[1]), jnp.float32)
    one = mixed[:half]
    two = mixed[half:]
    near = jnp.concatenate([jnp.where(first_core, one, two), blank], axis=0).T.astype(low)
    away = jnp.concatenate([jnp.where(first_core, two, one), blank], axis=0).T.astype(low)
    groups, rows, lanes = kept_ref.shape
    shard = columns.shape[0] // groups
    for ref, side in ((kept_ref, near), (sent_ref, away)):
        product = contract(columns, side, 1, 0)
        for j in range(groups):
            span = slice(j * shard, (j + 1) * shard)
            tail = jnp.zeros((rows - shard, lanes), jnp.float32)
            if gains is not None:
                tail = jnp.concatenate(
                    [gain[:, span] for gain in gains]
                    + [jnp.zeros((rows - shard - len(gains), shard), jnp.float32)],
                    axis=0,
                )
                tail = jnp.concatenate(
                    [tail, jnp.zeros((rows - shard, lanes - shard), jnp.float32)], axis=1
                )
            ref[j] = jnp.concatenate([product[span], tail], axis=0).astype(low)


def late_kernel(
    core_ref,
    terms_ref,
    mixed_ref,
    cosine_ref,
    sine_ref,
    normed_ref,
    mine_ref,
    theirs_ref,
    rows_ref,
    grad_ref,
    gain_ref,
    gain_grad_ref,
    out_ref,
    kept_ref,
    sent_ref,
):
    cosine = cosine_ref[...]
    sine = sine_ref[...]
    first_core = core_ref[0] == 0
    local = mixed_ref.shape[1]
    parts = []
    values = []
    for g in range(KV_HEADS):
        block = terms_ref[0, g].astype(jnp.float32)
        for j in range(1, terms_ref.shape[0]):
            block = block + terms_ref[j, g].astype(jnp.float32)
        block = block.T
        parts += back_rotated(block[:HEAD_DIM], cosine, sine)
        values.append(block[HEAD_DIM:])
    pair = jnp.concatenate(parts + values, axis=0)
    mixed = jnp.concatenate([mixed_ref[...].astype(jnp.float32), pair], axis=0)
    blank = jnp.zeros((PADDED - QKVW // 2, local), jnp.float32)
    one = mixed[: QKVW // 2]
    two = mixed[QKVW // 2 :]
    near = jnp.concatenate([jnp.where(first_core, one, two), blank], axis=0).T.astype(low)
    away = jnp.concatenate([jnp.where(first_core, two, one), blank], axis=0).T.astype(low)
    grad_normed = contract(near, mine_ref[:, :PADDED], 1, 1) + contract(
        away, theirs_ref[:, :PADDED], 1, 1
    )
    rows = rows_ref[...].astype(jnp.float32).T
    inverse = rms_scale(rows)
    scaled = grad_normed * gain_ref[0:1]
    inner = jnp.mean(scaled * rows, axis=-1, keepdims=True)
    back = inverse * (scaled - rows * inverse * inverse * inner)
    out_ref[...] = (grad_ref[...] + back).T.astype(low)
    gain_one = jnp.sum(grad_normed * rows * inverse, axis=0, keepdims=True)
    gains = (gain_one, gain_grad_ref[...])
    weight_halves(first_core, pair, normed_ref[...].T, gains, kept_ref, sent_ref)


def padded_rows(block, rows):
    return jnp.concatenate(
        [block, jnp.zeros((rows - block.shape[0], block.shape[1]), jnp.float32)], axis=0
    )


def pack_early_kernel(kept_ref, came_ref, expand_ref, out_ref):
    for j in range(out_ref.shape[0]):
        summed = kept_ref[j].astype(jnp.float32) + came_ref[j].astype(jnp.float32)
        expand = padded_rows(expand_ref[j].astype(jnp.float32), summed.shape[0])
        out_ref[j] = jnp.concatenate([summed, expand], axis=1).astype(low)


def pack_late_kernel(kept_ref, came_ref, tall_ref, out_ref):
    for j in range(out_ref.shape[0]):
        summed = kept_ref[j].astype(jnp.float32) + came_ref[j].astype(jnp.float32)
        tall = tall_ref[j].astype(jnp.float32)
        rows = summed.shape[0] // 2
        side = jnp.concatenate(
            [tall[:, 512:], jnp.zeros((tall.shape[0], 1024 - tall.shape[1]), jnp.float32)], axis=1
        )
        tall = jnp.concatenate([padded_rows(tall[:, :512], rows), padded_rows(side, rows)], axis=0)
        out_ref[j] = jnp.concatenate([summed, tall], axis=1).astype(low)


def sum_kernel(early_ref, late_ref, out_ref):
    sums = []
    for ref in (early_ref, late_ref):
        block = ref[0].astype(jnp.float32)
        for j in range(1, ref.shape[0]):
            block = block + ref[j].astype(jnp.float32)
        sums.append(block.astype(low))
    block = jnp.concatenate(sums, axis=1)
    for j in range(out_ref.shape[0]):
        out_ref[j] = block


def finish_kernel(all_ref, wide_ref, rest_ref):
    count = all_ref.shape[0]
    early = slice(0, 512)
    late = slice(512 + FF // 4, 512 + FF // 4 + 384)
    expand = slice(512, 512 + FF // 4)
    tall = slice(512 + FF // 4 + 384, 1024 + FF // 4 + 384)
    sums = []
    for span in (early, late):
        block = all_ref[0, :, span].astype(jnp.float32)
        for j in range(1, count):
            block = block + all_ref[j, :, span].astype(jnp.float32)
        sums.append(block.astype(low))
    wide_ref[...] = jnp.concatenate(sums, axis=1)
    for q in range(count // 2):
        parts = []
        for span in (expand, tall):
            pair = all_ref[q, :, span].astype(jnp.float32)
            pair = pair + all_ref[q + count // 2, :, span].astype(jnp.float32)
            parts.append(pair.astype(low))
        rest_ref[q] = jnp.concatenate(parts, axis=1)


def tall_part(rest, q):
    half = rest.shape[1] // 2
    left = rest[q, :TALL, FF // 4 :]
    right = rest[q, half : half + TALL, FF // 4 : FF // 4 + D - 512]
    return jnp.concatenate([left, right], axis=1)


def weave(one, two):
    step = FF // 16
    parts = []
    for k in range(4):
        span = slice(k * step, (k + 1) * step)
        parts += [one[0, : D // 8, span], two[0, : D // 8, span]]
    return jnp.concatenate(parts, axis=1)


def on_device(
    inputs,
    cotangent,
    span_order,
    w_qkv,
    qkv_first,
    qkv_second,
    w_proj,
    proj_first,
    proj_second,
    w_expand,
    expand_first,
    expand_second,
    w_down,
    down_first,
    down_second,
    gains,
    gains_first,
    gains_second,
):
    core = lax.axis_index("core")
    rank = lax.axis_index(CTX)
    groups = 8
    batch, local, width = inputs.shape
    shard = w_qkv.shape[0]
    hidden_shard = w_down.shape[0] // 2

    y = lax.axis_index("y")
    place = jnp.stack([core, y % 2 * 2 + y // 2]).astype(jnp.int32)
    core_at = place[:1]
    near, expand_low, down_low = stage(place, w_qkv, w_proj, w_expand, w_down, gains, groups)
    mine = exchange(near, CTX).reshape(width, NEAR)
    order_own = lax.dynamic_slice_in_dim(span_order, 2 * rank, 2)
    own_pos = (
        order_own[:, None] * (local // 2) + jnp.arange(local // 2, dtype=jnp.int32)
    ).reshape(local)
    cosine, sine = rope_tables(own_pos)
    mine, cosine, sine, expand_low = lax.optimization_barrier((mine, cosine, sine, expand_low))
    theirs = swap_cores(mine)
    expand_low = exchange(expand_low, CTX).reshape(width, FF // 4)

    tokens = inputs.reshape(local, width).T
    square = (local, width)
    normed_one, query, all_keys, full_gains = whole_call(
        project_kernel,
        "project",
        1000,
        (
            jax.ShapeDtypeStruct(square, low),
            jax.ShapeDtypeStruct((width, local), low),
            jax.ShapeDtypeStruct((groups, KV_HEADS, 2 * HEAD_DIM, local), low),
            jax.ShapeDtypeStruct((2, width), jnp.float32),
        ),
        core_at,
        tokens,
        mine,
        theirs,
        cosine,
        sine,
    )
    all_keys, expand_low = lax.optimization_barrier((all_keys, expand_low))
    expand_low = lax.all_gather(expand_low, "y", axis=0, tiled=False)
    all_keys = exchange(all_keys, CTX)
    all_keys, down_low = lax.optimization_barrier((all_keys, down_low))
    half_down = exchange(down_low, CTX).reshape(HALF, width)
    attended, lse = attend(span_order, order_own, query, all_keys)
    middle, normed_two = whole_call(
        middle_kernel,
        "middle",
        2 * 10**9,
        (jax.ShapeDtypeStruct(square, jnp.float32), jax.ShapeDtypeStruct(square, low)),
        core_at,
        attended,
        mine,
        theirs,
        tokens,
        full_gains,
    )
    normed_two, half_down = lax.optimization_barrier((normed_two, half_down))

    back_rows = cotangent.reshape(local, width)
    fed, fed_other, grad_normed, grad_other, grad_down, grad_expand = feed(
        (normed_two, swap_cores(normed_two)),
        (back_rows, swap_cores(back_rows)),
        expand_low,
        half_down,
    )
    grad_middle, grad_att, proj_kept, proj_sent, gain_grad_two = whole_call(
        turn_kernel,
        "turn",
        3 * 10**9,
        (
            jax.ShapeDtypeStruct(square, jnp.float32),
            jax.ShapeDtypeStruct((width, local), low),
            jax.ShapeDtypeStruct((groups, 64, width), low),
            jax.ShapeDtypeStruct((groups, 64, width), low),
            jax.ShapeDtypeStruct((1, width), jnp.float32),
        ),
        core_at,
        grad_normed,
        swap_cores(grad_other),
        middle,
        back_rows,
        full_gains,
        mine,
        theirs,
        attended,
    )
    output = whole_call(
        emit_kernel,
        "emit",
        1000,
        jax.ShapeDtypeStruct((width, local), low),
        middle,
        fed,
        swap_cores(fed_other),
    )

    expand_sum = lax.psum_scatter(grad_expand, "y", scatter_dimension=0, tiled=False)
    grad_query, key_terms = attend_back(
        span_order, order_own, query, all_keys, grad_att, attended, lse
    )
    key_terms, proj_sent = lax.optimization_barrier((key_terms, proj_sent))
    tall = lax.psum_scatter(
        stack_tall(grad_down, proj_kept, swap_cores(proj_sent)),
        "y",
        scatter_dimension=0,
        tiled=False,
    )
    key_terms = exchange(key_terms, CTX)
    key_terms, output, expand_sum = lax.optimization_barrier((key_terms, output, expand_sum))
    early_half = jax.ShapeDtypeStruct((groups, 128, 512), low)
    query_mixed, kept, sent = whole_call(
        early_kernel,
        "early",
        6 * 10**9,
        (jax.ShapeDtypeStruct((width, local), low), early_half, early_half),
        core_at,
        grad_query,
        cosine,
        sine,
        normed_one,
    )
    early = whole_call(
        pack_early_kernel,
        "pack_early",
        1000,
        jax.ShapeDtypeStruct((groups, 128, 512 + FF // 4), low),
        kept,
        swap_cores(sent),
        expand_sum.reshape(groups, shard, FF // 4),
    )
    early, key_terms = lax.optimization_barrier((early, key_terms))
    early = exchange(early, CTX)
    late_half = jax.ShapeDtypeStruct((groups, 128, 384), low)
    input_grad, kept, sent = whole_call(
        late_kernel,
        "late",
        8 * 10**9,
        (jax.ShapeDtypeStruct((width, local), low), late_half, late_half),
        core_at,
        key_terms,
        query_mixed,
        cosine,
        sine,
        normed_one,
        mine,
        theirs,
        tokens,
        grad_middle,
        full_gains,
        gain_grad_two,
    )
    sent, early = lax.optimization_barrier((sent, early))
    late = whole_call(
        pack_late_kernel,
        "pack_late",
        1000,
        jax.ShapeDtypeStruct((groups, 128, 384 + 512), low),
        kept,
        swap_cores(sent),
        tall.reshape(groups, TALL, width),
    )
    late = exchange(late, CTX)
    parts = whole_call(
        sum_kernel,
        "sum_parts",
        1000,
        jax.ShapeDtypeStruct((8, 128, 512 + FF // 4 + 384 + 512), low),
        early,
        late,
    )
    wide, rest = whole_call(
        finish_kernel,
        "finish",
        1000,
        (
            jax.ShapeDtypeStruct((128, 512 + 384), low),
            jax.ShapeDtypeStruct((4, 128, FF // 4 + 512), low),
        ),
        exchange(parts, CHIPS),
    )
    wide_other = swap_cores(wide)
    rest_other = swap_cores(rest)
    quarter = hidden_shard // 4
    new_expand, expand_mean, expand_square = adam(
        weave,
        2.0 * D ** (-0.5),
        core,
        rest,
        rest_other,
        (w_expand, expand_first, expand_second),
        (4,),
        pl.BlockSpec((1,) + rest.shape[1:], lambda i: (i % 2 * 2 + i // 2, 0, 0)),
        pl.BlockSpec((shard, HALF), lambda i: (0, i)),
        "adam_expand",
    )
    all_rest = pl.BlockSpec(rest.shape, lambda i: (0, 0, 0))
    new_down, down_mean, down_square = adam(
        lambda one, two: jnp.concatenate(
            [tall_part(part, q)[:quarter] for part in (one, two) for q in range(4)], axis=0
        ),
        2.0 * FF ** (-0.5),
        core,
        rest,
        rest_other,
        (w_down, down_first, down_second),
        (1,),
        all_rest,
        pl.BlockSpec((2 * hidden_shard, width), lambda i: (0, 0)),
        "adam_down",
    )
    new_proj, proj_mean, proj_square = adam(
        lambda one, two: jnp.concatenate(
            [tall_part(one, q)[quarter:] for q in range(4)]
            + [tall_part(two, 0)[quarter + 8 :]]
            + [tall_part(two, q)[quarter:] for q in range(1, 4)],
            axis=0,
        ),
        2.0 * (D // 8) ** (-0.5),
        core,
        rest,
        rest_other,
        (w_proj, proj_first, proj_second),
        (1,),
        all_rest,
        pl.BlockSpec((shard, width), lambda i: (0, 0)),
        "adam_proj",
    )
    wide_one, _ = ordered(core, wide, wide_other)
    whole_gains = wide_one[shard : shard + 2, 512 : 512 + shard].astype(jnp.float32)
    new_qkv, qkv_mean, qkv_square = adam(
        lambda one, two: jnp.concatenate(
            [one[:shard, : D // 2], two[:shard, : D // 2]]
            + [part[:shard, 512 : 512 + KV_HEADS * HEAD_DIM] for part in (one, two)],
            axis=1,
        ),
        2.0 * D ** (-0.5),
        core,
        wide,
        wide_other,
        (w_qkv, qkv_first, qkv_second),
        (1,),
        pl.BlockSpec(wide.shape, lambda i: (0, 0)),
        pl.BlockSpec((shard, QKVW), lambda i: (0, 0)),
        "adam_qkv",
    )
    new_gains, gains_mean, gains_square = adam_step(
        gains, gains_first, gains_second, whole_gains, 1.0, 0.0
    )
    return (
        output.T.reshape(batch, local, width),
        input_grad.T.reshape(batch, local, width),
        new_qkv,
        qkv_mean,
        qkv_square,
        new_proj,
        proj_mean,
        proj_square,
        new_expand,
        expand_mean,
        expand_square,
        new_down,
        down_mean,
        down_square,
        new_gains,
        gains_mean,
        gains_square,
    )


def solution(mesh):
    parts = jax.sharding.Mesh(mesh.devices.reshape(2, 4, 2, 2, 4), AXES)
    dp, ctx = ("zh", "y", "core"), CTX
    rows = P(dp, ctx, None)
    owned = P(ctx, None)
    split = P(None, ctx)
    return jax.shard_map(
        on_device,
        mesh=parts,
        in_specs=(rows, rows, P()) + (owned,) * 12 + (split,) * 3,
        out_specs=(rows, rows) + (owned,) * 12 + (split,) * 3,
        check_vma=False,
    )
```

```python
import functools
import math

import jax
import jax.numpy as jnp
from jax import lax
from jax.experimental import pallas as pl
from jax.experimental.pallas import tpu as pltpu
from jax.sharding import PartitionSpec as P

D = 960
HEADS = 15
KV_HEADS = 5
GROUP = HEADS // KV_HEADS
HEAD_DIM = 64
FF = 2560
STEP = 10
HALF = FF // 2
QKVW = D + 2 * KV_HEADS * HEAD_DIM


eps = 1e-05
rope_base = 100000.0
beta_first = 0.9
beta_second = 0.95
adam_eps = 1e-08
masked_score = -1e30
SPLIT = 3
LOG2E = math.log2(math.e)
TALL = 56
PADDED = 896
PROJ = 120
NEAR = 896
BESIDE = 768
ATTEND_FLOPS = 20 * 10**9
BACK_FLOPS = 25 * 10**9
FEED_FLOPS = 20 * 10**9
low = jnp.bfloat16


AXES = ("zh", "y", "core", "zl", "x")
CHIPS = ("zh", "y")
CTX = ("zl", "x")
CHIP_CTX = ("zh", "zl", "x")


def swap_cores(value):
    return lax.ppermute(value, "core", [(0, 1), (1, 0)])


def to_peer(value, axis, k):
    count = lax.axis_size(axis)
    return lax.ppermute(value, axis, [(i, i ^ k) for i in range(count)])


def double(piece, axis, k, side):
    bit = lax.axis_index(axis) // k % 2 == 0
    came = to_peer(piece, axis, k)
    return jnp.concatenate(
        [jnp.where(bit, piece, came), jnp.where(bit, came, piece)], axis=side
    )


def add_peer(piece, axis, k):
    return (piece.astype(jnp.float32) + to_peer(piece, axis, k).astype(jnp.float32)).astype(low)


def exchange(stack, axes):
    return lax.all_to_all(stack, axes, 0, 0, tiled=True)


def spread(piece, axes, count):
    return exchange(jnp.broadcast_to(piece[None], (count,) + piece.shape), axes)


def total(stack):
    return jnp.sum(stack.astype(jnp.float32), axis=0).astype(low)


def ordered(core, mine, theirs):
    first = core == 0
    return jnp.where(first, mine, theirs), jnp.where(first, theirs, mine)


def rope_tables(positions):
    halfway = HEAD_DIM // 2
    freqs = rope_base ** (-(jnp.arange(halfway, dtype=jnp.float32) * 2.0) / HEAD_DIM)
    angles = freqs[:, None] * positions.astype(jnp.float32)[None, :]
    return (jnp.cos(angles), jnp.sin(angles))


def rms_scale(rows):
    return lax.rsqrt(jnp.mean(rows * rows, axis=-1, keepdims=True) + eps)


def contract(left, right, left_axis, right_axis):
    return lax.dot_general(
        left,
        right,
        (((left_axis,), (right_axis,)), ((), ())),
        preferred_element_type=jnp.float32,
    )


def in_three(row):
    rows = []
    for _ in range(3):
        part = row.astype(low).astype(jnp.float32)
        rows.append(part)
        row = row - part
    return jnp.concatenate(rows + [jnp.zeros((13, row.shape[1]), jnp.float32)], axis=0).astype(low)


def prepare(order_ref, own_ref, rank_ref, corner_ref, hide_ref):
    slots = order_ref.shape[0]
    span = corner_ref.shape[0] // 2
    ahead = lax.broadcasted_iota(jnp.int32, (span, span), 0) - lax.broadcasted_iota(
        jnp.int32, (span, span), 1
    )
    for s in range(2):
        for t in range(2):
            gap = (own_ref[s] - own_ref[t]) * span
            corner_ref[s * span : (s + 1) * span, t * span : (t + 1) * span] = jnp.where(
                ahead + gap <= 0, 0.0, masked_score
            )
    left = lax.broadcasted_iota(jnp.int32, (1, 2 * span), 1) < span
    rows = [jnp.zeros((2, 2 * span), jnp.float32)]
    for s in range(2, slots):
        at = order_ref[lax.rem(2 * rank_ref[0] + s, slots)]
        one = jnp.where(at > own_ref[0], masked_score, 0.0)
        two = jnp.where(at > own_ref[1], masked_score, 0.0)
        rows.append(jnp.where(left, one, two))
    hide_ref[...] = jnp.concatenate(rows, axis=0).astype(low)


def load_keys(rank_ref, kv_ref, per):
    chunks, _, wide, local = kv_ref.shape
    columns, keys, values = [], [], []
    for c in range(0, chunks, per):
        block = jnp.concatenate(
            [kv_ref[lax.rem(rank_ref[0] + i, chunks), 0] for i in range(c, c + per)], axis=1
        )
        rows = block.T
        lane = lax.broadcasted_iota(jnp.int32, (per * local, wide), 1)
        span = lax.broadcasted_iota(jnp.int32, (per * local, wide), 0) // (local // 2) + 2 * c
        ones = ((lane >= HEAD_DIM) & (lane < HEAD_DIM + 3)) | (lane == HEAD_DIM + 16 + span)
        keys.append(jnp.where(lane < HEAD_DIM, rows, jnp.where(ones, 1.0, 0.0).astype(low)))
        ones = jnp.where(lane < 3, 1.0, 0.0).astype(low)
        values.append(jnp.where(lane >= HEAD_DIM, rows, ones))
        columns.append(block)
    return columns, keys, values


def score(c, keys, query, corner):
    scores = contract(keys[c], query, 1, 0)
    if c == 0:
        local = corner.shape[0]
        scores = jnp.concatenate([scores[:local] + corner, scores[local:]], axis=0)
    return scores


def attend_kernel(
    order_ref, own_ref, rank_ref, q_ref, kv_ref, o_ref, lse_ref, corner_ref, hide_ref
):
    @pl.when(pl.program_id(0) == 0)
    def _():
        prepare(order_ref, own_ref, rank_ref, corner_ref, hide_ref)

    local = q_ref.shape[1]
    columns, keys, _ = load_keys(rank_ref, kv_ref, 2)
    corner = corner_ref[...]
    hide = hide_ref[...]
    blank = jnp.zeros((16, local), low)
    ones = jnp.ones((16, columns[0].shape[1]), low)
    sides = [jnp.concatenate([block[HEAD_DIM:], ones], axis=0) for block in columns]
    for h in range(GROUP):
        part = slice(h * HEAD_DIM, (h + 1) * HEAD_DIM)
        query = jnp.concatenate([q_ref[part, :], blank, hide, blank, blank], axis=0)
        scores = [score(c, keys, query, corner) for c in range(len(keys))]
        top = None
        for block in scores:
            block = jnp.max(block.reshape(-1, 8, local), axis=0)
            top = block if top is None else jnp.maximum(top, block)
        top = jnp.max(top, axis=0, keepdims=True)
        mixed = None
        for c, block in enumerate(scores):
            block = contract(sides[c], jnp.exp2(block - top).astype(low), 1, 0)
            mixed = block if mixed is None else mixed + block
        sums = mixed[HEAD_DIM : HEAD_DIM + 1]
        o_ref[part, :] = (mixed[:HEAD_DIM] / sums).astype(low)
        lse_ref[h] = top + jnp.log2(sums)


def attend_back_kernel(
    order_ref,
    own_ref,
    rank_ref,
    q_ref,
    kv_ref,
    do_ref,
    o_ref,
    lse_ref,
    dq_ref,
    dkv_ref,
    corner_ref,
    hide_ref,
):
    @pl.when(pl.program_id(0) == 0)
    def _():
        prepare(order_ref, own_ref, rank_ref, corner_ref, hide_ref)

    per = 4
    local = q_ref.shape[1]
    chunks = kv_ref.shape[0]
    columns, keys, values = load_keys(rank_ref, kv_ref, per)
    corner = corner_ref[...]
    hide = hide_ref[...]
    blank = jnp.zeros((16, local), low)
    wide_blank = jnp.zeros((HEAD_DIM, local), low)
    terms = [None] * len(keys)
    for h in range(GROUP):
        part = slice(h * HEAD_DIM, (h + 1) * HEAD_DIM)
        query = q_ref[part, :]
        back = do_ref[part, :]
        delta = jnp.sum(
            back.astype(jnp.float32) * o_ref[part, :].astype(jnp.float32), axis=0, keepdims=True
        )
        query_side = jnp.concatenate([query, in_three(-lse_ref[h]), hide, blank, blank], axis=0)
        back_side = jnp.concatenate([in_three(-delta), blank, blank, blank, back], axis=0)
        pair = jnp.concatenate(
            [
                jnp.concatenate([query, wide_blank], axis=0).T,
                jnp.concatenate([wide_blank, back], axis=0).T,
            ],
            axis=0,
        )
        grad_query = None
        for c in range(len(keys)):
            weights = jnp.exp2(score(c, keys, query_side, corner))
            grad = (weights * contract(values[c], back_side, 1, 0)).astype(low)
            term = contract(jnp.concatenate([grad, weights.astype(low)], axis=1), pair, 1, 0)
            terms[c] = term if terms[c] is None else terms[c] + term
            term = contract(columns[c][:HEAD_DIM], grad, 1, 0)
            grad_query = term if grad_query is None else grad_query + term
        dq_ref[part, :] = grad_query * HEAD_DIM ** (-0.5)
    lane = lax.broadcasted_iota(jnp.int32, (1, 2 * HEAD_DIM), 1)
    scale = jnp.where(lane < HEAD_DIM, 1.0 / LOG2E, 1.0)
    for i in range(chunks):
        term = terms[i // per][i % per * local : (i % per + 1) * local]
        dkv_ref[lax.rem(rank_ref[0] + i, chunks), 0] = (term * scale).astype(low)


def attention_specs(chunks, local, start=0):
    wide = GROUP * HEAD_DIM
    heads = pl.BlockSpec((wide, local), lambda g: (g + start, 0))
    keys = pl.BlockSpec((chunks, 1, 2 * HEAD_DIM, local), lambda g: (0, g + start, 0, 0))
    sums = pl.BlockSpec((GROUP, 1, local), lambda g: (g + start, 0, 0))
    return heads, keys, sums


def scalars():
    return pl.BlockSpec(memory_space=pltpu.SMEM)


def attention_scratch(local, slots):
    return [pltpu.VMEM((local, local), jnp.float32), pltpu.VMEM((slots, local), low)]


def attend(order, own, rank, query, keys):
    chunks, _, _, local = keys.shape
    heads, kv, sums = attention_specs(chunks, local)
    return pl.pallas_call(
        attend_kernel,
        grid=(KV_HEADS,),
        out_shape=(
            jax.ShapeDtypeStruct((D, local), low),
            jax.ShapeDtypeStruct((HEADS, 1, local), jnp.float32),
        ),
        in_specs=[scalars(), scalars(), scalars(), heads, kv],
        out_specs=(heads, sums),
        scratch_shapes=attention_scratch(local, order.shape[0]),
        compiler_params=pltpu.CompilerParams(vmem_limit_bytes=60 * 1024 * 1024),
        cost_estimate=pl.CostEstimate(
            flops=ATTEND_FLOPS, bytes_accessed=1000, transcendentals=0
        ),
        name="attend",
    )(order, own, rank, query, keys)


def attend_back(start, count, order, own, rank, query, keys, back, out, lse):
    chunks, _, _, local = keys.shape
    heads, kv, sums = attention_specs(chunks, local, start)
    part, _, _ = attention_specs(chunks, local)
    grads = pl.BlockSpec((chunks, 1, local, 2 * HEAD_DIM), lambda g: (0, g, 0, 0))
    return pl.pallas_call(
        attend_back_kernel,
        grid=(count,),
        out_shape=(
            jax.ShapeDtypeStruct((count * GROUP * HEAD_DIM, local), jnp.float32),
            jax.ShapeDtypeStruct((chunks, count, local, 2 * HEAD_DIM), low),
        ),
        in_specs=[scalars(), scalars(), scalars(), heads, kv, heads, heads, sums],
        out_specs=(part, grads),
        scratch_shapes=attention_scratch(local, order.shape[0]),
        compiler_params=pltpu.CompilerParams(vmem_limit_bytes=60 * 1024 * 1024),
        cost_estimate=pl.CostEstimate(
            flops=BACK_FLOPS * count // KV_HEADS, bytes_accessed=1000, transcendentals=0
        ),
        name=f"attend_back_{start}",
    )(order, own, rank, query, keys, back, out, lse)


def whole_call(kernel, name, flops, out_shape, *operands, near=False):
    single = not isinstance(out_shape, tuple)
    shapes = (out_shape,) if single else out_shape
    far = [] if near else [i for i, value in enumerate(operands) if value.ndim > 1]
    away = [] if near else list(range(len(shapes)))
    space = pl.BlockSpec(memory_space=pltpu.VMEM if near else pltpu.HBM)

    def staged(*refs):
        ins = list(refs[: len(operands)])
        outs = list(refs[len(operands) : len(operands) + len(shapes)])
        scratch = refs[len(operands) + len(shapes) :]
        copies = []
        for k, i in enumerate(far):
            copies.append(pltpu.make_async_copy(ins[i], scratch[k], scratch[-2].at[k]))
            ins[i] = scratch[k]
        for copy in copies:
            copy.start()
        for copy in copies:
            copy.wait()
        held = outs if near else list(scratch[len(far) : len(far) + len(away)])
        kernel(*ins, *held)
        copies = [
            pltpu.make_async_copy(held[k], outs[k], scratch[-1].at[k]) for k in away
        ]
        for copy in copies:
            copy.start()
        for copy in copies:
            copy.wait()

    scratch = [pltpu.VMEM(operands[i].shape, operands[i].dtype) for i in far]
    scratch += [pltpu.VMEM(shapes[k].shape, shapes[k].dtype) for k in away]
    if not near:
        scratch += [pltpu.SemaphoreType.DMA((len(far),)), pltpu.SemaphoreType.DMA((len(away),))]
    outs = pl.pallas_call(
        staged,
        out_shape=shapes,
        in_specs=[scalars() if value.ndim == 1 else space for value in operands],
        out_specs=(space,) * len(shapes),
        scratch_shapes=scratch,
        compiler_params=pltpu.CompilerParams(vmem_limit_bytes=(24 if near else 60) * 1024 * 1024),
        cost_estimate=pl.CostEstimate(flops=flops, bytes_accessed=1000, transcendentals=0),
        name=name,
    )(*operands)
    return outs[0] if single else outs


def stage_kernel(core_ref, qkv_ref, gains_ref, near_ref):
    first = core_ref[0] == 0
    shard = qkv_ref.shape[0]
    gains = jnp.concatenate(
        [gains_ref[...], jnp.zeros((6, gains_ref.shape[1]), jnp.float32)], axis=0
    )
    gains = jnp.concatenate([gains, jnp.zeros((8, 128 - shard), jnp.float32)], axis=1).T
    near = jnp.concatenate(
        [
            jnp.where(first, qkv_ref[:, : QKVW // 2], qkv_ref[:, QKVW // 2 :]),
            gains[:shard, :2],
            jnp.zeros((shard, PADDED - QKVW // 2 - 2), jnp.float32),
        ],
        axis=1,
    ).astype(low)
    for j in range(near_ref.shape[0]):
        near_ref[j] = near


def stage_feed_kernel(place_ref, expand_ref, down_ref, proj_ref, wide_ref, tall_ref):
    first = place_ref[0] == 0
    step = FF // 16
    parts = []
    for k in range(4):
        left = expand_ref[:, 2 * k * step : (2 * k + 1) * step]
        right = expand_ref[:, (2 * k + 1) * step : (2 * k + 2) * step]
        parts.append(jnp.where(first, left, right))
    proj = jnp.where(first, proj_ref[:, : D // 2], proj_ref[:, D // 2 :])
    quarter = proj[:, :PROJ]
    for k in range(1, 4):
        quarter = jnp.where(place_ref[2] == k, proj[:, k * PROJ : (k + 1) * PROJ], quarter)
    blank = jnp.zeros((proj.shape[0], BESIDE - FF // 4 - PROJ), jnp.float32)
    wide = jnp.concatenate(parts + [quarter, blank], axis=1).astype(low)
    tall = down_ref[...].astype(low)
    for j in range(wide_ref.shape[0]):
        wide_ref[j] = wide
        tall_ref[j] = tall


def stage_feed(place, expand, down, proj, groups):
    shard = expand.shape[0]
    half = down.shape[0] // 2
    outs = [(groups, shard, BESIDE), (groups, half, D)]
    return pl.pallas_call(
        stage_feed_kernel,
        grid_spec=pltpu.PrefetchScalarGridSpec(
            num_scalar_prefetch=1,
            grid=(1,),
            in_specs=[
                pl.BlockSpec((shard, HALF), lambda i, place: (0, place[1])),
                pl.BlockSpec((half, D), lambda i, place: (place[0], 0)),
                pl.BlockSpec(proj.shape, lambda i, place: (0, 0)),
            ],
            out_specs=[pl.BlockSpec(out, lambda i, place: (0, 0, 0)) for out in outs],
        ),
        out_shape=[jax.ShapeDtypeStruct(out, low) for out in outs],
        compiler_params=pltpu.CompilerParams(vmem_limit_bytes=60 * 1024 * 1024),
        cost_estimate=pl.CostEstimate(flops=1000, bytes_accessed=8 * 10**6, transcendentals=0),
        name="stage_feed",
    )(place, expand, down, proj)


def rotated(block, cosine, sine):
    first = block[: HEAD_DIM // 2]
    second = block[HEAD_DIM // 2 :]
    return [first * cosine - second * sine, second * cosine + first * sine]


def project_kernel(
    core_ref,
    rows_ref,
    mine_ref,
    theirs_ref,
    cosine_ref,
    sine_ref,
    normed_ref,
    query_ref,
    keys_ref,
    gains_ref,
):
    first_core = core_ref[0] == 0
    cosine = cosine_ref[...]
    sine = sine_ref[...]
    rows = rows_ref[...].astype(jnp.float32).T
    gains = mine_ref[:, PADDED - 128 : PADDED].astype(jnp.float32).T
    at = QKVW // 2 - (PADDED - 128)
    gains_ref[...] = gains[at : at + 2]
    normed = (rows * rms_scale(rows) * gains[at : at + 1]).astype(low)
    normed_ref[...] = normed
    near = contract(normed, mine_ref[...], 1, 0).T
    away = contract(normed, theirs_ref[...], 1, 0).T
    half = QKVW // 2
    one = jnp.where(first_core, near, away)[:half]
    two = jnp.where(first_core, away, near)[:half]
    mixed = jnp.concatenate([one, two], axis=0)
    scale = HEAD_DIM ** (-0.5) * LOG2E
    for h in range(HEADS):
        span = slice(h * HEAD_DIM, (h + 1) * HEAD_DIM)
        turned = jnp.concatenate(rotated(mixed[span], cosine, sine), axis=0)
        query_ref[span] = (turned * scale).astype(low)
    for g in range(KV_HEADS):
        at = D + g * HEAD_DIM
        to = at + KV_HEADS * HEAD_DIM
        pair = rotated(mixed[at : at + HEAD_DIM], cosine, sine) + [mixed[to : to + HEAD_DIM]]
        pair = jnp.concatenate(pair, axis=0).astype(low)
        for j in range(keys_ref.shape[0]):
            keys_ref[j, g] = pair


def join_proj(ref):
    return jnp.concatenate([ref[q, :, :PROJ] for q in range(4)], axis=1)


def middle_kernel(core_ref, out_ref, mine_ref, theirs_ref, rows_ref, gains_ref, mid_ref, normed_ref):
    first_core = core_ref[0] == 0
    mixed = out_ref[...].T
    near = contract(mixed, join_proj(mine_ref), 1, 0)
    away = contract(mixed, join_proj(theirs_ref), 1, 0)
    near, away = jnp.where(first_core, near, away), jnp.where(first_core, away, near)
    middle = rows_ref[...].astype(jnp.float32).T + jnp.concatenate([near, away], axis=1)
    mid_ref[...] = middle
    normed_ref[...] = (middle * rms_scale(middle) * gains_ref[1:2]).astype(low)


def turn_kernel(
    core_ref,
    own_ref,
    came_ref,
    mid_ref,
    back_ref,
    gains_ref,
    mine_ref,
    theirs_ref,
    out_ref,
    grad_ref,
    grad_out_ref,
    kept_ref,
    sent_ref,
    gain_grad_ref,
):
    first_core = core_ref[0] == 0
    normed = own_ref[...] + came_ref[...].astype(jnp.float32)
    middle = mid_ref[...]
    inverse = rms_scale(middle)
    scaled = normed * gains_ref[1:2]
    inner = jnp.mean(scaled * middle, axis=-1, keepdims=True)
    grad = back_ref[...].astype(jnp.float32) + inverse * (
        scaled - middle * inverse * inverse * inner
    )
    grad_ref[...] = grad
    gain_grad_ref[...] = jnp.sum(normed * middle * inverse, axis=0, keepdims=True)
    one = grad[:, : D // 2]
    two = grad[:, D // 2 :]
    near = jnp.where(first_core, one, two).astype(low)
    away = jnp.where(first_core, two, one).astype(low)
    grad_out = contract(near, join_proj(mine_ref), 1, 1) + contract(
        away, join_proj(theirs_ref), 1, 1
    )
    grad_out_ref[...] = grad_out.T.astype(low)
    product = contract(out_ref[...], grad.astype(low), 1, 0)
    groups, window, _ = kept_ref.shape
    shard = product.shape[0] // groups
    for j in range(groups):
        top = product[j * shard : j * shard + window]
        bottom = product[(j + 1) * shard - window : (j + 1) * shard]
        kept_ref[j] = jnp.where(first_core, top, bottom).astype(low)
        sent_ref[j] = jnp.where(first_core, bottom, top).astype(low)


def emit_kernel(mid_ref, own_ref, came_ref, out_ref):
    value = mid_ref[...] + own_ref[...] + came_ref[...].astype(jnp.float32)
    out_ref[...] = value.T.astype(low)


def feed_kernel(
    rows_one,
    rows_two,
    back_one,
    back_two,
    expand_ref,
    down_ref,
    fed_ref,
    fed_other_ref,
    normed_ref,
    normed_other_ref,
    down_grad_ref,
    expand_grad_ref,
    rows_ref,
    back_ref,
    columns_ref,
    fed_sum,
    normed_sum,
):
    local = rows_one.shape[0]
    h = pl.program_id(0)

    @pl.when(h == 0)
    def _():
        rows_ref[:local] = rows_one[...]
        rows_ref[local:] = rows_two[...]
        back_ref[:local] = back_one[...]
        back_ref[local:] = back_two[...]
        columns_ref[...] = rows_ref[...].T

    rows = rows_ref[...]
    back = back_ref[...]
    columns = columns_ref[...]
    wide_gate = expand_ref[0]
    wide_up = expand_ref[1]
    down = down_ref[...]
    gate = contract(rows, wide_gate, 1, 0)
    upward = contract(rows, wide_up, 1, 0)
    sigmoid = jax.nn.sigmoid(gate)
    active = gate * sigmoid
    hidden = (active * upward).astype(low)
    grad_hidden = contract(back, down, 1, 1)
    grad_up = (grad_hidden * active).astype(low)
    grad_gate = (grad_hidden * upward * sigmoid * (1.0 + gate * (1.0 - sigmoid))).astype(low)
    fed = contract(hidden, down, 1, 0)
    normed = contract(grad_gate, wide_gate, 1, 1) + contract(grad_up, wide_up, 1, 1)
    down_grad_ref[...] = contract(hidden.T, back, 1, 0).astype(low)
    expand_grad_ref[0] = contract(columns, grad_gate, 1, 0).astype(low)
    expand_grad_ref[1] = contract(columns, grad_up, 1, 0).astype(low)

    @pl.when(h == 0)
    def _():
        fed_sum[...] = fed
        normed_sum[...] = normed

    @pl.when(h == 1)
    def _():
        fed_all = fed_sum[...] + fed
        normed_all = normed_sum[...] + normed
        fed_ref[...] = fed_all[:local]
        fed_other_ref[...] = fed_all[local:].astype(low)
        normed_ref[...] = normed_all[:local]
        normed_other_ref[...] = normed_all[local:].astype(low)


def feed(rows, back, expand, down):
    local, width = rows[0].shape
    step = FF // 4
    held = pl.BlockSpec((local, width), lambda h: (0, 0))
    pair = pl.BlockSpec((2, width, step), lambda h: (h, 0, 0))
    tall = pl.BlockSpec((step, width), lambda h: (h, 0))
    own = jax.ShapeDtypeStruct((local, width), jnp.float32)
    other = jax.ShapeDtypeStruct((local, width), low)
    return pl.pallas_call(
        feed_kernel,
        grid=(2,),
        out_shape=(
            own,
            other,
            own,
            other,
            jax.ShapeDtypeStruct(down.shape, low),
            jax.ShapeDtypeStruct((4, width, step), low),
        ),
        in_specs=[held] * 4 + [pair, tall],
        out_specs=(held,) * 4 + (tall, pair),
        scratch_shapes=[
            pltpu.VMEM((2 * local, width), low),
            pltpu.VMEM((2 * local, width), low),
            pltpu.VMEM((width, 2 * local), low),
            pltpu.VMEM((2 * local, width), jnp.float32),
            pltpu.VMEM((2 * local, width), jnp.float32),
        ],
        compiler_params=pltpu.CompilerParams(vmem_limit_bytes=60 * 1024 * 1024),
        cost_estimate=pl.CostEstimate(flops=FEED_FLOPS, bytes_accessed=1000, transcendentals=0),
        name="feed",
    )(*rows, *back, expand, down)


def stack_kernel(down_ref, kept_ref, came_ref, out_ref):
    groups, window, _ = kept_ref.shape
    quarter = down_ref.shape[0] // (4 * groups)
    down = down_ref[...].astype(jnp.float32)
    proj = kept_ref[...].astype(jnp.float32) + came_ref[...].astype(jnp.float32)
    for y in range(4):
        parts = []
        for j in range(groups):
            at = (4 * j + y) * quarter
            parts.append(down[at : at + quarter])
            parts.append(proj[j, y * window // 4 : (y + 1) * window // 4])
        out_ref[y] = jnp.concatenate(parts, axis=0).astype(low)


def adam_step(master, first, second, grad, rate, decay):
    new_first = beta_first * first + (1.0 - beta_first) * grad
    new_second = beta_second * second + (1.0 - beta_second) * grad * grad
    fix_one = 1.0 - beta_first**STEP
    fix_two = 1.0 - beta_second**STEP
    update = new_first / fix_one / (jnp.sqrt(new_second / fix_two) + adam_eps) + decay * master
    return (master - rate * update, new_first, new_second)


def update_kernel(
    core_ref,
    wide_ref,
    wide_other,
    rest_ref,
    rest_other,
    gains_ref,
    gains_first,
    gains_second,
    *refs,
):
    states, outs, gain_outs = refs[:12], refs[12:24], refs[24:27]
    held = refs[27:31]
    near = refs[31:35]
    load_sem, store_sem, near_sem = refs[35:]
    grads = (wide_ref, wide_other, rest_ref, rest_other)
    fetches = [pltpu.make_async_copy(grads[k], near[k], near_sem.at[k]) for k in range(4)]
    wide_ref, wide_other, rest_ref, rest_other = near
    first_core = core_ref[0] == 0
    shard = gains_ref.shape[1]
    quarter = held[3].shape[1] // 8

    def both(mine, theirs):
        return (
            jnp.where(first_core, mine, theirs).astype(jnp.float32),
            jnp.where(first_core, theirs, mine).astype(jnp.float32),
        )

    def expand_grad(q):
        step = FF // 16
        one, two = both(rest_ref[q, :shard, : FF // 4], rest_other[q, :shard, : FF // 4])
        parts = []
        for k in range(4):
            span = slice(k * step, (k + 1) * step)
            parts += [one[:, span], two[:, span]]
        return jnp.concatenate(parts, axis=1)

    def tall_grads():
        parts = [both(tall_part(rest_ref, q), tall_part(rest_other, q)) for q in range(4)]
        one = [part[0] for part in parts]
        two = [part[1] for part in parts]
        down = jnp.concatenate([part[:quarter] for part in one + two], axis=0)
        proj = jnp.concatenate(
            [part[quarter:] for part in one]
            + [two[0][quarter + 8 :]]
            + [part[quarter:] for part in two[1:]],
            axis=0,
        )
        return down, proj

    def wide_grad():
        one, two = both(wide_ref[:shard], wide_other[:shard])
        return jnp.concatenate([one[:, : QKVW // 2], two[:, : QKVW // 2]], axis=1)

    full = slice(None)
    pieces = [(2, pl.ds(i * HALF, HALF), 2.0 * D ** (-0.5)) for i in range(4)]
    pieces += [
        (3, full, 2.0 * FF ** (-0.5)),
        (1, full, 2.0 * (D // 8) ** (-0.5)),
        (0, full, 2.0 * D ** (-0.5)),
    ]

    def copies(p, out):
        weight, columns, _ = pieces[p]
        for k in range(3):
            near = held[weight].at[k, :, columns]
            if out:
                yield pltpu.make_async_copy(
                    near, outs[3 * weight + k].at[:, columns], store_sem.at[p, k]
                )
            else:
                yield pltpu.make_async_copy(
                    states[3 * weight + k].at[:, columns], near, load_sem.at[p, k]
                )

    for copy in fetches:
        copy.start()
    for p in range(len(pieces)):
        for copy in copies(p, False):
            copy.start()
    for copy in fetches:
        copy.wait()
    down, proj = tall_grads()
    for p, (weight, columns, rate) in enumerate(pieces):
        for copy in copies(p, False):
            copy.wait()
        if p < 4:
            grad = expand_grad(p % 2 * 2 + p // 2)
        else:
            grad = (down, proj)[p - 4] if p < 6 else wide_grad()
        new = adam_step(*[held[weight][k, :, columns] for k in range(3)], grad, rate, 0.1)
        for k in range(3):
            held[weight][k, :, columns] = new[k]
        for copy in copies(p, True):
            copy.start()
    mine, theirs = both(wide_ref[...], wide_other[...])
    grad = mine[shard : shard + 2, :shard]
    new = adam_step(gains_ref[...], gains_first[...], gains_second[...], grad, 1.0, 0.0)
    for out, value in zip(gain_outs, new):
        out[...] = value
    for p in range(len(pieces)):
        for copy in copies(p, True):
            copy.wait()


def update(core, wide, wide_other, rest, rest_other, gains, states):
    whole = pl.BlockSpec(memory_space=pltpu.VMEM)
    away = pl.BlockSpec(memory_space=pltpu.HBM)
    shapes = [jax.ShapeDtypeStruct(value.shape, jnp.float32) for value in states + gains]
    return pl.pallas_call(
        update_kernel,
        out_shape=shapes,
        in_specs=[scalars()] + [away] * 4 + [whole] * 3 + [away] * 12,
        out_specs=[away] * 12 + [whole] * 3,
        scratch_shapes=[
            pltpu.VMEM((3,) + states[3 * weight].shape, jnp.float32) for weight in range(4)
        ]
        + [pltpu.VMEM(value.shape, low) for value in (wide, wide, rest, rest)]
        + [pltpu.SemaphoreType.DMA(shape) for shape in ((7, 3), (7, 3), (4,))],
        compiler_params=pltpu.CompilerParams(vmem_limit_bytes=32 * 1024 * 1024),
        cost_estimate=pl.CostEstimate(
            flops=1000, bytes_accessed=30 * 10**6, transcendentals=0
        ),
        name="update",
    )(core, wide, wide_other, rest, rest_other, *gains, *states)


def back_rotated(block, cosine, sine):
    first = block[: HEAD_DIM // 2]
    second = block[HEAD_DIM // 2 :]
    return [first * cosine + second * sine, second * cosine - first * sine]


def late_kernel(
    core_ref,
    first_terms,
    second_terms,
    first_dq,
    second_dq,
    cosine_ref,
    sine_ref,
    normed_ref,
    mine_ref,
    theirs_ref,
    rows_ref,
    grad_ref,
    gain_ref,
    gain_grad_ref,
    out_ref,
    kept_ref,
    sent_ref,
):
    cosine = cosine_ref[...]
    sine = sine_ref[...]
    first_core = core_ref[0] == 0
    parts = []
    for ref in (first_dq, second_dq):
        for h in range(ref.shape[0] // HEAD_DIM):
            parts += back_rotated(ref[h * HEAD_DIM : (h + 1) * HEAD_DIM], cosine, sine)
    values = []
    for ref in (first_terms, second_terms):
        for g in range(ref.shape[1]):
            block = ref[0, g].astype(jnp.float32)
            for j in range(1, ref.shape[0]):
                block = block + ref[j, g].astype(jnp.float32)
            block = block.T
            parts += back_rotated(block[:HEAD_DIM], cosine, sine)
            values.append(block[HEAD_DIM:])
    mixed = jnp.concatenate(parts + values, axis=0)
    half = QKVW // 2
    blank = jnp.zeros((PADDED - half, mixed.shape[1]), jnp.float32)
    one = mixed[:half]
    two = mixed[half:]
    near = jnp.concatenate([jnp.where(first_core, one, two), blank], axis=0).T.astype(low)
    away = jnp.concatenate([jnp.where(first_core, two, one), blank], axis=0).T.astype(low)
    grad_normed = contract(near, mine_ref[...], 1, 1) + contract(away, theirs_ref[...], 1, 1)
    rows = rows_ref[...].astype(jnp.float32).T
    inverse = rms_scale(rows)
    scaled = grad_normed * gain_ref[0:1]
    inner = jnp.mean(scaled * rows, axis=-1, keepdims=True)
    back = inverse * (scaled - rows * inverse * inverse * inner)
    out_ref[...] = (grad_ref[...] + back).T.astype(low)
    gain_one = jnp.sum(grad_normed * rows * inverse, axis=0, keepdims=True)
    gains = (gain_one, gain_grad_ref[...])
    columns = normed_ref[...].T
    groups, count, lanes = kept_ref.shape
    shard = columns.shape[0] // groups
    for ref, side in ((kept_ref, near), (sent_ref, away)):
        product = contract(columns, side, 1, 0)
        for j in range(groups):
            span = slice(j * shard, (j + 1) * shard)
            tail = padded_rows(
                jnp.concatenate([gain[:, span] for gain in gains], axis=0), count - shard
            )
            tail = jnp.concatenate(
                [tail, jnp.zeros((count - shard, lanes - shard), jnp.float32)], axis=1
            )
            ref[j] = jnp.concatenate([product[span], tail], axis=0).astype(low)


def padded_rows(block, rows):
    return jnp.concatenate(
        [block, jnp.zeros((rows - block.shape[0], block.shape[1]), jnp.float32)], axis=0
    )


def put_halves(out_ref, j, block):
    groups = out_ref.shape[0] // 2
    rows = out_ref.shape[1]
    for half in range(2):
        out_ref[half * groups + j] = block[half * rows : (half + 1) * rows].astype(low)


def pack_early_kernel(expand_ref, out_ref):
    for j in range(expand_ref.shape[0]):
        put_halves(out_ref, j, padded_rows(expand_ref[j].astype(jnp.float32), 128))


def pack_late_kernel(kept_ref, came_ref, tall_ref, out_ref):
    for j in range(kept_ref.shape[0]):
        summed = kept_ref[j].astype(jnp.float32) + came_ref[j].astype(jnp.float32)
        tall = tall_ref[j].astype(jnp.float32)
        rows = summed.shape[0] // 2
        side = jnp.concatenate(
            [tall[:, 512:], jnp.zeros((tall.shape[0], 1024 - tall.shape[1]), jnp.float32)], axis=1
        )
        tall = jnp.concatenate([padded_rows(tall[:, :512], rows), padded_rows(side, rows)], axis=0)
        put_halves(out_ref, j, jnp.concatenate([summed, tall], axis=1))


def sum_kernel(early_ref, late_ref, out_ref):
    sums = []
    for ref in (early_ref, late_ref):
        block = ref[0].astype(jnp.float32)
        for j in range(1, ref.shape[0]):
            block = block + ref[j].astype(jnp.float32)
        sums.append(block.astype(low))
    block = jnp.concatenate(sums, axis=1)
    for j in range(out_ref.shape[0]):
        out_ref[j] = block


def finish_kernel(all_ref, wide_ref, rest_ref):
    count = all_ref.shape[0] // 2
    rows = all_ref.shape[1]
    expand = slice(0, FF // 4)
    wide = slice(FF // 4, FF // 4 + PADDED)
    tall = slice(FF // 4 + PADDED, FF // 4 + PADDED + 512)
    for half in range(2):
        span = slice(half * rows, (half + 1) * rows)
        block = all_ref[half * count, :, wide].astype(jnp.float32)
        for y in range(1, count):
            block = block + all_ref[half * count + y, :, wide].astype(jnp.float32)
        wide_ref[span] = block.astype(low)
        for y in range(count):
            rest_ref[y, span] = jnp.concatenate(
                [all_ref[half * count + y, :, lanes] for lanes in (expand, tall)], axis=1
            )


def tall_part(rest, q):
    half = rest.shape[1] // 2
    left = rest[q, :TALL, FF // 4 :]
    right = rest[q, half : half + TALL, FF // 4 : FF // 4 + D - 512]
    return jnp.concatenate([left, right], axis=1)


def on_device(
    inputs,
    cotangent,
    span_order,
    w_qkv,
    qkv_first,
    qkv_second,
    w_proj,
    proj_first,
    proj_second,
    w_expand,
    expand_first,
    expand_second,
    w_down,
    down_first,
    down_second,
    gains,
    gains_first,
    gains_second,
):
    core = lax.axis_index("core")
    rank = lax.axis_index(CTX)
    groups = 8
    batch, local, width = inputs.shape
    shard = w_qkv.shape[0]
    hidden_shard = w_down.shape[0] // 2

    y = lax.axis_index("y")
    place = jnp.stack([core, y % 2 * 2 + y // 2, y]).astype(jnp.int32)
    core_at = place[:1]
    rank_at = rank.reshape(1).astype(jnp.int32)
    near = whole_call(
        stage_kernel,
        "stage",
        1000,
        jax.ShapeDtypeStruct((groups, shard, NEAR), low),
        core_at,
        w_qkv,
        gains,
    )
    mine = exchange(near, CTX).reshape(width, NEAR)
    expand_low, down_low = stage_feed(place, w_expand, w_down, w_proj, groups)
    back_rows = cotangent.reshape(local, width)
    order_own = lax.dynamic_slice_in_dim(span_order, 2 * rank, 2)
    own_pos = (
        order_own[:, None] * (local // 2) + jnp.arange(local // 2, dtype=jnp.int32)
    ).reshape(local)
    cosine, sine = rope_tables(own_pos)
    mine, cosine, sine, expand_low, down_low, back_rows = lax.optimization_barrier(
        (mine, cosine, sine, expand_low, down_low, back_rows)
    )
    theirs = swap_cores(mine)
    expand_low = exchange(expand_low, CTX).reshape(width, BESIDE)

    tokens = inputs.reshape(local, width).T
    square = (local, width)
    normed_one, query, all_keys, full_gains = whole_call(
        project_kernel,
        "project",
        1000,
        (
            jax.ShapeDtypeStruct(square, low),
            jax.ShapeDtypeStruct((width, local), low),
            jax.ShapeDtypeStruct((groups, KV_HEADS, 2 * HEAD_DIM, local), low),
            jax.ShapeDtypeStruct((2, width), jnp.float32),
        ),
        core_at,
        tokens,
        mine,
        theirs,
        cosine,
        sine,
    )
    all_keys, expand_low = lax.optimization_barrier((all_keys, expand_low))
    expand_low = lax.all_gather(expand_low, "y", axis=0, tiled=False)
    all_keys = exchange(all_keys, CTX)
    all_keys, down_low = lax.optimization_barrier((all_keys, down_low))
    half_down = exchange(down_low, CTX).reshape(HALF, width)
    attended, lse = attend(span_order, order_own, rank_at, query, all_keys)
    attended, expand_low = lax.optimization_barrier((attended, expand_low))
    proj_mine = expand_low[:, :, FF // 4 :]
    proj_theirs = swap_cores(proj_mine)
    middle, normed_two = whole_call(
        middle_kernel,
        "middle",
        2 * 10**9,
        (jax.ShapeDtypeStruct(square, jnp.float32), jax.ShapeDtypeStruct(square, low)),
        core_at,
        attended,
        proj_mine,
        proj_theirs,
        tokens,
        full_gains,
    )
    normed_two, half_down = lax.optimization_barrier((normed_two, half_down))

    fed, fed_other, grad_normed, grad_other, grad_down, grad_expand = feed(
        (normed_two, swap_cores(normed_two)),
        (back_rows, swap_cores(back_rows)),
        expand_low,
        half_down,
    )
    grad_middle, grad_att, proj_kept, proj_sent, gain_grad_two = whole_call(
        turn_kernel,
        "turn",
        3 * 10**9,
        (
            jax.ShapeDtypeStruct(square, jnp.float32),
            jax.ShapeDtypeStruct((width, local), low),
            jax.ShapeDtypeStruct((groups, 64, width), low),
            jax.ShapeDtypeStruct((groups, 64, width), low),
            jax.ShapeDtypeStruct((1, width), jnp.float32),
        ),
        core_at,
        grad_normed,
        swap_cores(grad_other),
        middle,
        back_rows,
        full_gains,
        proj_mine,
        proj_theirs,
        attended,
    )
    output = whole_call(
        emit_kernel,
        "emit",
        1000,
        jax.ShapeDtypeStruct((width, local), low),
        middle,
        fed,
        swap_cores(fed_other),
    )

    expand_sum = lax.psum_scatter(grad_expand, "y", scatter_dimension=0, tiled=False)
    context = (span_order, order_own, rank_at, query, all_keys, grad_att, attended, lse)
    first_query, first_terms = attend_back(0, SPLIT, *context)
    first_terms = exchange(first_terms, CTX)
    grad_query, key_terms = attend_back(SPLIT, KV_HEADS - SPLIT, *context)
    key_terms, grad_down = lax.optimization_barrier((key_terms, grad_down))
    key_terms = exchange(key_terms, CTX)
    early = whole_call(
        pack_early_kernel,
        "pack_early",
        1000,
        jax.ShapeDtypeStruct((2 * groups, 64, FF // 4), low),
        expand_sum.reshape(groups, shard, FF // 4),
    )
    key_terms, first_terms, output, early = lax.optimization_barrier(
        (key_terms, first_terms, output, early)
    )
    early = exchange(early, CHIP_CTX)
    tall = lax.psum_scatter(
        whole_call(
            stack_kernel,
            "stack",
            1000,
            jax.ShapeDtypeStruct((4, groups * TALL, width), low),
            grad_down,
            proj_kept,
            swap_cores(proj_sent),
        ),
        "y",
        scatter_dimension=0,
        tiled=False,
    )
    half = jax.ShapeDtypeStruct((groups, 128, PADDED), low)
    input_grad, kept, sent = whole_call(
        late_kernel,
        "late",
        8 * 10**9,
        (jax.ShapeDtypeStruct((width, local), low), half, half),
        core_at,
        first_terms,
        key_terms,
        first_query,
        grad_query,
        cosine,
        sine,
        normed_one,
        mine,
        theirs,
        tokens,
        grad_middle,
        full_gains,
        gain_grad_two,
    )
    sent, early = lax.optimization_barrier((sent, early))
    late = whole_call(
        pack_late_kernel,
        "pack_late",
        1000,
        jax.ShapeDtypeStruct((2 * groups, 64, PADDED + 512), low),
        kept,
        swap_cores(sent),
        tall.reshape(groups, TALL, width),
        near=True,
    )
    late = exchange(late, CHIP_CTX)
    parts = whole_call(
        sum_kernel,
        "sum_parts",
        1000,
        jax.ShapeDtypeStruct((8, 64, FF // 4 + PADDED + 512), low),
        early,
        late,
        near=True,
    )
    wide, rest = whole_call(
        finish_kernel,
        "finish",
        1000,
        (
            jax.ShapeDtypeStruct((128, PADDED), low),
            jax.ShapeDtypeStruct((4, 128, FF // 4 + 512), low),
        ),
        exchange(parts, CHIPS),
        near=True,
    )
    wide_other = swap_cores(wide)
    rest_other = swap_cores(rest)
    news = update(
        core_at,
        wide,
        wide_other,
        rest,
        rest_other,
        [gains, gains_first, gains_second],
        [
            w_qkv,
            qkv_first,
            qkv_second,
            w_proj,
            proj_first,
            proj_second,
            w_expand,
            expand_first,
            expand_second,
            w_down,
            down_first,
            down_second,
        ],
    )
    return (
        output.T.reshape(batch, local, width),
        input_grad.T.reshape(batch, local, width),
        *news,
    )


def solution(mesh):
    parts = jax.sharding.Mesh(mesh.devices.reshape(2, 4, 2, 2, 4), AXES)
    dp, ctx = ("zh", "y", "core"), CTX
    rows = P(dp, ctx, None)
    owned = P(ctx, None)
    split = P(None, ctx)
    return jax.shard_map(
        on_device,
        mesh=parts,
        in_specs=(rows, rows, P()) + (owned,) * 12 + (split,) * 3,
        out_specs=(rows, rows) + (owned,) * 12 + (split,) * 3,
        check_vma=False,
    )
```

```python
import functools
import math

import jax
import jax.numpy as jnp
from jax import lax
from jax.experimental import pallas as pl
from jax.experimental.pallas import tpu as pltpu
from jax.sharding import PartitionSpec as P

D = 960
HEADS = 15
KV_HEADS = 5
GROUP = HEADS // KV_HEADS
HEAD_DIM = 64
FF = 2560
STEP = 10
HALF = FF // 2
QKVW = D + 2 * KV_HEADS * HEAD_DIM


eps = 1e-05
rope_base = 100000.0
beta_first = 0.9
beta_second = 0.95
adam_eps = 1e-08
masked_score = -1e30
TALL_WIDE = (slice(0, 384), slice(384, 768))
TALL_NARROW = (slice(768, 864), slice(864, 960))
LATE = 1280
SPLIT = 2
LOG2E = math.log2(math.e)
TALL = 56
PADDED = 896
PROJ = 120
NEAR = 896
BESIDE = 768
ATTEND_FLOPS = 20 * 10**9
BACK_FLOPS = 25 * 10**9
FEED_FLOPS = 20 * 10**9
low = jnp.bfloat16


AXES = ("zh", "y", "core", "zl", "x")
CHIPS = ("zh", "y")
CTX = ("zl", "x")
CHIP_CTX = ("zh", "zl", "x")


def swap_cores(value):
    return lax.ppermute(value, "core", [(0, 1), (1, 0)])


def to_peer(value, axis, k):
    count = lax.axis_size(axis)
    return lax.ppermute(value, axis, [(i, i ^ k) for i in range(count)])


def double(piece, axis, k, side):
    bit = lax.axis_index(axis) // k % 2 == 0
    came = to_peer(piece, axis, k)
    return jnp.concatenate(
        [jnp.where(bit, piece, came), jnp.where(bit, came, piece)], axis=side
    )


def add_peer(piece, axis, k):
    return (piece.astype(jnp.float32) + to_peer(piece, axis, k).astype(jnp.float32)).astype(low)


def exchange(stack, axes):
    return lax.all_to_all(stack, axes, 0, 0, tiled=True)


def spread(piece, axes, count):
    return exchange(jnp.broadcast_to(piece[None], (count,) + piece.shape), axes)


def total(stack):
    return jnp.sum(stack.astype(jnp.float32), axis=0).astype(low)


def ordered(core, mine, theirs):
    first = core == 0
    return jnp.where(first, mine, theirs), jnp.where(first, theirs, mine)


def rope_tables(positions):
    halfway = HEAD_DIM // 2
    freqs = rope_base ** (-(jnp.arange(halfway, dtype=jnp.float32) * 2.0) / HEAD_DIM)
    angles = freqs[:, None] * positions.astype(jnp.float32)[None, :]
    return (jnp.cos(angles), jnp.sin(angles))


def rms_scale(rows):
    return lax.rsqrt(jnp.mean(rows * rows, axis=-1, keepdims=True) + eps)


def contract(left, right, left_axis, right_axis):
    return lax.dot_general(
        left,
        right,
        (((left_axis,), (right_axis,)), ((), ())),
        preferred_element_type=jnp.float32,
    )


def in_three(row):
    rows = []
    for _ in range(3):
        part = row.astype(low).astype(jnp.float32)
        rows.append(part)
        row = row - part
    return jnp.concatenate(rows + [jnp.zeros((13, row.shape[1]), jnp.float32)], axis=0).astype(low)


def prepare(order_ref, own_ref, rank_ref, corner_ref, hide_ref):
    slots = order_ref.shape[0]
    span = corner_ref.shape[0] // 2
    ahead = lax.broadcasted_iota(jnp.int32, (span, span), 0) - lax.broadcasted_iota(
        jnp.int32, (span, span), 1
    )
    for s in range(2):
        for t in range(2):
            gap = (own_ref[s] - own_ref[t]) * span
            corner_ref[s * span : (s + 1) * span, t * span : (t + 1) * span] = jnp.where(
                ahead + gap <= 0, 0.0, masked_score
            )
    left = lax.broadcasted_iota(jnp.int32, (1, 2 * span), 1) < span
    rows = [jnp.zeros((2, 2 * span), jnp.float32)]
    for s in range(2, slots):
        at = order_ref[lax.rem(2 * rank_ref[0] + s, slots)]
        one = jnp.where(at > own_ref[0], masked_score, 0.0)
        two = jnp.where(at > own_ref[1], masked_score, 0.0)
        rows.append(jnp.where(left, one, two))
    hide_ref[...] = jnp.concatenate(rows, axis=0).astype(low)


def load_keys(rank_ref, kv_ref, per):
    chunks, _, wide, local = kv_ref.shape
    columns, keys, values = [], [], []
    for c in range(0, chunks, per):
        block = jnp.concatenate(
            [kv_ref[lax.rem(rank_ref[0] + i, chunks), 0] for i in range(c, c + per)], axis=1
        )
        rows = block.T
        lane = lax.broadcasted_iota(jnp.int32, (per * local, wide), 1)
        span = lax.broadcasted_iota(jnp.int32, (per * local, wide), 0) // (local // 2) + 2 * c
        ones = ((lane >= HEAD_DIM) & (lane < HEAD_DIM + 3)) | (lane == HEAD_DIM + 16 + span)
        keys.append(jnp.where(lane < HEAD_DIM, rows, jnp.where(ones, 1.0, 0.0).astype(low)))
        ones = jnp.where(lane < 3, 1.0, 0.0).astype(low)
        values.append(jnp.where(lane >= HEAD_DIM, rows, ones))
        columns.append(block)
    return columns, keys, values


def score(c, keys, query, corner):
    scores = contract(keys[c], query, 1, 0)
    if c == 0:
        local = corner.shape[0]
        scores = jnp.concatenate([scores[:local] + corner, scores[local:]], axis=0)
    return scores


def attend_kernel(
    order_ref, own_ref, rank_ref, q_ref, kv_ref, o_ref, lse_ref, corner_ref, hide_ref
):
    @pl.when(pl.program_id(0) == 0)
    def _():
        prepare(order_ref, own_ref, rank_ref, corner_ref, hide_ref)

    local = q_ref.shape[1]
    columns, keys, _ = load_keys(rank_ref, kv_ref, 2)
    corner = corner_ref[...]
    hide = hide_ref[...]
    blank = jnp.zeros((16, local), low)
    ones = jnp.ones((16, columns[0].shape[1]), low)
    sides = [jnp.concatenate([block[HEAD_DIM:], ones], axis=0) for block in columns]
    for h in range(GROUP):
        part = slice(h * HEAD_DIM, (h + 1) * HEAD_DIM)
        query = jnp.concatenate([q_ref[part, :], blank, hide, blank, blank], axis=0)
        scores = [score(c, keys, query, corner) for c in range(len(keys))]
        top = None
        for block in scores:
            block = jnp.max(block.reshape(-1, 8, local), axis=0)
            top = block if top is None else jnp.maximum(top, block)
        top = jnp.max(top, axis=0, keepdims=True)
        mixed = None
        for c, block in enumerate(scores):
            block = contract(sides[c], jnp.exp2(block - top).astype(low), 1, 0)
            mixed = block if mixed is None else mixed + block
        sums = mixed[HEAD_DIM : HEAD_DIM + 1]
        o_ref[part, :] = (mixed[:HEAD_DIM] / sums).astype(low)
        lse_ref[h] = top + jnp.log2(sums)


def attend_back_kernel(
    order_ref,
    own_ref,
    rank_ref,
    q_ref,
    kv_ref,
    do_ref,
    o_ref,
    lse_ref,
    dq_ref,
    dkv_ref,
    corner_ref,
    hide_ref,
):
    @pl.when(pl.program_id(0) == 0)
    def _():
        prepare(order_ref, own_ref, rank_ref, corner_ref, hide_ref)

    per = 4
    local = q_ref.shape[1]
    chunks = kv_ref.shape[0]
    columns, keys, values = load_keys(rank_ref, kv_ref, per)
    corner = corner_ref[...]
    hide = hide_ref[...]
    blank = jnp.zeros((16, local), low)
    wide_blank = jnp.zeros((HEAD_DIM, local), low)
    terms = [None] * len(keys)
    for h in range(GROUP):
        part = slice(h * HEAD_DIM, (h + 1) * HEAD_DIM)
        query = q_ref[part, :]
        back = do_ref[part, :]
        delta = jnp.sum(
            back.astype(jnp.float32) * o_ref[part, :].astype(jnp.float32), axis=0, keepdims=True
        )
        query_side = jnp.concatenate([query, in_three(-lse_ref[h]), hide, blank, blank], axis=0)
        back_side = jnp.concatenate([in_three(-delta), blank, blank, blank, back], axis=0)
        pair = jnp.concatenate(
            [
                jnp.concatenate([query, wide_blank], axis=0).T,
                jnp.concatenate([wide_blank, back], axis=0).T,
            ],
            axis=0,
        )
        grad_query = None
        for c in range(len(keys)):
            weights = jnp.exp2(score(c, keys, query_side, corner))
            grad = (weights * contract(values[c], back_side, 1, 0)).astype(low)
            term = contract(jnp.concatenate([grad, weights.astype(low)], axis=1), pair, 1, 0)
            terms[c] = term if terms[c] is None else terms[c] + term
            term = contract(columns[c][:HEAD_DIM], grad, 1, 0)
            grad_query = term if grad_query is None else grad_query + term
        dq_ref[part, :] = grad_query * HEAD_DIM ** (-0.5)
    lane = lax.broadcasted_iota(jnp.int32, (1, 2 * HEAD_DIM), 1)
    scale = jnp.where(lane < HEAD_DIM, 1.0 / LOG2E, 1.0)
    for i in range(chunks):
        term = terms[i // per][i % per * local : (i % per + 1) * local]
        dkv_ref[lax.rem(rank_ref[0] + i, chunks), 0] = (term * scale).astype(low)


def attention_specs(chunks, local, start=0):
    wide = GROUP * HEAD_DIM
    heads = pl.BlockSpec((wide, local), lambda g: (g + start, 0))
    keys = pl.BlockSpec((chunks, 1, 2 * HEAD_DIM, local), lambda g: (0, g + start, 0, 0))
    sums = pl.BlockSpec((GROUP, 1, local), lambda g: (g + start, 0, 0))
    return heads, keys, sums


def scalars():
    return pl.BlockSpec(memory_space=pltpu.SMEM)


def attention_scratch(local, slots):
    return [pltpu.VMEM((local, local), jnp.float32), pltpu.VMEM((slots, local), low)]


def attend(order, own, rank, query, keys):
    chunks, _, _, local = keys.shape
    heads, kv, sums = attention_specs(chunks, local)
    return pl.pallas_call(
        attend_kernel,
        grid=(KV_HEADS,),
        out_shape=(
            jax.ShapeDtypeStruct((D, local), low),
            jax.ShapeDtypeStruct((HEADS, 1, local), jnp.float32),
        ),
        in_specs=[scalars(), scalars(), scalars(), heads, kv],
        out_specs=(heads, sums),
        scratch_shapes=attention_scratch(local, order.shape[0]),
        compiler_params=pltpu.CompilerParams(vmem_limit_bytes=60 * 1024 * 1024),
        cost_estimate=pl.CostEstimate(
            flops=ATTEND_FLOPS, bytes_accessed=1000, transcendentals=0
        ),
        name="attend",
    )(order, own, rank, query, keys)


def attend_back(start, count, order, own, rank, query, keys, back, out, lse):
    chunks, _, _, local = keys.shape
    heads, kv, sums = attention_specs(chunks, local, start)
    part, _, _ = attention_specs(chunks, local)
    grads = pl.BlockSpec((chunks, 1, local, 2 * HEAD_DIM), lambda g: (0, g, 0, 0))
    return pl.pallas_call(
        attend_back_kernel,
        grid=(count,),
        out_shape=(
            jax.ShapeDtypeStruct((count * GROUP * HEAD_DIM, local), jnp.float32),
            jax.ShapeDtypeStruct((chunks, count, local, 2 * HEAD_DIM), low),
        ),
        in_specs=[scalars(), scalars(), scalars(), heads, kv, heads, heads, sums],
        out_specs=(part, grads),
        scratch_shapes=attention_scratch(local, order.shape[0]),
        compiler_params=pltpu.CompilerParams(vmem_limit_bytes=60 * 1024 * 1024),
        cost_estimate=pl.CostEstimate(
            flops=BACK_FLOPS * count // KV_HEADS, bytes_accessed=1000, transcendentals=0
        ),
        name=f"attend_back_{start}",
    )(order, own, rank, query, keys, back, out, lse)


def whole_call(kernel, name, flops, out_shape, *operands, near=False):
    single = not isinstance(out_shape, tuple)
    shapes = (out_shape,) if single else out_shape
    far = [] if near else [i for i, value in enumerate(operands) if value.ndim > 1]
    away = [] if near else list(range(len(shapes)))
    space = pl.BlockSpec(memory_space=pltpu.VMEM if near else pltpu.HBM)

    def staged(*refs):
        ins = list(refs[: len(operands)])
        outs = list(refs[len(operands) : len(operands) + len(shapes)])
        scratch = refs[len(operands) + len(shapes) :]
        copies = []
        for k, i in enumerate(far):
            copies.append(pltpu.make_async_copy(ins[i], scratch[k], scratch[-2].at[k]))
            ins[i] = scratch[k]
        for copy in copies:
            copy.start()
        for copy in copies:
            copy.wait()
        held = outs if near else list(scratch[len(far) : len(far) + len(away)])
        kernel(*ins, *held)
        copies = [
            pltpu.make_async_copy(held[k], outs[k], scratch[-1].at[k]) for k in away
        ]
        for copy in copies:
            copy.start()
        for copy in copies:
            copy.wait()

    scratch = [pltpu.VMEM(operands[i].shape, operands[i].dtype) for i in far]
    scratch += [pltpu.VMEM(shapes[k].shape, shapes[k].dtype) for k in away]
    if not near:
        scratch += [pltpu.SemaphoreType.DMA((len(far),)), pltpu.SemaphoreType.DMA((len(away),))]
    outs = pl.pallas_call(
        staged,
        out_shape=shapes,
        in_specs=[scalars() if value.ndim == 1 else space for value in operands],
        out_specs=(space,) * len(shapes),
        scratch_shapes=scratch,
        compiler_params=pltpu.CompilerParams(vmem_limit_bytes=(24 if near else 60) * 1024 * 1024),
        cost_estimate=pl.CostEstimate(flops=flops, bytes_accessed=1000, transcendentals=0),
        name=name,
    )(*operands)
    return outs[0] if single else outs


def stage_kernel(core_ref, qkv_ref, gains_ref, near_ref):
    first = core_ref[0] == 0
    shard = qkv_ref.shape[0]
    gains = jnp.concatenate(
        [gains_ref[...], jnp.zeros((6, gains_ref.shape[1]), jnp.float32)], axis=0
    )
    gains = jnp.concatenate([gains, jnp.zeros((8, 128 - shard), jnp.float32)], axis=1).T
    near = jnp.concatenate(
        [
            jnp.where(first, qkv_ref[:, : QKVW // 2], qkv_ref[:, QKVW // 2 :]),
            gains[:shard, :2],
            jnp.zeros((shard, PADDED - QKVW // 2 - 2), jnp.float32),
        ],
        axis=1,
    ).astype(low)
    for j in range(near_ref.shape[0]):
        near_ref[j] = near


def stage_feed_kernel(place_ref, expand_ref, down_ref, proj_ref, wide_ref, tall_ref):
    first = place_ref[0] == 0
    step = FF // 16
    parts = []
    for k in range(4):
        left = expand_ref[:, 2 * k * step : (2 * k + 1) * step]
        right = expand_ref[:, (2 * k + 1) * step : (2 * k + 2) * step]
        parts.append(jnp.where(first, left, right))
    proj = jnp.where(first, proj_ref[:, : D // 2], proj_ref[:, D // 2 :])
    quarter = proj[:, :PROJ]
    for k in range(1, 4):
        quarter = jnp.where(place_ref[2] == k, proj[:, k * PROJ : (k + 1) * PROJ], quarter)
    blank = jnp.zeros((proj.shape[0], BESIDE - FF // 4 - PROJ), jnp.float32)
    wide = jnp.concatenate(parts + [quarter, blank], axis=1).astype(low)
    tall = down_ref[...].astype(low)
    for j in range(wide_ref.shape[0]):
        wide_ref[j] = wide
        tall_ref[j] = tall


def stage_feed(place, expand, down, proj, groups):
    shard = expand.shape[0]
    half = down.shape[0] // 2
    outs = [(groups, shard, BESIDE), (groups, half, D)]
    return pl.pallas_call(
        stage_feed_kernel,
        grid_spec=pltpu.PrefetchScalarGridSpec(
            num_scalar_prefetch=1,
            grid=(1,),
            in_specs=[
                pl.BlockSpec((shard, HALF), lambda i, place: (0, place[1])),
                pl.BlockSpec((half, D), lambda i, place: (place[0], 0)),
                pl.BlockSpec(proj.shape, lambda i, place: (0, 0)),
            ],
            out_specs=[pl.BlockSpec(out, lambda i, place: (0, 0, 0)) for out in outs],
        ),
        out_shape=[jax.ShapeDtypeStruct(out, low) for out in outs],
        compiler_params=pltpu.CompilerParams(vmem_limit_bytes=60 * 1024 * 1024),
        cost_estimate=pl.CostEstimate(flops=1000, bytes_accessed=8 * 10**6, transcendentals=0),
        name="stage_feed",
    )(place, expand, down, proj)


def rotated(block, cosine, sine):
    first = block[: HEAD_DIM // 2]
    second = block[HEAD_DIM // 2 :]
    return [first * cosine - second * sine, second * cosine + first * sine]


def project_kernel(
    core_ref,
    rows_ref,
    mine_ref,
    theirs_ref,
    cosine_ref,
    sine_ref,
    normed_ref,
    query_ref,
    keys_ref,
    gains_ref,
):
    first_core = core_ref[0] == 0
    cosine = cosine_ref[...]
    sine = sine_ref[...]
    rows = rows_ref[...].astype(jnp.float32).T
    gains = mine_ref[:, PADDED - 128 : PADDED].astype(jnp.float32).T
    at = QKVW // 2 - (PADDED - 128)
    gains_ref[...] = gains[at : at + 2]
    normed = (rows * rms_scale(rows) * gains[at : at + 1]).astype(low)
    normed_ref[...] = normed
    near = contract(normed, mine_ref[...], 1, 0).T
    away = contract(normed, theirs_ref[...], 1, 0).T
    half = QKVW // 2
    one = jnp.where(first_core, near, away)[:half]
    two = jnp.where(first_core, away, near)[:half]
    mixed = jnp.concatenate([one, two], axis=0)
    scale = HEAD_DIM ** (-0.5) * LOG2E
    for h in range(HEADS):
        span = slice(h * HEAD_DIM, (h + 1) * HEAD_DIM)
        turned = jnp.concatenate(rotated(mixed[span], cosine, sine), axis=0)
        query_ref[span] = (turned * scale).astype(low)
    for g in range(KV_HEADS):
        at = D + g * HEAD_DIM
        to = at + KV_HEADS * HEAD_DIM
        pair = rotated(mixed[at : at + HEAD_DIM], cosine, sine) + [mixed[to : to + HEAD_DIM]]
        pair = jnp.concatenate(pair, axis=0).astype(low)
        for j in range(keys_ref.shape[0]):
            keys_ref[j, g] = pair


def join_proj(ref):
    return jnp.concatenate([ref[q, :, :PROJ] for q in range(4)], axis=1)


def rows_kernel(own_ref, other_ref, out_ref):
    out_ref[...] = jnp.concatenate([own_ref[...], other_ref[...]], axis=1).T


def branch_kernel(mixed_ref, beside_ref, out_ref, proj_ref, sem):
    copy = pltpu.make_async_copy(beside_ref.at[:, :, pl.ds(FF // 4, 128)], proj_ref, sem)
    copy.start()
    copy.wait()
    product = contract(mixed_ref[...], join_proj(proj_ref), 1, 0)
    blank = jnp.zeros((product.shape[0], 512 - product.shape[1]), jnp.float32)
    out_ref[...] = jnp.concatenate([product, blank], axis=1).astype(low)


def branch(mixed, beside):
    rows, width = mixed.shape
    whole = pl.BlockSpec(memory_space=pltpu.VMEM)
    return pl.pallas_call(
        branch_kernel,
        out_shape=(
            jax.ShapeDtypeStruct((rows, 512), low),
            jax.ShapeDtypeStruct((4, width, 128), low),
        ),
        in_specs=[whole, pl.BlockSpec(memory_space=pltpu.HBM)],
        out_specs=(whole, whole),
        scratch_shapes=[pltpu.SemaphoreType.DMA(())],
        compiler_params=pltpu.CompilerParams(vmem_limit_bytes=60 * 1024 * 1024),
        cost_estimate=pl.CostEstimate(flops=1000, bytes_accessed=1000, transcendentals=0),
        name="branch",
    )(mixed, beside)


def middle_kernel(
    core_ref,
    near_ref,
    away_ref,
    rows_ref,
    other_ref,
    gains_ref,
    mid_ref,
    normed_ref,
    normed_other,
):
    first_core = core_ref[0] == 0
    local = rows_ref.shape[1]
    for at, rows, out in ((0, rows_ref, normed_ref), (local, other_ref, normed_other)):
        near = near_ref[at : at + local, : D // 2].astype(jnp.float32)
        away = away_ref[local - at : 2 * local - at, : D // 2].astype(jnp.float32)
        near, away = jnp.where(first_core, near, away), jnp.where(first_core, away, near)
        middle = rows[...].astype(jnp.float32).T + jnp.concatenate([near, away], axis=1)
        if at == 0:
            mid_ref[...] = middle
        out[...] = (middle * rms_scale(middle) * gains_ref[1:2]).astype(low)


def turn_kernel(
    core_ref,
    own_ref,
    came_ref,
    mid_ref,
    back_ref,
    gains_ref,
    mine_ref,
    theirs_ref,
    out_ref,
    grad_ref,
    grad_out_ref,
    kept_ref,
    sent_ref,
    gain_grad_ref,
):
    first_core = core_ref[0] == 0
    normed = own_ref[...] + came_ref[...].astype(jnp.float32)
    middle = mid_ref[...]
    inverse = rms_scale(middle)
    scaled = normed * gains_ref[1:2]
    inner = jnp.mean(scaled * middle, axis=-1, keepdims=True)
    grad = back_ref[...].astype(jnp.float32) + inverse * (
        scaled - middle * inverse * inverse * inner
    )
    grad_ref[...] = grad
    gain_grad_ref[...] = jnp.sum(normed * middle * inverse, axis=0, keepdims=True)
    one = grad[:, : D // 2]
    two = grad[:, D // 2 :]
    near = jnp.where(first_core, one, two).astype(low)
    away = jnp.where(first_core, two, one).astype(low)
    grad_out = contract(near, join_proj(mine_ref), 1, 1) + contract(
        away, join_proj(theirs_ref), 1, 1
    )
    grad_out_ref[...] = grad_out.T.astype(low)
    product = contract(out_ref[...], grad.astype(low), 1, 0)
    groups, window, _ = kept_ref.shape
    shard = product.shape[0] // groups
    for j in range(groups):
        top = product[j * shard : j * shard + window]
        bottom = product[(j + 1) * shard - window : (j + 1) * shard]
        kept_ref[j] = jnp.where(first_core, top, bottom).astype(low)
        sent_ref[j] = jnp.where(first_core, bottom, top).astype(low)


def emit_kernel(mid_ref, own_ref, came_ref, out_ref):
    value = mid_ref[...] + own_ref[...] + came_ref[...].astype(jnp.float32)
    out_ref[...] = value.T.astype(low)


def feed_kernel(
    rows_one,
    rows_two,
    back_one,
    back_two,
    expand_ref,
    down_ref,
    fed_ref,
    fed_other_ref,
    normed_ref,
    normed_other_ref,
    tall_ref,
    expand_grad_ref,
    rows_ref,
    back_ref,
    columns_ref,
    fed_sum,
    normed_sum,
):
    local = rows_one.shape[0]
    h = pl.program_id(0)

    @pl.when(h == 0)
    def _():
        rows_ref[:local] = rows_one[...]
        rows_ref[local:] = rows_two[...]
        back_ref[:local] = back_one[...]
        back_ref[local:] = back_two[...]
        columns_ref[...] = rows_ref[...].T

    rows = rows_ref[...]
    back = back_ref[...]
    columns = columns_ref[...]
    down = down_ref[...]
    step = down_ref.shape[0]
    wide = jnp.concatenate([expand_ref[0], expand_ref[1]], axis=1)
    both = contract(rows, wide, 1, 0)
    gate = both[:, :step]
    upward = both[:, step:]
    sigmoid = jax.nn.sigmoid(gate)
    active = gate * sigmoid
    hidden = (active * upward).astype(low)
    grad_hidden = contract(back, down, 1, 1)
    grad_up = (grad_hidden * active).astype(low)
    grad_gate = (grad_hidden * upward * sigmoid * (1.0 + gate * (1.0 - sigmoid))).astype(low)
    fed = contract(hidden, down, 1, 0)
    grad_both = jnp.concatenate([grad_gate, grad_up], axis=1)
    normed = contract(grad_both, wide, 1, 1)
    product = contract(hidden.T, back, 1, 0)
    quarter = FF // 64
    for y in range(4):
        tall_ref[y] = jnp.concatenate(
            [product[(4 * j + y) * quarter : (4 * j + y + 1) * quarter] for j in range(4)], axis=0
        ).astype(low)
    both = contract(columns, grad_both, 1, 0).astype(low)
    expand_grad_ref[0] = both[:, :step]
    expand_grad_ref[1] = both[:, step:]

    @pl.when(h == 0)
    def _():
        fed_sum[...] = fed
        normed_sum[...] = normed

    @pl.when(h == 1)
    def _():
        fed_all = fed_sum[...] + fed
        normed_all = normed_sum[...] + normed
        fed_ref[...] = fed_all[:local]
        fed_other_ref[...] = fed_all[local:].astype(low)
        normed_ref[...] = normed_all[:local]
        normed_other_ref[...] = normed_all[local:].astype(low)


def feed(rows, back, expand, down):
    local, width = rows[0].shape
    step = FF // 4
    held = pl.BlockSpec((local, width), lambda h: (0, 0))
    pair = pl.BlockSpec((2, width, step), lambda h: (h, 0, 0))
    tall = pl.BlockSpec((step, width), lambda h: (h, 0))
    rows_out = pl.BlockSpec((4, FF // 16, width), lambda h: (0, h, 0))
    own = jax.ShapeDtypeStruct((local, width), jnp.float32)
    other = jax.ShapeDtypeStruct((local, width), low)
    return pl.pallas_call(
        feed_kernel,
        grid=(2,),
        out_shape=(
            own,
            other,
            own,
            other,
            jax.ShapeDtypeStruct((4, 8 * TALL, width), low),
            jax.ShapeDtypeStruct((4, width, step), low),
        ),
        in_specs=[held] * 4 + [pair, tall],
        out_specs=(held,) * 4 + (rows_out, pair),
        scratch_shapes=[
            pltpu.VMEM((2 * local, width), low),
            pltpu.VMEM((2 * local, width), low),
            pltpu.VMEM((width, 2 * local), low),
            pltpu.VMEM((2 * local, width), jnp.float32),
            pltpu.VMEM((2 * local, width), jnp.float32),
        ],
        compiler_params=pltpu.CompilerParams(vmem_limit_bytes=60 * 1024 * 1024),
        cost_estimate=pl.CostEstimate(flops=FEED_FLOPS, bytes_accessed=1000, transcendentals=0),
        name="feed",
    )(*rows, *back, expand, down)


def stack_kernel(tall_in, kept_ref, came_ref, tall_ref, held, sem):
    proj = (kept_ref[...].astype(jnp.float32) + came_ref[...].astype(jnp.float32)).astype(low)
    rows = proj.shape[1] // 4
    for y in range(4):
        held[y] = jnp.concatenate(
            [proj[j, y * rows : (y + 1) * rows] for j in range(proj.shape[0])], axis=0
        )
    span = pl.ds(tall_ref.shape[1] - held.shape[1], held.shape[1])
    copy = pltpu.make_async_copy(held, tall_ref.at[:, span], sem)
    copy.start()
    copy.wait()


def stack(tall, kept, came):
    groups, window, width = kept.shape
    away = pl.BlockSpec(memory_space=pltpu.HBM)
    whole = pl.BlockSpec(memory_space=pltpu.VMEM)
    return pl.pallas_call(
        stack_kernel,
        out_shape=jax.ShapeDtypeStruct(tall.shape, low),
        in_specs=[away, whole, whole],
        out_specs=away,
        scratch_shapes=[
            pltpu.VMEM((4, groups * window // 4, width), low),
            pltpu.SemaphoreType.DMA(()),
        ],
        input_output_aliases={0: 0},
        compiler_params=pltpu.CompilerParams(vmem_limit_bytes=60 * 1024 * 1024),
        cost_estimate=pl.CostEstimate(flops=1000, bytes_accessed=1000, transcendentals=0),
        name="stack",
    )(tall, kept, came)


def adam_step(master, first, second, grad, rate, decay):
    new_first = beta_first * first + (1.0 - beta_first) * grad
    new_second = beta_second * second + (1.0 - beta_second) * grad * grad
    fix_one = 1.0 - beta_first**STEP
    fix_two = 1.0 - beta_second**STEP
    update = new_first / fix_one / (jnp.sqrt(new_second / fix_two) + adam_eps) + decay * master
    return (master - rate * update, new_first, new_second)


def update_kernel(
    core_ref,
    wide_ref,
    wide_other,
    rest_ref,
    rest_other,
    gains_ref,
    gains_first,
    gains_second,
    *refs,
):
    states, outs, gain_outs = refs[:12], refs[12:24], refs[24:27]
    held = refs[27:31]
    near = refs[31:35]
    load_sem, store_sem, near_sem = refs[35:]
    grads = (wide_ref, wide_other, rest_ref, rest_other)
    fetches = [pltpu.make_async_copy(grads[k], near[k], near_sem.at[k]) for k in range(4)]
    wide_ref, wide_other, rest_ref, rest_other = near
    first_core = core_ref[0] == 0
    shard = gains_ref.shape[1]
    quarter = held[3].shape[1] // 8

    def both(mine, theirs):
        return (
            jnp.where(first_core, mine, theirs).astype(jnp.float32),
            jnp.where(first_core, theirs, mine).astype(jnp.float32),
        )

    def expand_grad(q):
        step = FF // 16
        one, two = both(rest_ref[q, :shard, : FF // 4], rest_other[q, :shard, : FF // 4])
        parts = []
        for k in range(4):
            span = slice(k * step, (k + 1) * step)
            parts += [one[:, span], two[:, span]]
        return jnp.concatenate(parts, axis=1)

    def tall_grads():
        parts = [both(tall_part(rest_ref, q), tall_part(rest_other, q)) for q in range(4)]
        one = [part[0] for part in parts]
        two = [part[1] for part in parts]
        down = jnp.concatenate([part[:quarter] for part in one + two], axis=0)
        proj = jnp.concatenate(
            [part[TALL - 16 :] for part in one]
            + [two[0][TALL - 8 :]]
            + [part[TALL - 16 :] for part in two[1:]],
            axis=0,
        )
        return down, proj

    def wide_grad():
        one, two = both(wide_ref[:shard], wide_other[:shard])
        return jnp.concatenate([one[:, : QKVW // 2], two[:, : QKVW // 2]], axis=1)

    full = slice(None)
    pieces = [(2, pl.ds(i * HALF, HALF), 2.0 * D ** (-0.5)) for i in range(4)]
    pieces += [
        (3, full, 2.0 * FF ** (-0.5)),
        (1, full, 2.0 * (D // 8) ** (-0.5)),
        (0, full, 2.0 * D ** (-0.5)),
    ]

    def copies(p, out):
        weight, columns, _ = pieces[p]
        for k in range(3):
            near = held[weight].at[k, :, columns]
            if out:
                yield pltpu.make_async_copy(
                    near, outs[3 * weight + k].at[:, columns], store_sem.at[p, k]
                )
            else:
                yield pltpu.make_async_copy(
                    states[3 * weight + k].at[:, columns], near, load_sem.at[p, k]
                )

    for copy in fetches:
        copy.start()
    for p in range(len(pieces)):
        for copy in copies(p, False):
            copy.start()
    for copy in fetches:
        copy.wait()
    down, proj = tall_grads()
    for p, (weight, columns, rate) in enumerate(pieces):
        for copy in copies(p, False):
            copy.wait()
        if p < 4:
            grad = expand_grad(p % 2 * 2 + p // 2)
        else:
            grad = (down, proj)[p - 4] if p < 6 else wide_grad()
        new = adam_step(*[held[weight][k, :, columns] for k in range(3)], grad, rate, 0.1)
        for k in range(3):
            held[weight][k, :, columns] = new[k]
        for copy in copies(p, True):
            copy.start()
    one, two = both(wide_ref[...], wide_other[...])
    grad = one[shard : shard + 2, :shard] + two[shard : shard + 2, :shard]
    new = adam_step(gains_ref[...], gains_first[...], gains_second[...], grad, 1.0, 0.0)
    for out, value in zip(gain_outs, new):
        out[...] = value
    for p in range(len(pieces)):
        for copy in copies(p, True):
            copy.wait()


def update(core, wide, wide_other, rest, rest_other, gains, states):
    whole = pl.BlockSpec(memory_space=pltpu.VMEM)
    away = pl.BlockSpec(memory_space=pltpu.HBM)
    shapes = [jax.ShapeDtypeStruct(value.shape, jnp.float32) for value in states + gains]
    return pl.pallas_call(
        update_kernel,
        out_shape=shapes,
        in_specs=[scalars()] + [away] * 4 + [whole] * 3 + [away] * 12,
        out_specs=[away] * 12 + [whole] * 3,
        scratch_shapes=[
            pltpu.VMEM((3,) + states[3 * weight].shape, jnp.float32) for weight in range(4)
        ]
        + [pltpu.VMEM(value.shape, low) for value in (wide, wide, rest, rest)]
        + [pltpu.SemaphoreType.DMA(shape) for shape in ((7, 3), (7, 3), (4,))],
        compiler_params=pltpu.CompilerParams(vmem_limit_bytes=32 * 1024 * 1024),
        cost_estimate=pl.CostEstimate(
            flops=1000, bytes_accessed=30 * 10**6, transcendentals=0
        ),
        name="update",
    )(core, wide, wide_other, rest, rest_other, *gains, *states)


def back_rotated(block, cosine, sine):
    first = block[: HEAD_DIM // 2]
    second = block[HEAD_DIM // 2 :]
    return [first * cosine + second * sine, second * cosine - first * sine]


def late_kernel(
    core_ref,
    first_terms,
    second_terms,
    first_dq,
    second_dq,
    cosine_ref,
    sine_ref,
    mine_ref,
    theirs_ref,
    rows_ref,
    grad_ref,
    gain_ref,
    gain_grad_ref,
    out_ref,
    near_ref,
    away_ref,
    gains_ref,
):
    cosine = cosine_ref[...]
    sine = sine_ref[...]
    first_core = core_ref[0] == 0
    parts = []
    for ref in (first_dq, second_dq):
        for h in range(ref.shape[0] // HEAD_DIM):
            parts += back_rotated(ref[h * HEAD_DIM : (h + 1) * HEAD_DIM], cosine, sine)
    values = []
    for ref in (first_terms, second_terms):
        for g in range(ref.shape[1]):
            block = ref[0, g].astype(jnp.float32)
            for j in range(1, ref.shape[0]):
                block = block + ref[j, g].astype(jnp.float32)
            block = block.T
            parts += back_rotated(block[:HEAD_DIM], cosine, sine)
            values.append(block[HEAD_DIM:])
    mixed = jnp.concatenate(parts + values, axis=0)
    half = QKVW // 2
    blank = jnp.zeros((PADDED - half, mixed.shape[1]), jnp.float32)
    one = mixed[:half]
    two = mixed[half:]
    near = jnp.concatenate([jnp.where(first_core, one, two), blank], axis=0).T.astype(low)
    away = jnp.concatenate([jnp.where(first_core, two, one), blank], axis=0).T.astype(low)
    grad_normed = contract(near, mine_ref[...], 1, 1) + contract(away, theirs_ref[...], 1, 1)
    rows = rows_ref[...].astype(jnp.float32).T
    inverse = rms_scale(rows)
    scaled = grad_normed * gain_ref[0:1]
    inner = jnp.mean(scaled * rows, axis=-1, keepdims=True)
    back = inverse * (scaled - rows * inverse * inverse * inner)
    out_ref[...] = (grad_ref[...] + back).T.astype(low)
    gain_one = jnp.sum(grad_normed * rows * inverse, axis=0, keepdims=True)
    gains = (gain_one, gain_grad_ref[...])
    near_ref[...] = near
    away_ref[...] = away
    gains_ref[...] = jnp.concatenate(gains, axis=0)


def weight_kernel(
    normed_ref, normed_other, near_ref, came_ref, gains_ref, tall_ref, out_ref
):
    columns = jnp.concatenate([normed_ref[...], normed_other[...]], axis=0).T
    product = contract(columns, jnp.concatenate([near_ref[...], came_ref[...]], axis=0), 1, 0)
    groups = out_ref.shape[0] // 2
    shard = product.shape[0] // groups
    lanes = product.shape[1]
    gains = gains_ref[...]
    quarter = FF // 64
    down = tall_ref[: groups * quarter].astype(jnp.float32)
    proj = tall_ref[groups * quarter :].astype(jnp.float32)
    for j in range(groups):
        span = slice(j * shard, (j + 1) * shard)
        tail = padded_rows(gains[:, span], 128 - shard)
        tail = jnp.concatenate(
            [tail, jnp.zeros((128 - shard, lanes - shard), jnp.float32)], axis=1
        )
        summed = jnp.concatenate([product[span], tail], axis=0)
        tall = jnp.concatenate(
            [down[j * quarter : (j + 1) * quarter], proj[j * 16 : (j + 1) * 16]], axis=0
        )
        halves = [
            jnp.concatenate([padded_rows(tall[:, span], 64) for span in spans], axis=0)
            for spans in (TALL_NARROW, TALL_WIDE)
        ]
        put_halves(out_ref, j, jnp.concatenate([summed[:, : QKVW // 2]] + halves, axis=1))


def padded_rows(block, rows):
    return jnp.concatenate(
        [block, jnp.zeros((rows - block.shape[0], block.shape[1]), jnp.float32)], axis=0
    )


def put_halves(out_ref, j, block):
    groups = out_ref.shape[0] // 2
    rows = out_ref.shape[1]
    for half in range(2):
        out_ref[half * groups + j] = block[half * rows : (half + 1) * rows].astype(low)


def pack_early_kernel(expand_ref, out_ref):
    for j in range(expand_ref.shape[0]):
        put_halves(out_ref, j, padded_rows(expand_ref[j].astype(jnp.float32), 128))


def sum_kernel(early_ref, late_ref, out_ref):
    sums = []
    for ref in (early_ref, late_ref):
        block = ref[0].astype(jnp.float32)
        for j in range(1, ref.shape[0]):
            block = block + ref[j].astype(jnp.float32)
        sums.append(block.astype(low))
    block = jnp.concatenate(sums, axis=1)
    for j in range(out_ref.shape[0]):
        out_ref[j] = block


def finish_kernel(all_ref, wide_ref, rest_ref):
    count = all_ref.shape[0] // 2
    rows = all_ref.shape[1]
    expand = slice(0, FF // 4)
    wide = slice(FF // 4, FF // 4 + PADDED)
    tall = slice(FF // 4 + LATE - 512, FF // 4 + LATE)
    for half in range(2):
        span = slice(half * rows, (half + 1) * rows)
        block = all_ref[half * count, :, wide].astype(jnp.float32)
        for y in range(1, count):
            block = block + all_ref[half * count + y, :, wide].astype(jnp.float32)
        wide_ref[span] = block.astype(low)
        for y in range(count):
            rest_ref[y, span] = jnp.concatenate(
                [all_ref[half * count + y, :, lanes] for lanes in (expand, tall)], axis=1
            )


def tall_part(rest, q):
    parts = []
    for lanes in (slice(FF // 4 + 128, FF // 4 + 512), slice(FF // 4 + 32, FF // 4 + 128)):
        parts += [rest[q, at : at + TALL, lanes] for at in (0, rest.shape[1] // 2)]
    return jnp.concatenate(parts, axis=1)


def on_device(
    inputs,
    cotangent,
    span_order,
    w_qkv,
    qkv_first,
    qkv_second,
    w_proj,
    proj_first,
    proj_second,
    w_expand,
    expand_first,
    expand_second,
    w_down,
    down_first,
    down_second,
    gains,
    gains_first,
    gains_second,
):
    core = lax.axis_index("core")
    rank = lax.axis_index(CTX)
    groups = 8
    batch, local, width = inputs.shape
    shard = w_qkv.shape[0]
    hidden_shard = w_down.shape[0] // 2

    y = lax.axis_index("y")
    place = jnp.stack([core, y % 2 * 2 + y // 2, y]).astype(jnp.int32)
    core_at = place[:1]
    rank_at = rank.reshape(1).astype(jnp.int32)
    near = whole_call(
        stage_kernel,
        "stage",
        1000,
        jax.ShapeDtypeStruct((groups, shard, NEAR), low),
        core_at,
        w_qkv,
        gains,
    )
    mine = exchange(near, CTX).reshape(width, NEAR)
    expand_low, down_low = stage_feed(place, w_expand, w_down, w_proj, groups)
    back_rows = cotangent.reshape(local, width)
    order_own = lax.dynamic_slice_in_dim(span_order, 2 * rank, 2)
    own_pos = (
        order_own[:, None] * (local // 2) + jnp.arange(local // 2, dtype=jnp.int32)
    ).reshape(local)
    cosine, sine = rope_tables(own_pos)
    mine, cosine, sine, expand_low, down_low, back_rows = lax.optimization_barrier(
        (mine, cosine, sine, expand_low, down_low, back_rows)
    )
    theirs = swap_cores(mine)
    expand_low = exchange(expand_low, CTX).reshape(width, BESIDE)

    tokens = inputs.reshape(local, width).T
    square = (local, width)
    normed_one, query, all_keys, full_gains = whole_call(
        project_kernel,
        "project",
        1000,
        (
            jax.ShapeDtypeStruct(square, low),
            jax.ShapeDtypeStruct((width, local), low),
            jax.ShapeDtypeStruct((groups, KV_HEADS, 2 * HEAD_DIM, local), low),
            jax.ShapeDtypeStruct((2, width), jnp.float32),
        ),
        core_at,
        tokens,
        mine,
        theirs,
        cosine,
        sine,
    )
    all_keys, expand_low = lax.optimization_barrier((all_keys, expand_low))
    expand_low = lax.all_gather(expand_low, "y", axis=0, tiled=False)
    all_keys = exchange(all_keys, CTX)
    all_keys, down_low = lax.optimization_barrier((all_keys, down_low))
    normed_other = swap_cores(normed_one)
    tokens_other = swap_cores(tokens)
    half_down = exchange(down_low, CTX).reshape(HALF, width)
    attended, lse = attend(span_order, order_own, rank_at, query, all_keys)
    mixed = whole_call(
        rows_kernel,
        "rows",
        1000,
        jax.ShapeDtypeStruct((2 * local, width), low),
        attended,
        swap_cores(attended),
        near=True,
    )
    mixed, expand_low = lax.optimization_barrier((mixed, expand_low))
    mixed, proj_mine = branch(mixed, expand_low)
    middle, normed_two, normed_two_other = whole_call(
        middle_kernel,
        "middle",
        1000,
        (
            jax.ShapeDtypeStruct(square, jnp.float32),
            jax.ShapeDtypeStruct(square, low),
            jax.ShapeDtypeStruct(square, low),
        ),
        core_at,
        mixed,
        swap_cores(mixed),
        tokens,
        tokens_other,
        full_gains,
    )
    proj_theirs = swap_cores(proj_mine)
    normed_two, half_down = lax.optimization_barrier((normed_two, half_down))

    fed, fed_other, grad_normed, grad_other, tall, grad_expand = feed(
        (normed_two, normed_two_other),
        (back_rows, swap_cores(back_rows)),
        expand_low,
        half_down,
    )
    grad_middle, grad_att, proj_kept, proj_sent, gain_grad_two = whole_call(
        turn_kernel,
        "turn",
        3 * 10**9,
        (
            jax.ShapeDtypeStruct(square, jnp.float32),
            jax.ShapeDtypeStruct((width, local), low),
            jax.ShapeDtypeStruct((groups, 64, width), low),
            jax.ShapeDtypeStruct((groups, 64, width), low),
            jax.ShapeDtypeStruct((1, width), jnp.float32),
        ),
        core_at,
        grad_normed,
        swap_cores(grad_other),
        middle,
        back_rows,
        full_gains,
        proj_mine,
        proj_theirs,
        attended,
    )
    output = whole_call(
        emit_kernel,
        "emit",
        1000,
        jax.ShapeDtypeStruct((width, local), low),
        middle,
        fed,
        swap_cores(fed_other),
    )

    expand_sum = lax.psum_scatter(grad_expand, "y", scatter_dimension=0, tiled=False)
    context = (span_order, order_own, rank_at, query, all_keys, grad_att, attended, lse)
    first_query, first_terms = attend_back(0, SPLIT, *context)
    first_terms, tall = lax.optimization_barrier((first_terms, tall))
    first_terms = exchange(first_terms, CTX)
    grad_query, key_terms = attend_back(SPLIT, KV_HEADS - SPLIT, *context)
    key_terms = exchange(key_terms, CTX)
    early = whole_call(
        pack_early_kernel,
        "pack_early",
        1000,
        jax.ShapeDtypeStruct((2 * groups, 64, FF // 4), low),
        expand_sum.reshape(groups, shard, FF // 4),
    )
    key_terms, first_terms, output, early = lax.optimization_barrier(
        (key_terms, first_terms, output, early)
    )
    early = exchange(early, CHIP_CTX)
    tall = stack(tall, proj_kept, swap_cores(proj_sent))
    tall = lax.psum_scatter(tall, "y", scatter_dimension=0, tiled=False)
    half = jax.ShapeDtypeStruct((local, PADDED), low)
    input_grad, near, away, late_gains = whole_call(
        late_kernel,
        "late",
        30 * 10**9,
        (
            jax.ShapeDtypeStruct((width, local), low),
            half,
            half,
            jax.ShapeDtypeStruct((2, width), jnp.float32),
        ),
        core_at,
        first_terms,
        key_terms,
        first_query,
        grad_query,
        cosine,
        sine,
        mine,
        theirs,
        tokens,
        grad_middle,
        full_gains,
        gain_grad_two,
    )
    late = whole_call(
        weight_kernel,
        "weight",
        1000,
        jax.ShapeDtypeStruct((2 * groups, 64, LATE), low),
        normed_one,
        normed_other,
        near,
        swap_cores(away),
        late_gains,
        tall.reshape(groups * TALL, width),
    )
    late, early = lax.optimization_barrier((late, early))
    late = exchange(late, CHIP_CTX)
    parts = whole_call(
        sum_kernel,
        "sum_parts",
        1000,
        jax.ShapeDtypeStruct((8, 64, FF // 4 + LATE), low),
        early,
        late,
        near=True,
    )
    wide, rest = whole_call(
        finish_kernel,
        "finish",
        1000,
        (
            jax.ShapeDtypeStruct((128, PADDED), low),
            jax.ShapeDtypeStruct((4, 128, FF // 4 + 512), low),
        ),
        exchange(parts, CHIPS),
        near=True,
    )
    wide_other = swap_cores(wide)
    rest_other = swap_cores(rest)
    news = update(
        core_at,
        wide,
        wide_other,
        rest,
        rest_other,
        [gains, gains_first, gains_second],
        [
            w_qkv,
            qkv_first,
            qkv_second,
            w_proj,
            proj_first,
            proj_second,
            w_expand,
            expand_first,
            expand_second,
            w_down,
            down_first,
            down_second,
        ],
    )
    return (
        output.T.reshape(batch, local, width),
        input_grad.T.reshape(batch, local, width),
        *news,
    )


def solution(mesh):
    parts = jax.sharding.Mesh(mesh.devices.reshape(2, 4, 2, 2, 4), AXES)
    dp, ctx = ("zh", "y", "core"), CTX
    rows = P(dp, ctx, None)
    owned = P(ctx, None)
    split = P(None, ctx)
    return jax.shard_map(
        on_device,
        mesh=parts,
        in_specs=(rows, rows, P()) + (owned,) * 12 + (split,) * 3,
        out_specs=(rows, rows) + (owned,) * 12 + (split,) * 3,
        check_vma=False,
    )
```

```python
import functools
import math

import jax
import jax.numpy as jnp
from jax import lax
from jax.experimental import pallas as pl
from jax.experimental.pallas import tpu as pltpu
from jax.sharding import PartitionSpec as P

D = 960
HEADS = 15
KV_HEADS = 5
GROUP = HEADS // KV_HEADS
HEAD_DIM = 64
FF = 2560
STEP = 10
HALF = FF // 2
QKVW = D + 2 * KV_HEADS * HEAD_DIM


eps = 1e-05
rope_base = 100000.0
beta_first = 0.9
beta_second = 0.95
adam_eps = 1e-08
masked_score = -1e30
TALL_WIDE = (slice(0, 384), slice(384, 768))
TALL_NARROW = (slice(768, 864), slice(864, 960))
LATE = 1280
SPLIT = 2
LOG2E = math.log2(math.e)
TALL = 56
PADDED = 896
PROJ = 120
NEAR = 896
BESIDE = 768
ATTEND_FLOPS = 20 * 10**9
BACK_FLOPS = 25 * 10**9
FEED_FLOPS = 20 * 10**9
low = jnp.bfloat16


AXES = ("zh", "y", "core", "zl", "x")
CHIPS = ("zh", "y")
CTX = ("zl", "x")
CHIP_CTX = ("zh", "zl", "x")


def swap_cores(value):
    return lax.ppermute(value, "core", [(0, 1), (1, 0)])


def to_peer(value, axis, k):
    count = lax.axis_size(axis)
    return lax.ppermute(value, axis, [(i, i ^ k) for i in range(count)])


def double(piece, axis, k, side):
    bit = lax.axis_index(axis) // k % 2 == 0
    came = to_peer(piece, axis, k)
    return jnp.concatenate(
        [jnp.where(bit, piece, came), jnp.where(bit, came, piece)], axis=side
    )


def add_peer(piece, axis, k):
    return (piece.astype(jnp.float32) + to_peer(piece, axis, k).astype(jnp.float32)).astype(low)


def exchange(stack, axes):
    return lax.all_to_all(stack, axes, 0, 0, tiled=True)


def spread(piece, axes, count):
    return exchange(jnp.broadcast_to(piece[None], (count,) + piece.shape), axes)


def total(stack):
    return jnp.sum(stack.astype(jnp.float32), axis=0).astype(low)


def ordered(core, mine, theirs):
    first = core == 0
    return jnp.where(first, mine, theirs), jnp.where(first, theirs, mine)


def rope_tables(positions):
    halfway = HEAD_DIM // 2
    freqs = rope_base ** (-(jnp.arange(halfway, dtype=jnp.float32) * 2.0) / HEAD_DIM)
    angles = freqs[:, None] * positions.astype(jnp.float32)[None, :]
    return (jnp.cos(angles), jnp.sin(angles))


def rms_scale(rows):
    return lax.rsqrt(jnp.mean(rows * rows, axis=-1, keepdims=True) + eps)


def contract(left, right, left_axis, right_axis):
    return lax.dot_general(
        left,
        right,
        (((left_axis,), (right_axis,)), ((), ())),
        preferred_element_type=jnp.float32,
    )


def in_three(row):
    rows = []
    for _ in range(3):
        part = row.astype(low).astype(jnp.float32)
        rows.append(part)
        row = row - part
    return jnp.concatenate(rows + [jnp.zeros((13, row.shape[1]), jnp.float32)], axis=0).astype(low)


def prepare(order_ref, own_ref, rank_ref, corner_ref, hide_ref):
    slots = order_ref.shape[0]
    span = corner_ref.shape[0] // 2
    ahead = lax.broadcasted_iota(jnp.int32, (span, span), 0) - lax.broadcasted_iota(
        jnp.int32, (span, span), 1
    )
    for s in range(2):
        for t in range(2):
            gap = (own_ref[s] - own_ref[t]) * span
            corner_ref[s * span : (s + 1) * span, t * span : (t + 1) * span] = jnp.where(
                ahead + gap <= 0, 0.0, masked_score
            )
    left = lax.broadcasted_iota(jnp.int32, (1, 2 * span), 1) < span
    rows = [jnp.zeros((2, 2 * span), jnp.float32)]
    for s in range(2, slots):
        at = order_ref[lax.rem(2 * rank_ref[0] + s, slots)]
        one = jnp.where(at > own_ref[0], masked_score, 0.0)
        two = jnp.where(at > own_ref[1], masked_score, 0.0)
        rows.append(jnp.where(left, one, two))
    hide_ref[...] = jnp.concatenate(rows, axis=0).astype(low)


def load_keys(rank_ref, kv_ref, per):
    chunks, _, wide, local = kv_ref.shape
    columns, keys, values = [], [], []
    for c in range(0, chunks, per):
        block = jnp.concatenate(
            [kv_ref[lax.rem(rank_ref[0] + i, chunks), 0] for i in range(c, c + per)], axis=1
        )
        rows = block.T
        lane = lax.broadcasted_iota(jnp.int32, (per * local, wide), 1)
        span = lax.broadcasted_iota(jnp.int32, (per * local, wide), 0) // (local // 2) + 2 * c
        ones = ((lane >= HEAD_DIM) & (lane < HEAD_DIM + 3)) | (lane == HEAD_DIM + 16 + span)
        keys.append(jnp.where(lane < HEAD_DIM, rows, jnp.where(ones, 1.0, 0.0).astype(low)))
        ones = jnp.where(lane < 3, 1.0, 0.0).astype(low)
        values.append(jnp.where(lane >= HEAD_DIM, rows, ones))
        columns.append(block)
    return columns, keys, values


def score(c, keys, query, corner):
    scores = contract(keys[c], query, 1, 0)
    if c == 0:
        local = corner.shape[0]
        scores = jnp.concatenate([scores[:local] + corner, scores[local:]], axis=0)
    return scores


def attend_kernel(
    order_ref, own_ref, rank_ref, q_ref, kv_ref, o_ref, lse_ref, corner_ref, hide_ref
):
    @pl.when(pl.program_id(0) == 0)
    def _():
        prepare(order_ref, own_ref, rank_ref, corner_ref, hide_ref)

    local = q_ref.shape[1]
    columns, keys, _ = load_keys(rank_ref, kv_ref, 2)
    corner = corner_ref[...]
    hide = hide_ref[...]
    blank = jnp.zeros((16, local), low)
    ones = jnp.ones((16, columns[0].shape[1]), low)
    sides = [jnp.concatenate([block[HEAD_DIM:], ones], axis=0) for block in columns]
    for h in range(GROUP):
        part = slice(h * HEAD_DIM, (h + 1) * HEAD_DIM)
        query = jnp.concatenate([q_ref[part, :], blank, hide, blank, blank], axis=0)
        scores = [score(c, keys, query, corner) for c in range(len(keys))]
        top = None
        for block in scores:
            block = jnp.max(block.reshape(-1, 8, local), axis=0)
            top = block if top is None else jnp.maximum(top, block)
        top = jnp.max(top, axis=0, keepdims=True)
        mixed = None
        for c, block in enumerate(scores):
            block = contract(sides[c], jnp.exp2(block - top).astype(low), 1, 0)
            mixed = block if mixed is None else mixed + block
        sums = mixed[HEAD_DIM : HEAD_DIM + 1]
        o_ref[part, :] = (mixed[:HEAD_DIM] / sums).astype(low)
        lse_ref[h] = top + jnp.log2(sums)


def attend_back_kernel(
    order_ref,
    own_ref,
    rank_ref,
    q_ref,
    kv_ref,
    do_ref,
    o_ref,
    lse_ref,
    dq_ref,
    dkv_ref,
    corner_ref,
    hide_ref,
):
    @pl.when(pl.program_id(0) == 0)
    def _():
        prepare(order_ref, own_ref, rank_ref, corner_ref, hide_ref)

    per = 4
    local = q_ref.shape[1]
    chunks = kv_ref.shape[0]
    columns, keys, values = load_keys(rank_ref, kv_ref, per)
    corner = corner_ref[...]
    hide = hide_ref[...]
    blank = jnp.zeros((16, local), low)
    wide_blank = jnp.zeros((HEAD_DIM, local), low)
    terms = [None] * len(keys)
    for h in range(GROUP):
        part = slice(h * HEAD_DIM, (h + 1) * HEAD_DIM)
        query = q_ref[part, :]
        back = do_ref[part, :]
        delta = jnp.sum(
            back.astype(jnp.float32) * o_ref[part, :].astype(jnp.float32), axis=0, keepdims=True
        )
        query_side = jnp.concatenate([query, in_three(-lse_ref[h]), hide, blank, blank], axis=0)
        back_side = jnp.concatenate([in_three(-delta), blank, blank, blank, back], axis=0)
        pair = jnp.concatenate(
            [
                jnp.concatenate([query, wide_blank], axis=0).T,
                jnp.concatenate([wide_blank, back], axis=0).T,
            ],
            axis=0,
        )
        grad_query = None
        for c in range(len(keys)):
            weights = jnp.exp2(score(c, keys, query_side, corner))
            grad = (weights * contract(values[c], back_side, 1, 0)).astype(low)
            term = contract(jnp.concatenate([grad, weights.astype(low)], axis=1), pair, 1, 0)
            terms[c] = term if terms[c] is None else terms[c] + term
            term = contract(columns[c][:HEAD_DIM], grad, 1, 0)
            grad_query = term if grad_query is None else grad_query + term
        dq_ref[part, :] = grad_query * HEAD_DIM ** (-0.5)
    lane = lax.broadcasted_iota(jnp.int32, (1, 2 * HEAD_DIM), 1)
    scale = jnp.where(lane < HEAD_DIM, 1.0 / LOG2E, 1.0)
    for i in range(chunks):
        term = terms[i // per][i % per * local : (i % per + 1) * local]
        dkv_ref[lax.rem(rank_ref[0] + i, chunks), 0] = (term * scale).astype(low)


def attention_specs(chunks, local, start=0):
    wide = GROUP * HEAD_DIM
    heads = pl.BlockSpec((wide, local), lambda g: (g + start, 0))
    keys = pl.BlockSpec((chunks, 1, 2 * HEAD_DIM, local), lambda g: (0, g + start, 0, 0))
    sums = pl.BlockSpec((GROUP, 1, local), lambda g: (g + start, 0, 0))
    return heads, keys, sums


def scalars():
    return pl.BlockSpec(memory_space=pltpu.SMEM)


def attention_scratch(local, slots):
    return [pltpu.VMEM((local, local), jnp.float32), pltpu.VMEM((slots, local), low)]


def attend(order, own, rank, query, keys):
    chunks, _, _, local = keys.shape
    heads, kv, sums = attention_specs(chunks, local)
    return pl.pallas_call(
        attend_kernel,
        grid=(KV_HEADS,),
        out_shape=(
            jax.ShapeDtypeStruct((D, local), low),
            jax.ShapeDtypeStruct((HEADS, 1, local), jnp.float32),
        ),
        in_specs=[scalars(), scalars(), scalars(), heads, kv],
        out_specs=(heads, sums),
        scratch_shapes=attention_scratch(local, order.shape[0]),
        compiler_params=pltpu.CompilerParams(vmem_limit_bytes=60 * 1024 * 1024),
        cost_estimate=pl.CostEstimate(
            flops=ATTEND_FLOPS, bytes_accessed=1000, transcendentals=0
        ),
        name="attend",
    )(order, own, rank, query, keys)


def attend_back(start, count, order, own, rank, query, keys, back, out, lse):
    chunks, _, _, local = keys.shape
    heads, kv, sums = attention_specs(chunks, local, start)
    part, _, _ = attention_specs(chunks, local)
    grads = pl.BlockSpec((chunks, 1, local, 2 * HEAD_DIM), lambda g: (0, g, 0, 0))
    return pl.pallas_call(
        attend_back_kernel,
        grid=(count,),
        out_shape=(
            jax.ShapeDtypeStruct((count * GROUP * HEAD_DIM, local), jnp.float32),
            jax.ShapeDtypeStruct((chunks, count, local, 2 * HEAD_DIM), low),
        ),
        in_specs=[scalars(), scalars(), scalars(), heads, kv, heads, heads, sums],
        out_specs=(part, grads),
        scratch_shapes=attention_scratch(local, order.shape[0]),
        compiler_params=pltpu.CompilerParams(vmem_limit_bytes=60 * 1024 * 1024),
        cost_estimate=pl.CostEstimate(
            flops=BACK_FLOPS * count // KV_HEADS, bytes_accessed=1000, transcendentals=0
        ),
        name=f"attend_back_{start}",
    )(order, own, rank, query, keys, back, out, lse)


def whole_call(kernel, name, flops, out_shape, *operands, near=False):
    single = not isinstance(out_shape, tuple)
    shapes = (out_shape,) if single else out_shape
    far = [] if near else [i for i, value in enumerate(operands) if value.ndim > 1]
    away = [] if near else list(range(len(shapes)))
    space = pl.BlockSpec(memory_space=pltpu.VMEM if near else pltpu.HBM)

    def staged(*refs):
        ins = list(refs[: len(operands)])
        outs = list(refs[len(operands) : len(operands) + len(shapes)])
        scratch = refs[len(operands) + len(shapes) :]
        copies = []
        for k, i in enumerate(far):
            copies.append(pltpu.make_async_copy(ins[i], scratch[k], scratch[-2].at[k]))
            ins[i] = scratch[k]
        for copy in copies:
            copy.start()
        for copy in copies:
            copy.wait()
        held = outs if near else list(scratch[len(far) : len(far) + len(away)])
        kernel(*ins, *held)
        copies = [
            pltpu.make_async_copy(held[k], outs[k], scratch[-1].at[k]) for k in away
        ]
        for copy in copies:
            copy.start()
        for copy in copies:
            copy.wait()

    scratch = [pltpu.VMEM(operands[i].shape, operands[i].dtype) for i in far]
    scratch += [pltpu.VMEM(shapes[k].shape, shapes[k].dtype) for k in away]
    if not near:
        scratch += [pltpu.SemaphoreType.DMA((len(far),)), pltpu.SemaphoreType.DMA((len(away),))]
    outs = pl.pallas_call(
        staged,
        out_shape=shapes,
        in_specs=[scalars() if value.ndim == 1 else space for value in operands],
        out_specs=(space,) * len(shapes),
        scratch_shapes=scratch,
        compiler_params=pltpu.CompilerParams(vmem_limit_bytes=(24 if near else 60) * 1024 * 1024),
        cost_estimate=pl.CostEstimate(flops=flops, bytes_accessed=1000, transcendentals=0),
        name=name,
    )(*operands)
    return outs[0] if single else outs


def stage_kernel(core_ref, qkv_ref, gains_ref, near_ref):
    first = core_ref[0] == 0
    shard = qkv_ref.shape[0]
    gains = jnp.concatenate(
        [gains_ref[...], jnp.zeros((6, gains_ref.shape[1]), jnp.float32)], axis=0
    )
    gains = jnp.concatenate([gains, jnp.zeros((8, 128 - shard), jnp.float32)], axis=1).T
    near = jnp.concatenate(
        [
            jnp.where(first, qkv_ref[:, : QKVW // 2], qkv_ref[:, QKVW // 2 :]),
            gains[:shard, :2],
            jnp.zeros((shard, PADDED - QKVW // 2 - 2), jnp.float32),
        ],
        axis=1,
    ).astype(low)
    for j in range(near_ref.shape[0]):
        near_ref[j] = near


def stage_feed_kernel(place_ref, expand_ref, down_ref, proj_ref, wide_ref, tall_ref):
    first = place_ref[0] == 0
    step = FF // 16
    parts = []
    for k in range(4):
        left = expand_ref[:, 2 * k * step : (2 * k + 1) * step]
        right = expand_ref[:, (2 * k + 1) * step : (2 * k + 2) * step]
        parts.append(jnp.where(first, left, right))
    proj = jnp.where(first, proj_ref[:, : D // 2], proj_ref[:, D // 2 :])
    quarter = proj[:, :PROJ]
    for k in range(1, 4):
        quarter = jnp.where(place_ref[2] == k, proj[:, k * PROJ : (k + 1) * PROJ], quarter)
    blank = jnp.zeros((proj.shape[0], BESIDE - FF // 4 - PROJ), jnp.float32)
    wide = jnp.concatenate(parts + [quarter, blank], axis=1).astype(low)
    tall = down_ref[...].astype(low)
    for j in range(wide_ref.shape[0]):
        wide_ref[j] = wide
        tall_ref[j] = tall


def stage_feed(place, expand, down, proj, groups):
    shard = expand.shape[0]
    half = down.shape[0] // 2
    outs = [(groups, shard, BESIDE), (groups, half, D)]
    return pl.pallas_call(
        stage_feed_kernel,
        grid_spec=pltpu.PrefetchScalarGridSpec(
            num_scalar_prefetch=1,
            grid=(1,),
            in_specs=[
                pl.BlockSpec((shard, HALF), lambda i, place: (0, place[1])),
                pl.BlockSpec((half, D), lambda i, place: (place[0], 0)),
                pl.BlockSpec(proj.shape, lambda i, place: (0, 0)),
            ],
            out_specs=[pl.BlockSpec(out, lambda i, place: (0, 0, 0)) for out in outs],
        ),
        out_shape=[jax.ShapeDtypeStruct(out, low) for out in outs],
        compiler_params=pltpu.CompilerParams(vmem_limit_bytes=60 * 1024 * 1024),
        cost_estimate=pl.CostEstimate(flops=1000, bytes_accessed=8 * 10**6, transcendentals=0),
        name="stage_feed",
    )(place, expand, down, proj)


def rotated(block, cosine, sine):
    first = block[: HEAD_DIM // 2]
    second = block[HEAD_DIM // 2 :]
    return [first * cosine - second * sine, second * cosine + first * sine]


def project_kernel(
    core_ref,
    rows_ref,
    mine_ref,
    theirs_ref,
    cosine_ref,
    sine_ref,
    normed_ref,
    query_ref,
    keys_ref,
    gains_ref,
):
    first_core = core_ref[0] == 0
    cosine = cosine_ref[...]
    sine = sine_ref[...]
    rows = rows_ref[...].astype(jnp.float32).T
    gains = mine_ref[:, PADDED - 128 : PADDED].astype(jnp.float32).T
    at = QKVW // 2 - (PADDED - 128)
    gains_ref[...] = gains[at : at + 2]
    normed = (rows * rms_scale(rows) * gains[at : at + 1]).astype(low)
    normed_ref[...] = normed
    near = contract(normed, mine_ref[...], 1, 0).T
    away = contract(normed, theirs_ref[...], 1, 0).T
    half = QKVW // 2
    one = jnp.where(first_core, near, away)[:half]
    two = jnp.where(first_core, away, near)[:half]
    mixed = jnp.concatenate([one, two], axis=0)
    scale = HEAD_DIM ** (-0.5) * LOG2E
    for h in range(HEADS):
        span = slice(h * HEAD_DIM, (h + 1) * HEAD_DIM)
        turned = jnp.concatenate(rotated(mixed[span], cosine, sine), axis=0)
        query_ref[span] = (turned * scale).astype(low)
    for g in range(KV_HEADS):
        at = D + g * HEAD_DIM
        to = at + KV_HEADS * HEAD_DIM
        pair = rotated(mixed[at : at + HEAD_DIM], cosine, sine) + [mixed[to : to + HEAD_DIM]]
        pair = jnp.concatenate(pair, axis=0).astype(low)
        for j in range(keys_ref.shape[0]):
            keys_ref[j, g] = pair


def join_proj(ref):
    return jnp.concatenate([ref[q, :, :PROJ] for q in range(4)], axis=1)


def rows_kernel(own_ref, other_ref, out_ref):
    out_ref[...] = jnp.concatenate([own_ref[...], other_ref[...]], axis=1).T


def branch_kernel(mixed_ref, beside_ref, out_ref, proj_ref, sem):
    copy = pltpu.make_async_copy(beside_ref.at[:, :, pl.ds(FF // 4, 128)], proj_ref, sem)
    copy.start()
    copy.wait()
    product = contract(mixed_ref[...], join_proj(proj_ref), 1, 0)
    blank = jnp.zeros((product.shape[0], 512 - product.shape[1]), jnp.float32)
    out_ref[...] = jnp.concatenate([product, blank], axis=1).astype(low)


def branch(mixed, beside):
    rows, width = mixed.shape
    whole = pl.BlockSpec(memory_space=pltpu.VMEM)
    return pl.pallas_call(
        branch_kernel,
        out_shape=(
            jax.ShapeDtypeStruct((rows, 512), low),
            jax.ShapeDtypeStruct((4, width, 128), low),
        ),
        in_specs=[whole, pl.BlockSpec(memory_space=pltpu.HBM)],
        out_specs=(whole, whole),
        scratch_shapes=[pltpu.SemaphoreType.DMA(())],
        compiler_params=pltpu.CompilerParams(vmem_limit_bytes=24 * 1024 * 1024),
        cost_estimate=pl.CostEstimate(flops=1000, bytes_accessed=1000, transcendentals=0),
        name="branch",
    )(mixed, beside)


def middle_kernel(
    core_ref,
    near_ref,
    away_ref,
    rows_ref,
    other_ref,
    gains_ref,
    mid_ref,
    normed_ref,
    normed_other,
):
    first_core = core_ref[0] == 0
    local = rows_ref.shape[1]
    for at, rows, out in ((0, rows_ref, normed_ref), (local, other_ref, normed_other)):
        near = near_ref[at : at + local, : D // 2].astype(jnp.float32)
        away = away_ref[local - at : 2 * local - at, : D // 2].astype(jnp.float32)
        near, away = jnp.where(first_core, near, away), jnp.where(first_core, away, near)
        middle = rows[...].astype(jnp.float32).T + jnp.concatenate([near, away], axis=1)
        if at == 0:
            mid_ref[...] = middle
        out[...] = (middle * rms_scale(middle) * gains_ref[1:2]).astype(low)


def turn_kernel(
    core_ref,
    own_ref,
    came_ref,
    mid_ref,
    back_ref,
    gains_ref,
    mine_ref,
    theirs_ref,
    out_ref,
    grad_ref,
    grad_out_ref,
    kept_ref,
    sent_ref,
    gain_grad_ref,
):
    first_core = core_ref[0] == 0
    normed = own_ref[...] + came_ref[...].astype(jnp.float32)
    middle = mid_ref[...]
    inverse = rms_scale(middle)
    scaled = normed * gains_ref[1:2]
    inner = jnp.mean(scaled * middle, axis=-1, keepdims=True)
    grad = back_ref[...].astype(jnp.float32) + inverse * (
        scaled - middle * inverse * inverse * inner
    )
    grad_ref[...] = grad
    gain_grad_ref[...] = jnp.sum(normed * middle * inverse, axis=0, keepdims=True)
    one = grad[:, : D // 2]
    two = grad[:, D // 2 :]
    near = jnp.where(first_core, one, two).astype(low)
    away = jnp.where(first_core, two, one).astype(low)
    grad_out = contract(near, join_proj(mine_ref), 1, 1) + contract(
        away, join_proj(theirs_ref), 1, 1
    )
    grad_out_ref[...] = grad_out.T.astype(low)
    product = contract(out_ref[...], grad.astype(low), 1, 0)
    groups, window, _ = kept_ref.shape
    shard = product.shape[0] // groups
    for j in range(groups):
        top = product[j * shard : j * shard + window]
        bottom = product[(j + 1) * shard - window : (j + 1) * shard]
        kept_ref[j] = jnp.where(first_core, top, bottom).astype(low)
        sent_ref[j] = jnp.where(first_core, bottom, top).astype(low)


def emit_kernel(mid_ref, own_ref, came_ref, out_ref):
    value = mid_ref[...] + own_ref[...] + came_ref[...].astype(jnp.float32)
    out_ref[...] = value.T.astype(low)


def feed_kernel(
    rows_one,
    rows_two,
    back_one,
    back_two,
    expand_ref,
    down_ref,
    fed_ref,
    fed_other_ref,
    normed_ref,
    normed_other_ref,
    tall_ref,
    expand_grad_ref,
    rows_ref,
    back_ref,
    columns_ref,
    fed_sum,
    normed_sum,
):
    local = rows_one.shape[0]
    h = pl.program_id(0)

    @pl.when(h == 0)
    def _():
        rows_ref[:local] = rows_one[...]
        rows_ref[local:] = rows_two[...]
        back_ref[:local] = back_one[...]
        back_ref[local:] = back_two[...]
        columns_ref[...] = rows_ref[...].T

    rows = rows_ref[...]
    back = back_ref[...]
    columns = columns_ref[...]
    down = down_ref[...]
    step = down_ref.shape[0]
    wide = jnp.concatenate([expand_ref[0], expand_ref[1]], axis=1)
    both = contract(rows, wide, 1, 0)
    gate = both[:, :step]
    upward = both[:, step:]
    sigmoid = jax.nn.sigmoid(gate)
    active = gate * sigmoid
    hidden = (active * upward).astype(low)
    grad_hidden = contract(back, down, 1, 1)
    grad_up = (grad_hidden * active).astype(low)
    grad_gate = (grad_hidden * upward * sigmoid * (1.0 + gate * (1.0 - sigmoid))).astype(low)
    fed = contract(hidden, down, 1, 0)
    grad_both = jnp.concatenate([grad_gate, grad_up], axis=1)
    normed = contract(grad_both, wide, 1, 1)
    product = contract(hidden.T, back, 1, 0)
    quarter = FF // 64
    for y in range(4):
        tall_ref[y] = jnp.concatenate(
            [product[(4 * j + y) * quarter : (4 * j + y + 1) * quarter] for j in range(4)], axis=0
        ).astype(low)
    both = contract(columns, grad_both, 1, 0).astype(low)
    expand_grad_ref[0] = both[:, :step]
    expand_grad_ref[1] = both[:, step:]

    @pl.when(h == 0)
    def _():
        fed_sum[...] = fed
        normed_sum[...] = normed

    @pl.when(h == 1)
    def _():
        fed_all = fed_sum[...] + fed
        normed_all = normed_sum[...] + normed
        fed_ref[...] = fed_all[:local]
        fed_other_ref[...] = fed_all[local:].astype(low)
        normed_ref[...] = normed_all[:local]
        normed_other_ref[...] = normed_all[local:].astype(low)


def feed(rows, back, expand, down):
    local, width = rows[0].shape
    step = FF // 4
    held = pl.BlockSpec((local, width), lambda h: (0, 0))
    pair = pl.BlockSpec((2, width, step), lambda h: (h, 0, 0))
    tall = pl.BlockSpec((step, width), lambda h: (h, 0))
    rows_out = pl.BlockSpec((4, FF // 16, width), lambda h: (0, h, 0))
    own = jax.ShapeDtypeStruct((local, width), jnp.float32)
    other = jax.ShapeDtypeStruct((local, width), low)
    return pl.pallas_call(
        feed_kernel,
        grid=(2,),
        out_shape=(
            own,
            other,
            own,
            other,
            jax.ShapeDtypeStruct((4, 8 * TALL, width), low),
            jax.ShapeDtypeStruct((4, width, step), low),
        ),
        in_specs=[held] * 4 + [pair, tall],
        out_specs=(held,) * 4 + (rows_out, pair),
        scratch_shapes=[
            pltpu.VMEM((2 * local, width), low),
            pltpu.VMEM((2 * local, width), low),
            pltpu.VMEM((width, 2 * local), low),
            pltpu.VMEM((2 * local, width), jnp.float32),
            pltpu.VMEM((2 * local, width), jnp.float32),
        ],
        compiler_params=pltpu.CompilerParams(vmem_limit_bytes=60 * 1024 * 1024),
        cost_estimate=pl.CostEstimate(flops=FEED_FLOPS, bytes_accessed=1000, transcendentals=0),
        name="feed",
    )(*rows, *back, expand, down)


def stack_kernel(tall_in, kept_ref, came_ref, tall_ref, held, sem):
    proj = (kept_ref[...].astype(jnp.float32) + came_ref[...].astype(jnp.float32)).astype(low)
    rows = proj.shape[1] // 4
    for y in range(4):
        held[y] = jnp.concatenate(
            [proj[j, y * rows : (y + 1) * rows] for j in range(proj.shape[0])], axis=0
        )
    span = pl.ds(tall_ref.shape[1] - held.shape[1], held.shape[1])
    copy = pltpu.make_async_copy(held, tall_ref.at[:, span], sem)
    copy.start()
    copy.wait()


def stack(tall, kept, came):
    groups, window, width = kept.shape
    away = pl.BlockSpec(memory_space=pltpu.HBM)
    whole = pl.BlockSpec(memory_space=pltpu.VMEM)
    return pl.pallas_call(
        stack_kernel,
        out_shape=jax.ShapeDtypeStruct(tall.shape, low),
        in_specs=[away, whole, whole],
        out_specs=away,
        scratch_shapes=[
            pltpu.VMEM((4, groups * window // 4, width), low),
            pltpu.SemaphoreType.DMA(()),
        ],
        input_output_aliases={0: 0},
        compiler_params=pltpu.CompilerParams(vmem_limit_bytes=60 * 1024 * 1024),
        cost_estimate=pl.CostEstimate(flops=1000, bytes_accessed=1000, transcendentals=0),
        name="stack",
    )(tall, kept, came)


def adam_step(master, first, second, grad, rate, decay):
    new_first = beta_first * first + (1.0 - beta_first) * grad
    new_second = beta_second * second + (1.0 - beta_second) * grad * grad
    fix_one = 1.0 - beta_first**STEP
    fix_two = 1.0 - beta_second**STEP
    update = new_first / fix_one / (jnp.sqrt(new_second / fix_two) + adam_eps) + decay * master
    return (master - rate * update, new_first, new_second)


def update_kernel(
    core_ref,
    wide_ref,
    wide_other,
    rest_ref,
    rest_other,
    gains_ref,
    gains_first,
    gains_second,
    *refs,
):
    states, outs, gain_outs = refs[:12], refs[12:24], refs[24:27]
    held = refs[27:31]
    near = refs[31:35]
    load_sem, store_sem, near_sem = refs[35:]
    grads = (wide_ref, wide_other, rest_ref, rest_other)
    fetches = [pltpu.make_async_copy(grads[k], near[k], near_sem.at[k]) for k in range(4)]
    wide_ref, wide_other, rest_ref, rest_other = near
    first_core = core_ref[0] == 0
    shard = gains_ref.shape[1]
    quarter = held[3].shape[1] // 8

    def both(mine, theirs):
        return (
            jnp.where(first_core, mine, theirs).astype(jnp.float32),
            jnp.where(first_core, theirs, mine).astype(jnp.float32),
        )

    def expand_grad(q):
        step = FF // 16
        one, two = both(rest_ref[q, :, : FF // 4], rest_other[q, :, : FF // 4])
        one, two = one[:shard], two[:shard]
        parts = []
        for k in range(4):
            span = slice(k * step, (k + 1) * step)
            parts += [one[:, span], two[:, span]]
        return jnp.concatenate(parts, axis=1)

    def tall_grads():
        parts = [both(rest_ref[q], rest_other[q]) for q in range(4)]
        one = [tall_part(part[0]) for part in parts]
        two = [tall_part(part[1]) for part in parts]
        down = jnp.concatenate([part[:quarter] for part in one + two], axis=0)
        proj = jnp.concatenate(
            [part[TALL - 16 :] for part in one]
            + [two[0][TALL - 8 :]]
            + [part[TALL - 16 :] for part in two[1:]],
            axis=0,
        )
        return down, proj

    def wide_grad():
        one, two = both(wide_ref[...], wide_other[...])
        half = QKVW // 2
        return jnp.concatenate([one[:shard, :half], two[:shard, :half]], axis=1)

    full = slice(None)
    pieces = [(2, pl.ds(i * HALF, HALF), 2.0 * D ** (-0.5)) for i in range(4)]
    pieces += [
        (3, full, 2.0 * FF ** (-0.5)),
        (1, full, 2.0 * (D // 8) ** (-0.5)),
        (0, full, 2.0 * D ** (-0.5)),
    ]

    def copies(p, out):
        weight, columns, _ = pieces[p]
        for k in range(3):
            near = held[weight].at[k, :, columns]
            if out:
                yield pltpu.make_async_copy(
                    near, outs[3 * weight + k].at[:, columns], store_sem.at[p, k]
                )
            else:
                yield pltpu.make_async_copy(
                    states[3 * weight + k].at[:, columns], near, load_sem.at[p, k]
                )

    for copy in fetches:
        copy.start()
    for p in range(len(pieces)):
        for copy in copies(p, False):
            copy.start()
    for copy in fetches:
        copy.wait()
    down, proj = tall_grads()
    for p, (weight, columns, rate) in enumerate(pieces):
        for copy in copies(p, False):
            copy.wait()
        if p < 4:
            grad = expand_grad(p % 2 * 2 + p // 2)
        else:
            grad = (down, proj)[p - 4] if p < 6 else wide_grad()
        new = adam_step(*[held[weight][k, :, columns] for k in range(3)], grad, rate, 0.1)
        for k in range(3):
            held[weight][k, :, columns] = new[k]
        for copy in copies(p, True):
            copy.start()
    one, two = both(wide_ref[...], wide_other[...])
    grad = one[shard : shard + 2, :shard] + two[shard : shard + 2, :shard]
    new = adam_step(gains_ref[...], gains_first[...], gains_second[...], grad, 1.0, 0.0)
    for out, value in zip(gain_outs, new):
        out[...] = value
    for p in range(len(pieces)):
        for copy in copies(p, True):
            copy.wait()


def update(core, wide, wide_other, rest, rest_other, gains, states):
    whole = pl.BlockSpec(memory_space=pltpu.VMEM)
    away = pl.BlockSpec(memory_space=pltpu.HBM)
    shapes = [jax.ShapeDtypeStruct(value.shape, jnp.float32) for value in states + gains]
    return pl.pallas_call(
        update_kernel,
        out_shape=shapes,
        in_specs=[scalars()] + [away] * 4 + [whole] * 3 + [away] * 12,
        out_specs=[away] * 12 + [whole] * 3,
        scratch_shapes=[
            pltpu.VMEM((3,) + states[3 * weight].shape, jnp.float32) for weight in range(4)
        ]
        + [pltpu.VMEM(value.shape, low) for value in (wide, wide, rest, rest)]
        + [pltpu.SemaphoreType.DMA(shape) for shape in ((7, 3), (7, 3), (4,))],
        compiler_params=pltpu.CompilerParams(vmem_limit_bytes=32 * 1024 * 1024),
        cost_estimate=pl.CostEstimate(
            flops=1000, bytes_accessed=30 * 10**6, transcendentals=0
        ),
        name="update",
    )(core, wide, wide_other, rest, rest_other, *gains, *states)


def back_rotated(block, cosine, sine):
    first = block[: HEAD_DIM // 2]
    second = block[HEAD_DIM // 2 :]
    return [first * cosine + second * sine, second * cosine - first * sine]


def late_kernel(
    core_ref,
    first_terms,
    second_terms,
    first_dq,
    second_dq,
    cosine_ref,
    sine_ref,
    mine_ref,
    theirs_ref,
    rows_ref,
    grad_ref,
    gain_ref,
    gain_grad_ref,
    out_ref,
    near_ref,
    away_ref,
    gains_ref,
):
    cosine = cosine_ref[...]
    sine = sine_ref[...]
    first_core = core_ref[0] == 0
    parts = []
    for ref in (first_dq, second_dq):
        for h in range(ref.shape[0] // HEAD_DIM):
            parts += back_rotated(ref[h * HEAD_DIM : (h + 1) * HEAD_DIM], cosine, sine)
    values = []
    for ref in (first_terms, second_terms):
        for g in range(ref.shape[1]):
            block = ref[0, g].astype(jnp.float32)
            for j in range(1, ref.shape[0]):
                block = block + ref[j, g].astype(jnp.float32)
            block = block.T
            parts += back_rotated(block[:HEAD_DIM], cosine, sine)
            values.append(block[HEAD_DIM:])
    mixed = jnp.concatenate(parts + values, axis=0)
    half = QKVW // 2
    blank = jnp.zeros((PADDED - half, mixed.shape[1]), jnp.float32)
    one = mixed[:half]
    two = mixed[half:]
    near = jnp.concatenate([jnp.where(first_core, one, two), blank], axis=0).T.astype(low)
    away = jnp.concatenate([jnp.where(first_core, two, one), blank], axis=0).T.astype(low)
    grad_normed = contract(near, mine_ref[...], 1, 1) + contract(away, theirs_ref[...], 1, 1)
    rows = rows_ref[...].astype(jnp.float32).T
    inverse = rms_scale(rows)
    scaled = grad_normed * gain_ref[0:1]
    inner = jnp.mean(scaled * rows, axis=-1, keepdims=True)
    back = inverse * (scaled - rows * inverse * inverse * inner)
    out_ref[...] = (grad_ref[...] + back).T.astype(low)
    gain_one = jnp.sum(grad_normed * rows * inverse, axis=0, keepdims=True)
    gains = (gain_one, gain_grad_ref[...])
    near_ref[...] = near
    away_ref[...] = away
    gains_ref[...] = jnp.concatenate(gains, axis=0)


def weight_kernel(
    normed_ref, normed_other, near_ref, came_ref, gains_ref, tall_ref, out_ref
):
    columns = jnp.concatenate([normed_ref[...], normed_other[...]], axis=0).T
    product = contract(columns, jnp.concatenate([near_ref[...], came_ref[...]], axis=0), 1, 0)
    groups = out_ref.shape[0] // 2
    shard = product.shape[0] // groups
    lanes = product.shape[1]
    gains = gains_ref[...]
    quarter = FF // 64
    down = tall_ref[: groups * quarter].astype(jnp.float32)
    proj = tall_ref[groups * quarter :].astype(jnp.float32)
    for j in range(groups):
        span = slice(j * shard, (j + 1) * shard)
        tail = padded_rows(gains[:, span], 128 - shard)
        tail = jnp.concatenate(
            [tail, jnp.zeros((128 - shard, lanes - shard), jnp.float32)], axis=1
        )
        summed = jnp.concatenate([product[span], tail], axis=0)
        tall = jnp.concatenate(
            [down[j * quarter : (j + 1) * quarter], proj[j * 16 : (j + 1) * 16]], axis=0
        )
        halves = [
            jnp.concatenate([padded_rows(tall[:, span], 64) for span in spans], axis=0)
            for spans in (TALL_NARROW, TALL_WIDE)
        ]
        put_halves(out_ref, j, jnp.concatenate([summed[:, : QKVW // 2]] + halves, axis=1))


def padded_rows(block, rows):
    return jnp.concatenate(
        [block, jnp.zeros((rows - block.shape[0], block.shape[1]), jnp.float32)], axis=0
    )


def put_halves(out_ref, j, block):
    groups = out_ref.shape[0] // 2
    rows = out_ref.shape[1]
    for half in range(2):
        out_ref[half * groups + j] = block[half * rows : (half + 1) * rows].astype(low)


def pack_early_kernel(expand_ref, out_ref):
    for j in range(expand_ref.shape[0]):
        put_halves(out_ref, j, padded_rows(expand_ref[j].astype(jnp.float32), 128))


def sum_kernel(early_ref, late_ref, out_ref):
    sums = []
    for ref in (early_ref, late_ref):
        block = ref[0].astype(jnp.float32)
        for j in range(1, ref.shape[0]):
            block = block + ref[j].astype(jnp.float32)
        sums.append(block.astype(low))
    block = jnp.concatenate(sums, axis=1)
    for j in range(out_ref.shape[0]):
        out_ref[j] = block


def finish_kernel(all_ref, wide_ref, rest_ref):
    count = all_ref.shape[0] // 2
    rows = all_ref.shape[1]
    expand = slice(0, FF // 4)
    wide = slice(FF // 4, FF // 4 + PADDED)
    tall = slice(FF // 4 + LATE - 512, FF // 4 + LATE)
    for half in range(2):
        span = slice(half * rows, (half + 1) * rows)
        block = all_ref[half * count, :, wide].astype(jnp.float32)
        for y in range(1, count):
            block = block + all_ref[half * count + y, :, wide].astype(jnp.float32)
        wide_ref[span] = block.astype(low)
        for y in range(count):
            rest_ref[y, span] = jnp.concatenate(
                [all_ref[half * count + y, :, lanes] for lanes in (expand, tall)], axis=1
            )


def tall_part(rest):
    parts = []
    for lanes in (slice(FF // 4 + 128, FF // 4 + 512), slice(FF // 4 + 32, FF // 4 + 128)):
        parts += [rest[at : at + TALL, lanes] for at in (0, rest.shape[0] // 2)]
    return jnp.concatenate(parts, axis=1)


def on_device(
    inputs,
    cotangent,
    span_order,
    w_qkv,
    qkv_first,
    qkv_second,
    w_proj,
    proj_first,
    proj_second,
    w_expand,
    expand_first,
    expand_second,
    w_down,
    down_first,
    down_second,
    gains,
    gains_first,
    gains_second,
):
    core = lax.axis_index("core")
    rank = lax.axis_index(CTX)
    groups = 8
    batch, local, width = inputs.shape
    shard = w_qkv.shape[0]
    hidden_shard = w_down.shape[0] // 2

    y = lax.axis_index("y")
    place = jnp.stack([core, y % 2 * 2 + y // 2, y]).astype(jnp.int32)
    core_at = place[:1]
    rank_at = rank.reshape(1).astype(jnp.int32)
    near = whole_call(
        stage_kernel,
        "stage",
        1000,
        jax.ShapeDtypeStruct((groups, shard, NEAR), low),
        core_at,
        w_qkv,
        gains,
    )
    mine = exchange(near, CTX).reshape(width, NEAR)
    expand_low, down_low = stage_feed(place, w_expand, w_down, w_proj, groups)
    back_rows = cotangent.reshape(local, width)
    order_own = lax.dynamic_slice_in_dim(span_order, 2 * rank, 2)
    own_pos = (
        order_own[:, None] * (local // 2) + jnp.arange(local // 2, dtype=jnp.int32)
    ).reshape(local)
    cosine, sine = rope_tables(own_pos)
    mine, cosine, sine, expand_low, down_low, back_rows = lax.optimization_barrier(
        (mine, cosine, sine, expand_low, down_low, back_rows)
    )
    theirs = swap_cores(mine)
    expand_low = exchange(expand_low, CTX).reshape(width, BESIDE)

    tokens = inputs.reshape(local, width).T
    square = (local, width)
    normed_one, query, all_keys, full_gains = whole_call(
        project_kernel,
        "project",
        1000,
        (
            jax.ShapeDtypeStruct(square, low),
            jax.ShapeDtypeStruct((width, local), low),
            jax.ShapeDtypeStruct((groups, KV_HEADS, 2 * HEAD_DIM, local), low),
            jax.ShapeDtypeStruct((2, width), jnp.float32),
        ),
        core_at,
        tokens,
        mine,
        theirs,
        cosine,
        sine,
    )
    all_keys, expand_low = lax.optimization_barrier((all_keys, expand_low))
    expand_low = lax.all_gather(expand_low, "y", axis=0, tiled=False)
    all_keys = exchange(all_keys, CTX)
    all_keys, down_low = lax.optimization_barrier((all_keys, down_low))
    normed_other = swap_cores(normed_one)
    tokens_other = swap_cores(tokens)
    half_down = exchange(down_low, CTX).reshape(HALF, width)
    attended, lse = attend(span_order, order_own, rank_at, query, all_keys)
    mixed = whole_call(
        rows_kernel,
        "rows",
        1000,
        jax.ShapeDtypeStruct((2 * local, width), low),
        attended,
        swap_cores(attended),
        near=True,
    )
    mixed, expand_low = lax.optimization_barrier((mixed, expand_low))
    mixed, proj_mine = branch(mixed, expand_low)
    middle, normed_two, normed_two_other = whole_call(
        middle_kernel,
        "middle",
        1000,
        (
            jax.ShapeDtypeStruct(square, jnp.float32),
            jax.ShapeDtypeStruct(square, low),
            jax.ShapeDtypeStruct(square, low),
        ),
        core_at,
        mixed,
        swap_cores(mixed),
        tokens,
        tokens_other,
        full_gains,
    )
    proj_theirs = swap_cores(proj_mine)
    normed_two, half_down = lax.optimization_barrier((normed_two, half_down))

    fed, fed_other, grad_normed, grad_other, tall, grad_expand = feed(
        (normed_two, normed_two_other),
        (back_rows, swap_cores(back_rows)),
        expand_low,
        half_down,
    )
    grad_middle, grad_att, proj_kept, proj_sent, gain_grad_two = whole_call(
        turn_kernel,
        "turn",
        3 * 10**9,
        (
            jax.ShapeDtypeStruct(square, jnp.float32),
            jax.ShapeDtypeStruct((width, local), low),
            jax.ShapeDtypeStruct((groups, 64, width), low),
            jax.ShapeDtypeStruct((groups, 64, width), low),
            jax.ShapeDtypeStruct((1, width), jnp.float32),
        ),
        core_at,
        grad_normed,
        swap_cores(grad_other),
        middle,
        back_rows,
        full_gains,
        proj_mine,
        proj_theirs,
        attended,
    )
    output = whole_call(
        emit_kernel,
        "emit",
        1000,
        jax.ShapeDtypeStruct((width, local), low),
        middle,
        fed,
        swap_cores(fed_other),
    )

    expand_sum = lax.psum_scatter(grad_expand, "y", scatter_dimension=0, tiled=False)
    context = (span_order, order_own, rank_at, query, all_keys, grad_att, attended, lse)
    first_query, first_terms = attend_back(0, SPLIT, *context)
    first_terms, tall = lax.optimization_barrier((first_terms, tall))
    first_terms = exchange(first_terms, CTX)
    grad_query, key_terms = attend_back(SPLIT, KV_HEADS - SPLIT, *context)
    key_terms = exchange(key_terms, CTX)
    early = whole_call(
        pack_early_kernel,
        "pack_early",
        1000,
        jax.ShapeDtypeStruct((2 * groups, 64, FF // 4), low),
        expand_sum.reshape(groups, shard, FF // 4),
    )
    key_terms, first_terms, output, early = lax.optimization_barrier(
        (key_terms, first_terms, output, early)
    )
    early = exchange(early, CHIP_CTX)
    tall = stack(tall, proj_kept, swap_cores(proj_sent))
    tall = lax.psum_scatter(tall, "y", scatter_dimension=0, tiled=False)
    half = jax.ShapeDtypeStruct((local, PADDED), low)
    input_grad, near, away, late_gains = whole_call(
        late_kernel,
        "late",
        30 * 10**9,
        (
            jax.ShapeDtypeStruct((width, local), low),
            half,
            half,
            jax.ShapeDtypeStruct((2, width), jnp.float32),
        ),
        core_at,
        first_terms,
        key_terms,
        first_query,
        grad_query,
        cosine,
        sine,
        mine,
        theirs,
        tokens,
        grad_middle,
        full_gains,
        gain_grad_two,
    )
    late = whole_call(
        weight_kernel,
        "weight",
        1000,
        jax.ShapeDtypeStruct((2 * groups, 64, LATE), low),
        normed_one,
        normed_other,
        near,
        swap_cores(away),
        late_gains,
        tall.reshape(groups * TALL, width),
    )
    late, early = lax.optimization_barrier((late, early))
    late = exchange(late, CHIP_CTX)
    parts = whole_call(
        sum_kernel,
        "sum_parts",
        1000,
        jax.ShapeDtypeStruct((8, 64, FF // 4 + LATE), low),
        early,
        late,
        near=True,
    )
    wide, rest = whole_call(
        finish_kernel,
        "finish",
        1000,
        (
            jax.ShapeDtypeStruct((128, PADDED), low),
            jax.ShapeDtypeStruct((4, 128, FF // 4 + 512), low),
        ),
        exchange(parts, CHIPS),
        near=True,
    )
    wide_other = swap_cores(wide)
    rest_other = swap_cores(rest)
    news = update(
        core_at,
        wide,
        wide_other,
        rest,
        rest_other,
        [gains, gains_first, gains_second],
        [
            w_qkv,
            qkv_first,
            qkv_second,
            w_proj,
            proj_first,
            proj_second,
            w_expand,
            expand_first,
            expand_second,
            w_down,
            down_first,
            down_second,
        ],
    )
    return (
        output.T.reshape(batch, local, width),
        input_grad.T.reshape(batch, local, width),
        *news,
    )


def solution(mesh):
    parts = jax.sharding.Mesh(mesh.devices.reshape(2, 4, 2, 2, 4), AXES)
    dp, ctx = ("zh", "y", "core"), CTX
    rows = P(dp, ctx, None)
    owned = P(ctx, None)
    split = P(None, ctx)
    return jax.shard_map(
        on_device,
        mesh=parts,
        in_specs=(rows, rows, P()) + (owned,) * 12 + (split,) * 3,
        out_specs=(rows, rows) + (owned,) * 12 + (split,) * 3,
        check_vma=False,
    )
```

```python
import functools
import math

import jax
import jax.numpy as jnp
from jax import lax
from jax.experimental import pallas as pl
from jax.experimental.pallas import tpu as pltpu
from jax.sharding import PartitionSpec as P

D = 960
HEADS = 15
KV_HEADS = 5
GROUP = HEADS // KV_HEADS
HEAD_DIM = 64
FF = 2560
STEP = 10
HALF = FF // 2
QKVW = D + 2 * KV_HEADS * HEAD_DIM


eps = 1e-05
rope_base = 100000.0
beta_first = 0.9
beta_second = 0.95
adam_eps = 1e-08
masked_score = -1e30
TALL_WIDE = (slice(0, 384), slice(384, 768))
TALL_NARROW = (slice(768, 864), slice(864, 960))
LATE = 1280
SPLIT = 2
LOG2E = math.log2(math.e)
TALL = 56
PADDED = 896
PROJ = 120
NEAR = 896
BESIDE = 768
ATTEND_FLOPS = 20 * 10**9
BACK_FLOPS = 25 * 10**9
FEED_FLOPS = 20 * 10**9
low = jnp.bfloat16


AXES = ("zh", "y", "core", "zl", "x")
CHIPS = ("zh", "y")
CTX = ("zl", "x")
CHIP_CTX = ("zh", "zl", "x")


def swap_cores(value):
    return lax.ppermute(value, "core", [(0, 1), (1, 0)])


def to_peer(value, axis, k):
    count = lax.axis_size(axis)
    return lax.ppermute(value, axis, [(i, i ^ k) for i in range(count)])


def double(piece, axis, k, side):
    bit = lax.axis_index(axis) // k % 2 == 0
    came = to_peer(piece, axis, k)
    return jnp.concatenate(
        [jnp.where(bit, piece, came), jnp.where(bit, came, piece)], axis=side
    )


def add_peer(piece, axis, k):
    return (piece.astype(jnp.float32) + to_peer(piece, axis, k).astype(jnp.float32)).astype(low)


def exchange(stack, axes):
    return lax.all_to_all(stack, axes, 0, 0, tiled=True)


def spread(piece, axes, count):
    return exchange(jnp.broadcast_to(piece[None], (count,) + piece.shape), axes)


def total(stack):
    return jnp.sum(stack.astype(jnp.float32), axis=0).astype(low)


def ordered(core, mine, theirs):
    first = core == 0
    return jnp.where(first, mine, theirs), jnp.where(first, theirs, mine)


def rope_tables(positions):
    halfway = HEAD_DIM // 2
    freqs = rope_base ** (-(jnp.arange(halfway, dtype=jnp.float32) * 2.0) / HEAD_DIM)
    angles = freqs[:, None] * positions.astype(jnp.float32)[None, :]
    return (jnp.cos(angles), jnp.sin(angles))


def rms_scale(rows):
    return lax.rsqrt(jnp.mean(rows * rows, axis=-1, keepdims=True) + eps)


def contract(left, right, left_axis, right_axis):
    return lax.dot_general(
        left,
        right,
        (((left_axis,), (right_axis,)), ((), ())),
        preferred_element_type=jnp.float32,
    )


def in_three(row):
    rows = []
    for _ in range(3):
        part = row.astype(low).astype(jnp.float32)
        rows.append(part)
        row = row - part
    return jnp.concatenate(rows + [jnp.zeros((13, row.shape[1]), jnp.float32)], axis=0).astype(low)


def prepare(order_ref, own_ref, rank_ref, corner_ref, hide_ref):
    slots = order_ref.shape[0]
    span = corner_ref.shape[0] // 2
    ahead = lax.broadcasted_iota(jnp.int32, (span, span), 0) - lax.broadcasted_iota(
        jnp.int32, (span, span), 1
    )
    for s in range(2):
        for t in range(2):
            gap = (own_ref[s] - own_ref[t]) * span
            corner_ref[s * span : (s + 1) * span, t * span : (t + 1) * span] = jnp.where(
                ahead + gap <= 0, 0.0, masked_score
            )
    left = lax.broadcasted_iota(jnp.int32, (1, 2 * span), 1) < span
    rows = [jnp.zeros((2, 2 * span), jnp.float32)]
    for s in range(2, slots):
        at = order_ref[lax.rem(2 * rank_ref[0] + s, slots)]
        one = jnp.where(at > own_ref[0], masked_score, 0.0)
        two = jnp.where(at > own_ref[1], masked_score, 0.0)
        rows.append(jnp.where(left, one, two))
    hide_ref[...] = jnp.concatenate(rows, axis=0).astype(low)


def load_keys(rank_ref, kv_ref, per):
    chunks, _, wide, local = kv_ref.shape
    columns, keys, values = [], [], []
    for c in range(0, chunks, per):
        block = jnp.concatenate(
            [kv_ref[lax.rem(rank_ref[0] + i, chunks), 0] for i in range(c, c + per)], axis=1
        )
        rows = block.T
        lane = lax.broadcasted_iota(jnp.int32, (per * local, wide), 1)
        span = lax.broadcasted_iota(jnp.int32, (per * local, wide), 0) // (local // 2) + 2 * c
        ones = ((lane >= HEAD_DIM) & (lane < HEAD_DIM + 3)) | (lane == HEAD_DIM + 16 + span)
        keys.append(jnp.where(lane < HEAD_DIM, rows, jnp.where(ones, 1.0, 0.0).astype(low)))
        ones = jnp.where(lane < 3, 1.0, 0.0).astype(low)
        values.append(jnp.where(lane >= HEAD_DIM, rows, ones))
        columns.append(block)
    return columns, keys, values


def score(c, keys, query, corner):
    scores = contract(keys[c], query, 1, 0)
    if c == 0:
        local = corner.shape[0]
        scores = jnp.concatenate([scores[:local] + corner, scores[local:]], axis=0)
    return scores


def attend_kernel(
    order_ref, own_ref, rank_ref, q_ref, kv_ref, o_ref, lse_ref, corner_ref, hide_ref
):
    @pl.when(pl.program_id(0) == 0)
    def _():
        prepare(order_ref, own_ref, rank_ref, corner_ref, hide_ref)

    local = q_ref.shape[1]
    columns, keys, _ = load_keys(rank_ref, kv_ref, 2)
    corner = corner_ref[...]
    hide = hide_ref[...]
    blank = jnp.zeros((16, local), low)
    ones = jnp.ones((16, columns[0].shape[1]), low)
    sides = [jnp.concatenate([block[HEAD_DIM:], ones], axis=0) for block in columns]
    for h in range(GROUP):
        part = slice(h * HEAD_DIM, (h + 1) * HEAD_DIM)
        query = jnp.concatenate([q_ref[part, :], blank, hide, blank, blank], axis=0)
        scores = [score(c, keys, query, corner) for c in range(len(keys))]
        top = None
        for block in scores:
            block = jnp.max(block.reshape(-1, 8, local), axis=0)
            top = block if top is None else jnp.maximum(top, block)
        top = jnp.max(top, axis=0, keepdims=True)
        mixed = None
        for c, block in enumerate(scores):
            block = contract(sides[c], jnp.exp2(block - top).astype(low), 1, 0)
            mixed = block if mixed is None else mixed + block
        sums = mixed[HEAD_DIM : HEAD_DIM + 1]
        o_ref[part, :] = (mixed[:HEAD_DIM] / sums).astype(low)
        lse_ref[h] = top + jnp.log2(sums)


def attend_back_kernel(
    order_ref,
    own_ref,
    rank_ref,
    q_ref,
    kv_ref,
    do_ref,
    o_ref,
    lse_ref,
    dq_ref,
    dkv_ref,
    corner_ref,
    hide_ref,
):
    @pl.when(pl.program_id(0) == 0)
    def _():
        prepare(order_ref, own_ref, rank_ref, corner_ref, hide_ref)

    per = 4
    local = q_ref.shape[1]
    chunks = kv_ref.shape[0]
    columns, keys, values = load_keys(rank_ref, kv_ref, per)
    corner = corner_ref[...]
    hide = hide_ref[...]
    blank = jnp.zeros((16, local), low)
    wide_blank = jnp.zeros((HEAD_DIM, local), low)
    terms = [None] * len(keys)
    for h in range(GROUP):
        part = slice(h * HEAD_DIM, (h + 1) * HEAD_DIM)
        query = q_ref[part, :]
        back = do_ref[part, :]
        delta = jnp.sum(
            back.astype(jnp.float32) * o_ref[part, :].astype(jnp.float32), axis=0, keepdims=True
        )
        query_side = jnp.concatenate([query, in_three(-lse_ref[h]), hide, blank, blank], axis=0)
        back_side = jnp.concatenate([in_three(-delta), blank, blank, blank, back], axis=0)
        pair = jnp.concatenate(
            [
                jnp.concatenate([query, wide_blank], axis=0).T,
                jnp.concatenate([wide_blank, back], axis=0).T,
            ],
            axis=0,
        )
        grad_query = None
        for c in range(len(keys)):
            weights = jnp.exp2(score(c, keys, query_side, corner))
            grad = (weights * contract(values[c], back_side, 1, 0)).astype(low)
            term = contract(jnp.concatenate([grad, weights.astype(low)], axis=1), pair, 1, 0)
            terms[c] = term if terms[c] is None else terms[c] + term
            term = contract(columns[c][:HEAD_DIM], grad, 1, 0)
            grad_query = term if grad_query is None else grad_query + term
        dq_ref[part, :] = grad_query * HEAD_DIM ** (-0.5)
    lane = lax.broadcasted_iota(jnp.int32, (1, 2 * HEAD_DIM), 1)
    scale = jnp.where(lane < HEAD_DIM, 1.0 / LOG2E, 1.0)
    for i in range(chunks):
        term = terms[i // per][i % per * local : (i % per + 1) * local]
        dkv_ref[lax.rem(rank_ref[0] + i, chunks), 0] = (term * scale).astype(low)


def attention_specs(chunks, local, start=0):
    wide = GROUP * HEAD_DIM
    heads = pl.BlockSpec((wide, local), lambda g: (g + start, 0))
    keys = pl.BlockSpec((chunks, 1, 2 * HEAD_DIM, local), lambda g: (0, g + start, 0, 0))
    sums = pl.BlockSpec((GROUP, 1, local), lambda g: (g + start, 0, 0))
    return heads, keys, sums


def scalars():
    return pl.BlockSpec(memory_space=pltpu.SMEM)


def attention_scratch(local, slots):
    return [pltpu.VMEM((local, local), jnp.float32), pltpu.VMEM((slots, local), low)]


def attend(order, own, rank, query, keys):
    chunks, _, _, local = keys.shape
    heads, kv, sums = attention_specs(chunks, local)
    return pl.pallas_call(
        attend_kernel,
        grid=(KV_HEADS,),
        out_shape=(
            jax.ShapeDtypeStruct((D, local), low),
            jax.ShapeDtypeStruct((HEADS, 1, local), jnp.float32),
        ),
        in_specs=[scalars(), scalars(), scalars(), heads, kv],
        out_specs=(heads, sums),
        scratch_shapes=attention_scratch(local, order.shape[0]),
        compiler_params=pltpu.CompilerParams(vmem_limit_bytes=60 * 1024 * 1024),
        cost_estimate=pl.CostEstimate(
            flops=ATTEND_FLOPS, bytes_accessed=1000, transcendentals=0
        ),
        name="attend",
    )(order, own, rank, query, keys)


def attend_back(start, count, order, own, rank, query, keys, back, out, lse):
    chunks, _, _, local = keys.shape
    heads, kv, sums = attention_specs(chunks, local, start)
    part, _, _ = attention_specs(chunks, local)
    grads = pl.BlockSpec((chunks, 1, local, 2 * HEAD_DIM), lambda g: (0, g, 0, 0))
    return pl.pallas_call(
        attend_back_kernel,
        grid=(count,),
        out_shape=(
            jax.ShapeDtypeStruct((count * GROUP * HEAD_DIM, local), jnp.float32),
            jax.ShapeDtypeStruct((chunks, count, local, 2 * HEAD_DIM), low),
        ),
        in_specs=[scalars(), scalars(), scalars(), heads, kv, heads, heads, sums],
        out_specs=(part, grads),
        scratch_shapes=attention_scratch(local, order.shape[0]),
        compiler_params=pltpu.CompilerParams(vmem_limit_bytes=60 * 1024 * 1024),
        cost_estimate=pl.CostEstimate(
            flops=BACK_FLOPS * count // KV_HEADS, bytes_accessed=1000, transcendentals=0
        ),
        name=f"attend_back_{start}",
    )(order, own, rank, query, keys, back, out, lse)


def whole_call(kernel, name, flops, out_shape, *operands, near=False):
    single = not isinstance(out_shape, tuple)
    shapes = (out_shape,) if single else out_shape
    far = [] if near else [i for i, value in enumerate(operands) if value.ndim > 1]
    away = [] if near else list(range(len(shapes)))
    space = pl.BlockSpec(memory_space=pltpu.VMEM if near else pltpu.HBM)

    def staged(*refs):
        ins = list(refs[: len(operands)])
        outs = list(refs[len(operands) : len(operands) + len(shapes)])
        scratch = refs[len(operands) + len(shapes) :]
        copies = []
        for k, i in enumerate(far):
            copies.append(pltpu.make_async_copy(ins[i], scratch[k], scratch[-2].at[k]))
            ins[i] = scratch[k]
        for copy in copies:
            copy.start()
        for copy in copies:
            copy.wait()
        held = outs if near else list(scratch[len(far) : len(far) + len(away)])
        kernel(*ins, *held)
        copies = [
            pltpu.make_async_copy(held[k], outs[k], scratch[-1].at[k]) for k in away
        ]
        for copy in copies:
            copy.start()
        for copy in copies:
            copy.wait()

    scratch = [pltpu.VMEM(operands[i].shape, operands[i].dtype) for i in far]
    scratch += [pltpu.VMEM(shapes[k].shape, shapes[k].dtype) for k in away]
    if not near:
        scratch += [pltpu.SemaphoreType.DMA((len(far),)), pltpu.SemaphoreType.DMA((len(away),))]
    outs = pl.pallas_call(
        staged,
        out_shape=shapes,
        in_specs=[scalars() if value.ndim == 1 else space for value in operands],
        out_specs=(space,) * len(shapes),
        scratch_shapes=scratch,
        compiler_params=pltpu.CompilerParams(vmem_limit_bytes=(24 if near else 60) * 1024 * 1024),
        cost_estimate=pl.CostEstimate(flops=flops, bytes_accessed=1000, transcendentals=0),
        name=name,
    )(*operands)
    return outs[0] if single else outs


def stage_kernel(core_ref, qkv_ref, gains_ref, near_ref):
    first = core_ref[0] == 0
    shard = qkv_ref.shape[0]
    gains = jnp.concatenate(
        [gains_ref[...], jnp.zeros((6, gains_ref.shape[1]), jnp.float32)], axis=0
    )
    gains = jnp.concatenate([gains, jnp.zeros((8, 128 - shard), jnp.float32)], axis=1).T
    near = jnp.concatenate(
        [
            jnp.where(first, qkv_ref[:, : QKVW // 2], qkv_ref[:, QKVW // 2 :]),
            gains[:shard, :2],
            jnp.zeros((shard, PADDED - QKVW // 2 - 2), jnp.float32),
        ],
        axis=1,
    ).astype(low)
    for j in range(near_ref.shape[0]):
        near_ref[j] = near


def stage_feed_kernel(place_ref, expand_ref, down_ref, proj_ref, wide_ref, tall_ref):
    first = place_ref[0] == 0
    step = FF // 16
    parts = []
    for k in range(4):
        left = expand_ref[:, 2 * k * step : (2 * k + 1) * step]
        right = expand_ref[:, (2 * k + 1) * step : (2 * k + 2) * step]
        parts.append(jnp.where(first, left, right))
    proj = jnp.where(first, proj_ref[:, : D // 2], proj_ref[:, D // 2 :])
    quarter = proj[:, :PROJ]
    for k in range(1, 4):
        quarter = jnp.where(place_ref[2] == k, proj[:, k * PROJ : (k + 1) * PROJ], quarter)
    blank = jnp.zeros((proj.shape[0], BESIDE - FF // 4 - PROJ), jnp.float32)
    wide = jnp.concatenate(parts + [quarter, blank], axis=1).astype(low)
    tall = down_ref[...].astype(low)
    for j in range(wide_ref.shape[0]):
        wide_ref[j] = wide
        tall_ref[j] = tall


def stage_feed(place, expand, down, proj, groups):
    shard = expand.shape[0]
    half = down.shape[0] // 2
    outs = [(groups, shard, BESIDE), (groups, half, D)]
    return pl.pallas_call(
        stage_feed_kernel,
        grid_spec=pltpu.PrefetchScalarGridSpec(
            num_scalar_prefetch=1,
            grid=(1,),
            in_specs=[
                pl.BlockSpec((shard, HALF), lambda i, place: (0, place[1])),
                pl.BlockSpec((half, D), lambda i, place: (place[0], 0)),
                pl.BlockSpec(proj.shape, lambda i, place: (0, 0)),
            ],
            out_specs=[pl.BlockSpec(out, lambda i, place: (0, 0, 0)) for out in outs],
        ),
        out_shape=[jax.ShapeDtypeStruct(out, low) for out in outs],
        compiler_params=pltpu.CompilerParams(vmem_limit_bytes=60 * 1024 * 1024),
        cost_estimate=pl.CostEstimate(flops=1000, bytes_accessed=8 * 10**6, transcendentals=0),
        name="stage_feed",
    )(place, expand, down, proj)


def rotated(block, cosine, sine):
    first = block[: HEAD_DIM // 2]
    second = block[HEAD_DIM // 2 :]
    return [first * cosine - second * sine, second * cosine + first * sine]


def project_kernel(
    core_ref,
    rows_ref,
    mine_ref,
    theirs_ref,
    cosine_ref,
    sine_ref,
    normed_ref,
    query_ref,
    keys_ref,
    gains_ref,
):
    first_core = core_ref[0] == 0
    cosine = cosine_ref[...]
    sine = sine_ref[...]
    rows = rows_ref[...].astype(jnp.float32).T
    gains = mine_ref[:, PADDED - 128 : PADDED].astype(jnp.float32).T
    at = QKVW // 2 - (PADDED - 128)
    gains_ref[...] = gains[at : at + 2]
    normed = (rows * rms_scale(rows) * gains[at : at + 1]).astype(low)
    normed_ref[...] = normed
    near = contract(normed, mine_ref[...], 1, 0).T
    away = contract(normed, theirs_ref[...], 1, 0).T
    half = QKVW // 2
    one = jnp.where(first_core, near, away)[:half]
    two = jnp.where(first_core, away, near)[:half]
    mixed = jnp.concatenate([one, two], axis=0)
    scale = HEAD_DIM ** (-0.5) * LOG2E
    for h in range(HEADS):
        span = slice(h * HEAD_DIM, (h + 1) * HEAD_DIM)
        turned = jnp.concatenate(rotated(mixed[span], cosine, sine), axis=0)
        query_ref[span] = (turned * scale).astype(low)
    for g in range(KV_HEADS):
        at = D + g * HEAD_DIM
        to = at + KV_HEADS * HEAD_DIM
        pair = rotated(mixed[at : at + HEAD_DIM], cosine, sine) + [mixed[to : to + HEAD_DIM]]
        pair = jnp.concatenate(pair, axis=0).astype(low)
        for j in range(keys_ref.shape[0]):
            keys_ref[j, g] = pair


def join_proj(ref):
    return jnp.concatenate([ref[q, :, :PROJ] for q in range(4)], axis=1)


def rows_kernel(own_ref, other_ref, out_ref):
    out_ref[...] = jnp.concatenate([own_ref[...], other_ref[...]], axis=1).T


def branch_kernel(mixed_ref, beside_ref, out_ref, proj_ref, sem):
    copy = pltpu.make_async_copy(beside_ref.at[:, :, pl.ds(FF // 4, 128)], proj_ref, sem)
    copy.start()
    copy.wait()
    product = contract(mixed_ref[...], join_proj(proj_ref), 1, 0)
    blank = jnp.zeros((product.shape[0], 512 - product.shape[1]), jnp.float32)
    out_ref[...] = jnp.concatenate([product, blank], axis=1).astype(low)


def branch(mixed, beside):
    rows, width = mixed.shape
    whole = pl.BlockSpec(memory_space=pltpu.VMEM)
    return pl.pallas_call(
        branch_kernel,
        out_shape=(
            jax.ShapeDtypeStruct((rows, 512), low),
            jax.ShapeDtypeStruct((4, width, 128), low),
        ),
        in_specs=[whole, pl.BlockSpec(memory_space=pltpu.HBM)],
        out_specs=(whole, whole),
        scratch_shapes=[pltpu.SemaphoreType.DMA(())],
        compiler_params=pltpu.CompilerParams(vmem_limit_bytes=24 * 1024 * 1024),
        cost_estimate=pl.CostEstimate(flops=1000, bytes_accessed=1000, transcendentals=0),
        name="branch",
    )(mixed, beside)


def middle_kernel(
    core_ref,
    near_ref,
    away_ref,
    rows_ref,
    other_ref,
    gains_ref,
    mid_ref,
    normed_ref,
    normed_other,
):
    first_core = core_ref[0] == 0
    local = rows_ref.shape[1]
    for at, rows, out in ((0, rows_ref, normed_ref), (local, other_ref, normed_other)):
        near = near_ref[at : at + local, : D // 2].astype(jnp.float32)
        away = away_ref[local - at : 2 * local - at, : D // 2].astype(jnp.float32)
        near, away = jnp.where(first_core, near, away), jnp.where(first_core, away, near)
        middle = rows[...].astype(jnp.float32).T + jnp.concatenate([near, away], axis=1)
        if at == 0:
            mid_ref[...] = middle
        out[...] = (middle * rms_scale(middle) * gains_ref[1:2]).astype(low)


def turn_kernel(
    core_ref,
    own_ref,
    came_ref,
    mid_ref,
    back_ref,
    gains_ref,
    mine_ref,
    theirs_ref,
    out_ref,
    grad_ref,
    grad_out_ref,
    kept_ref,
    sent_ref,
    gain_grad_ref,
):
    first_core = core_ref[0] == 0
    normed = own_ref[...] + came_ref[...].astype(jnp.float32)
    middle = mid_ref[...]
    inverse = rms_scale(middle)
    scaled = normed * gains_ref[1:2]
    inner = jnp.mean(scaled * middle, axis=-1, keepdims=True)
    grad = back_ref[...].astype(jnp.float32) + inverse * (
        scaled - middle * inverse * inverse * inner
    )
    grad_ref[...] = grad
    gain_grad_ref[...] = jnp.sum(normed * middle * inverse, axis=0, keepdims=True)
    one = grad[:, : D // 2]
    two = grad[:, D // 2 :]
    near = jnp.where(first_core, one, two).astype(low)
    away = jnp.where(first_core, two, one).astype(low)
    grad_out = contract(near, join_proj(mine_ref), 1, 1) + contract(
        away, join_proj(theirs_ref), 1, 1
    )
    grad_out_ref[...] = grad_out.T.astype(low)
    product = contract(out_ref[...], grad.astype(low), 1, 0)
    groups, window, _ = kept_ref.shape
    shard = product.shape[0] // groups
    for j in range(groups):
        top = product[j * shard : j * shard + window]
        bottom = product[(j + 1) * shard - window : (j + 1) * shard]
        kept_ref[j] = jnp.where(first_core, top, bottom).astype(low)
        sent_ref[j] = jnp.where(first_core, bottom, top).astype(low)


def emit_kernel(mid_ref, own_ref, came_ref, out_ref):
    value = mid_ref[...] + own_ref[...] + came_ref[...].astype(jnp.float32)
    out_ref[...] = value.T.astype(low)


def feed_kernel(
    rows_one,
    rows_two,
    back_one,
    back_two,
    expand_ref,
    down_ref,
    fed_ref,
    fed_other_ref,
    normed_ref,
    normed_other_ref,
    tall_ref,
    expand_grad_ref,
    rows_ref,
    back_ref,
    columns_ref,
    fed_sum,
    normed_sum,
):
    local = rows_one.shape[0]
    h = pl.program_id(0)

    @pl.when(h == 0)
    def _():
        rows_ref[:local] = rows_one[...]
        rows_ref[local:] = rows_two[...]
        back_ref[:local] = back_one[...]
        back_ref[local:] = back_two[...]
        columns_ref[...] = rows_ref[...].T

    rows = rows_ref[...]
    back = back_ref[...]
    columns = columns_ref[...]
    down = down_ref[...]
    step = down_ref.shape[0]
    wide = jnp.concatenate([expand_ref[0], expand_ref[1]], axis=1)
    both = contract(rows, wide, 1, 0)
    gate = both[:, :step]
    upward = both[:, step:]
    sigmoid = jax.nn.sigmoid(gate)
    active = gate * sigmoid
    hidden = (active * upward).astype(low)
    grad_hidden = contract(back, down, 1, 1)
    grad_up = (grad_hidden * active).astype(low)
    grad_gate = (grad_hidden * upward * sigmoid * (1.0 + gate * (1.0 - sigmoid))).astype(low)
    fed = contract(hidden, down, 1, 0)
    grad_both = jnp.concatenate([grad_gate, grad_up], axis=1)
    normed = contract(grad_both, wide, 1, 1)
    product = contract(hidden.T, back, 1, 0)
    quarter = FF // 64
    for y in range(4):
        tall_ref[y] = jnp.concatenate(
            [product[(4 * j + y) * quarter : (4 * j + y + 1) * quarter] for j in range(4)], axis=0
        ).astype(low)
    both = contract(columns, grad_both, 1, 0).astype(low)
    expand_grad_ref[0] = both[:, :step]
    expand_grad_ref[1] = both[:, step:]

    @pl.when(h == 0)
    def _():
        fed_sum[...] = fed
        normed_sum[...] = normed

    @pl.when(h == 1)
    def _():
        fed_all = fed_sum[...] + fed
        normed_all = normed_sum[...] + normed
        fed_ref[...] = fed_all[:local]
        fed_other_ref[...] = fed_all[local:].astype(low)
        normed_ref[...] = normed_all[:local]
        normed_other_ref[...] = normed_all[local:].astype(low)


def feed(rows, back, expand, down):
    local, width = rows[0].shape
    step = FF // 4
    held = pl.BlockSpec((local, width), lambda h: (0, 0))
    pair = pl.BlockSpec((2, width, step), lambda h: (h, 0, 0))
    tall = pl.BlockSpec((step, width), lambda h: (h, 0))
    rows_out = pl.BlockSpec((4, FF // 16, width), lambda h: (0, h, 0))
    own = jax.ShapeDtypeStruct((local, width), jnp.float32)
    other = jax.ShapeDtypeStruct((local, width), low)
    return pl.pallas_call(
        feed_kernel,
        grid=(2,),
        out_shape=(
            own,
            other,
            own,
            other,
            jax.ShapeDtypeStruct((4, 8 * TALL, width), low),
            jax.ShapeDtypeStruct((4, width, step), low),
        ),
        in_specs=[held] * 4 + [pair, tall],
        out_specs=(held,) * 4 + (rows_out, pair),
        scratch_shapes=[
            pltpu.VMEM((2 * local, width), low),
            pltpu.VMEM((2 * local, width), low),
            pltpu.VMEM((width, 2 * local), low),
            pltpu.VMEM((2 * local, width), jnp.float32),
            pltpu.VMEM((2 * local, width), jnp.float32),
        ],
        compiler_params=pltpu.CompilerParams(vmem_limit_bytes=60 * 1024 * 1024),
        cost_estimate=pl.CostEstimate(flops=FEED_FLOPS, bytes_accessed=1000, transcendentals=0),
        name="feed",
    )(*rows, *back, expand, down)


def stack_kernel(tall_in, kept_ref, came_ref, tall_ref, held, sem):
    proj = (kept_ref[...].astype(jnp.float32) + came_ref[...].astype(jnp.float32)).astype(low)
    rows = proj.shape[1] // 4
    for y in range(4):
        held[y] = jnp.concatenate(
            [proj[j, y * rows : (y + 1) * rows] for j in range(proj.shape[0])], axis=0
        )
    span = pl.ds(tall_ref.shape[1] - held.shape[1], held.shape[1])
    copy = pltpu.make_async_copy(held, tall_ref.at[:, span], sem)
    copy.start()
    copy.wait()


def stack(tall, kept, came):
    groups, window, width = kept.shape
    away = pl.BlockSpec(memory_space=pltpu.HBM)
    whole = pl.BlockSpec(memory_space=pltpu.VMEM)
    return pl.pallas_call(
        stack_kernel,
        out_shape=jax.ShapeDtypeStruct(tall.shape, low),
        in_specs=[away, whole, whole],
        out_specs=away,
        scratch_shapes=[
            pltpu.VMEM((4, groups * window // 4, width), low),
            pltpu.SemaphoreType.DMA(()),
        ],
        input_output_aliases={0: 0},
        compiler_params=pltpu.CompilerParams(vmem_limit_bytes=60 * 1024 * 1024),
        cost_estimate=pl.CostEstimate(flops=1000, bytes_accessed=1000, transcendentals=0),
        name="stack",
    )(tall, kept, came)


def adam_step(master, first, second, grad, rate, decay):
    new_first = beta_first * first + (1.0 - beta_first) * grad
    new_second = beta_second * second + (1.0 - beta_second) * grad * grad
    fix_one = 1.0 - beta_first**STEP
    fix_two = 1.0 - beta_second**STEP
    update = new_first / fix_one / (jnp.sqrt(new_second / fix_two) + adam_eps) + decay * master
    return (master - rate * update, new_first, new_second)


def update_kernel(
    core_ref,
    wide_ref,
    wide_other,
    rest_ref,
    rest_other,
    gains_ref,
    gains_first,
    gains_second,
    *refs,
):
    states, outs, gain_outs = refs[:12], refs[12:24], refs[24:27]
    held = refs[27:31]
    near = refs[31:35]
    load_sem, store_sem, near_sem = refs[35:]
    grads = (wide_ref, wide_other, rest_ref, rest_other)
    fetches = [pltpu.make_async_copy(grads[k], near[k], near_sem.at[k]) for k in range(4)]
    wide_ref, wide_other, rest_ref, rest_other = near
    first_core = core_ref[0] == 0
    shard = gains_ref.shape[1]
    quarter = held[3].shape[1] // 8

    def both(mine, theirs):
        return (
            jnp.where(first_core, mine, theirs).astype(jnp.float32),
            jnp.where(first_core, theirs, mine).astype(jnp.float32),
        )

    def expand_grad(q):
        step = FF // 16
        one, two = both(rest_ref[q, :, : FF // 4], rest_other[q, :, : FF // 4])
        one, two = one[:shard], two[:shard]
        parts = []
        for k in range(4):
            span = slice(k * step, (k + 1) * step)
            parts += [one[:, span], two[:, span]]
        return jnp.concatenate(parts, axis=1)

    def tall_grads():
        parts = [both(rest_ref[q], rest_other[q]) for q in range(4)]
        one = [tall_part(part[0]) for part in parts]
        two = [tall_part(part[1]) for part in parts]
        down = jnp.concatenate([part[:quarter] for part in one + two], axis=0)
        proj = jnp.concatenate(
            [part[TALL - 16 :] for part in one]
            + [two[0][TALL - 8 :]]
            + [part[TALL - 16 :] for part in two[1:]],
            axis=0,
        )
        return down, proj

    def wide_grad():
        one, two = both(wide_ref[...], wide_other[...])
        half = QKVW // 2
        return jnp.concatenate([one[:shard, :half], two[:shard, :half]], axis=1)

    full = slice(None)
    pieces = [(2, pl.ds(i * HALF, HALF), 2.0 * D ** (-0.5)) for i in range(4)]
    pieces += [
        (3, full, 2.0 * FF ** (-0.5)),
        (1, full, 2.0 * (D // 8) ** (-0.5)),
        (0, full, 2.0 * D ** (-0.5)),
    ]

    def copies(p, out):
        weight, columns, _ = pieces[p]
        for k in range(3):
            near = held[weight].at[k, :, columns]
            if out:
                yield pltpu.make_async_copy(
                    near, outs[3 * weight + k].at[:, columns], store_sem.at[p, k]
                )
            else:
                yield pltpu.make_async_copy(
                    states[3 * weight + k].at[:, columns], near, load_sem.at[p, k]
                )

    for copy in fetches:
        copy.start()
    for p in range(len(pieces)):
        for copy in copies(p, False):
            copy.start()
    for copy in fetches:
        copy.wait()
    down, proj = tall_grads()
    for p, (weight, columns, rate) in enumerate(pieces):
        for copy in copies(p, False):
            copy.wait()
        if p < 4:
            grad = expand_grad(p % 2 * 2 + p // 2)
        else:
            grad = (down, proj)[p - 4] if p < 6 else wide_grad()
        new = adam_step(*[held[weight][k, :, columns] for k in range(3)], grad, rate, 0.1)
        for k in range(3):
            held[weight][k, :, columns] = new[k]
        for copy in copies(p, True):
            copy.start()
    one, two = both(wide_ref[...], wide_other[...])
    grad = one[shard : shard + 2, :shard] + two[shard : shard + 2, :shard]
    new = adam_step(gains_ref[...], gains_first[...], gains_second[...], grad, 1.0, 0.0)
    for out, value in zip(gain_outs, new):
        out[...] = value
    for p in range(len(pieces)):
        for copy in copies(p, True):
            copy.wait()


def update(core, wide, wide_other, rest, rest_other, gains, states):
    whole = pl.BlockSpec(memory_space=pltpu.VMEM)
    away = pl.BlockSpec(memory_space=pltpu.HBM)
    shapes = [jax.ShapeDtypeStruct(value.shape, jnp.float32) for value in states + gains]
    return pl.pallas_call(
        update_kernel,
        out_shape=shapes,
        in_specs=[scalars()] + [away] * 4 + [whole] * 3 + [away] * 12,
        out_specs=[away] * 12 + [whole] * 3,
        scratch_shapes=[
            pltpu.VMEM((3,) + states[3 * weight].shape, jnp.float32) for weight in range(4)
        ]
        + [pltpu.VMEM(value.shape, low) for value in (wide, wide, rest, rest)]
        + [pltpu.SemaphoreType.DMA(shape) for shape in ((7, 3), (7, 3), (4,))],
        compiler_params=pltpu.CompilerParams(vmem_limit_bytes=32 * 1024 * 1024),
        cost_estimate=pl.CostEstimate(
            flops=1000, bytes_accessed=30 * 10**6, transcendentals=0
        ),
        name="update",
    )(core, wide, wide_other, rest, rest_other, *gains, *states)


def back_rotated(block, cosine, sine):
    first = block[: HEAD_DIM // 2]
    second = block[HEAD_DIM // 2 :]
    return [first * cosine + second * sine, second * cosine - first * sine]


def late_kernel(
    core_ref,
    first_terms,
    second_terms,
    first_dq,
    second_dq,
    cosine_ref,
    sine_ref,
    mine_ref,
    theirs_ref,
    rows_ref,
    grad_ref,
    gain_ref,
    gain_grad_ref,
    out_ref,
    near_ref,
    away_ref,
    gains_ref,
):
    cosine = cosine_ref[...]
    sine = sine_ref[...]
    first_core = core_ref[0] == 0
    parts = []
    for ref in (first_dq, second_dq):
        for h in range(ref.shape[0] // HEAD_DIM):
            parts += back_rotated(ref[h * HEAD_DIM : (h + 1) * HEAD_DIM], cosine, sine)
    values = []
    for ref in (first_terms, second_terms):
        for g in range(ref.shape[1]):
            block = ref[0, g].astype(jnp.float32)
            for j in range(1, ref.shape[0]):
                block = block + ref[j, g].astype(jnp.float32)
            block = block.T
            parts += back_rotated(block[:HEAD_DIM], cosine, sine)
            values.append(block[HEAD_DIM:])
    mixed = jnp.concatenate(parts + values, axis=0)
    half = QKVW // 2
    blank = jnp.zeros((PADDED - half, mixed.shape[1]), jnp.float32)
    one = mixed[:half]
    two = mixed[half:]
    near = jnp.concatenate([jnp.where(first_core, one, two), blank], axis=0).T.astype(low)
    away = jnp.concatenate([jnp.where(first_core, two, one), blank], axis=0).T.astype(low)
    grad_normed = contract(near, mine_ref[...], 1, 1) + contract(away, theirs_ref[...], 1, 1)
    rows = rows_ref[...].astype(jnp.float32).T
    inverse = rms_scale(rows)
    scaled = grad_normed * gain_ref[0:1]
    inner = jnp.mean(scaled * rows, axis=-1, keepdims=True)
    back = inverse * (scaled - rows * inverse * inverse * inner)
    out_ref[...] = (grad_ref[...] + back).T.astype(low)
    gain_one = jnp.sum(grad_normed * rows * inverse, axis=0, keepdims=True)
    gains = (gain_one, gain_grad_ref[...])
    near_ref[...] = near
    away_ref[...] = away
    gains_ref[...] = jnp.concatenate(gains, axis=0)


def weight_kernel(normed_ref, normed_other, near_ref, came_ref, gains_ref, out_ref):
    columns = jnp.concatenate([normed_ref[...], normed_other[...]], axis=0).T
    product = contract(columns, jnp.concatenate([near_ref[...], came_ref[...]], axis=0), 1, 0)
    groups = out_ref.shape[0]
    shard = product.shape[0] // groups
    lanes = product.shape[1]
    gains = gains_ref[...]
    for j in range(groups):
        span = slice(j * shard, (j + 1) * shard)
        tail = padded_rows(gains[:, span], 128 - shard)
        tail = jnp.concatenate(
            [tail, jnp.zeros((128 - shard, lanes - shard), jnp.float32)], axis=1
        )
        out_ref[j] = jnp.concatenate([product[span], tail], axis=0).astype(low)


def pack_late_kernel(weight_ref, tall_ref, out_ref):
    groups = weight_ref.shape[0]
    quarter = FF // 64
    down = tall_ref[: groups * quarter].astype(jnp.float32)
    proj = tall_ref[groups * quarter :].astype(jnp.float32)
    for j in range(groups):
        tall = jnp.concatenate(
            [down[j * quarter : (j + 1) * quarter], proj[j * 16 : (j + 1) * 16]], axis=0
        )
        halves = [
            jnp.concatenate([padded_rows(tall[:, span], 64) for span in spans], axis=0)
            for spans in (TALL_NARROW, TALL_WIDE)
        ]
        weight = weight_ref[j].astype(jnp.float32)[:, : QKVW // 2]
        put_halves(out_ref, j, jnp.concatenate([weight] + halves, axis=1))


def padded_rows(block, rows):
    return jnp.concatenate(
        [block, jnp.zeros((rows - block.shape[0], block.shape[1]), jnp.float32)], axis=0
    )


def put_halves(out_ref, j, block):
    groups = out_ref.shape[0] // 2
    rows = out_ref.shape[1]
    for half in range(2):
        out_ref[half * groups + j] = block[half * rows : (half + 1) * rows].astype(low)


def pack_early_kernel(expand_ref, out_ref):
    for j in range(expand_ref.shape[0]):
        put_halves(out_ref, j, padded_rows(expand_ref[j].astype(jnp.float32), 128))


def sum_kernel(early_ref, late_ref, out_ref):
    sums = []
    for ref in (early_ref, late_ref):
        block = ref[0].astype(jnp.float32)
        for j in range(1, ref.shape[0]):
            block = block + ref[j].astype(jnp.float32)
        sums.append(block.astype(low))
    block = jnp.concatenate(sums, axis=1)
    for j in range(out_ref.shape[0]):
        out_ref[j] = block


def finish_kernel(all_ref, wide_ref, rest_ref):
    count = all_ref.shape[0] // 2
    rows = all_ref.shape[1]
    expand = slice(0, FF // 4)
    wide = slice(FF // 4, FF // 4 + PADDED)
    tall = slice(FF // 4 + LATE - 512, FF // 4 + LATE)
    for half in range(2):
        span = slice(half * rows, (half + 1) * rows)
        block = all_ref[half * count, :, wide].astype(jnp.float32)
        for y in range(1, count):
            block = block + all_ref[half * count + y, :, wide].astype(jnp.float32)
        wide_ref[span] = block.astype(low)
        for y in range(count):
            rest_ref[y, span] = jnp.concatenate(
                [all_ref[half * count + y, :, lanes] for lanes in (expand, tall)], axis=1
            )


def tall_part(rest):
    parts = []
    for lanes in (slice(FF // 4 + 128, FF // 4 + 512), slice(FF // 4 + 32, FF // 4 + 128)):
        parts += [rest[at : at + TALL, lanes] for at in (0, rest.shape[0] // 2)]
    return jnp.concatenate(parts, axis=1)


def on_device(
    inputs,
    cotangent,
    span_order,
    w_qkv,
    qkv_first,
    qkv_second,
    w_proj,
    proj_first,
    proj_second,
    w_expand,
    expand_first,
    expand_second,
    w_down,
    down_first,
    down_second,
    gains,
    gains_first,
    gains_second,
):
    core = lax.axis_index("core")
    rank = lax.axis_index(CTX)
    groups = 8
    batch, local, width = inputs.shape
    shard = w_qkv.shape[0]
    hidden_shard = w_down.shape[0] // 2

    y = lax.axis_index("y")
    place = jnp.stack([core, y % 2 * 2 + y // 2, y]).astype(jnp.int32)
    core_at = place[:1]
    rank_at = rank.reshape(1).astype(jnp.int32)
    near = whole_call(
        stage_kernel,
        "stage",
        1000,
        jax.ShapeDtypeStruct((groups, shard, NEAR), low),
        core_at,
        w_qkv,
        gains,
    )
    mine = exchange(near, CTX).reshape(width, NEAR)
    expand_low, down_low = stage_feed(place, w_expand, w_down, w_proj, groups)
    back_rows = cotangent.reshape(local, width)
    order_own = lax.dynamic_slice_in_dim(span_order, 2 * rank, 2)
    own_pos = (
        order_own[:, None] * (local // 2) + jnp.arange(local // 2, dtype=jnp.int32)
    ).reshape(local)
    cosine, sine = rope_tables(own_pos)
    mine, cosine, sine, expand_low, down_low, back_rows = lax.optimization_barrier(
        (mine, cosine, sine, expand_low, down_low, back_rows)
    )
    theirs = swap_cores(mine)
    expand_low = exchange(expand_low, CTX).reshape(width, BESIDE)

    tokens = inputs.reshape(local, width).T
    square = (local, width)
    normed_one, query, all_keys, full_gains = whole_call(
        project_kernel,
        "project",
        1000,
        (
            jax.ShapeDtypeStruct(square, low),
            jax.ShapeDtypeStruct((width, local), low),
            jax.ShapeDtypeStruct((groups, KV_HEADS, 2 * HEAD_DIM, local), low),
            jax.ShapeDtypeStruct((2, width), jnp.float32),
        ),
        core_at,
        tokens,
        mine,
        theirs,
        cosine,
        sine,
    )
    all_keys, expand_low = lax.optimization_barrier((all_keys, expand_low))
    expand_low = lax.all_gather(expand_low, "y", axis=0, tiled=False)
    all_keys = exchange(all_keys, CTX)
    all_keys, down_low = lax.optimization_barrier((all_keys, down_low))
    normed_other = swap_cores(normed_one)
    tokens_other = swap_cores(tokens)
    half_down = exchange(down_low, CTX).reshape(HALF, width)
    attended, lse = attend(span_order, order_own, rank_at, query, all_keys)
    mixed = whole_call(
        rows_kernel,
        "rows",
        1000,
        jax.ShapeDtypeStruct((2 * local, width), low),
        attended,
        swap_cores(attended),
        near=True,
    )
    mixed, expand_low = lax.optimization_barrier((mixed, expand_low))
    mixed, proj_mine = branch(mixed, expand_low)
    middle, normed_two, normed_two_other = whole_call(
        middle_kernel,
        "middle",
        1000,
        (
            jax.ShapeDtypeStruct(square, jnp.float32),
            jax.ShapeDtypeStruct(square, low),
            jax.ShapeDtypeStruct(square, low),
        ),
        core_at,
        mixed,
        swap_cores(mixed),
        tokens,
        tokens_other,
        full_gains,
    )
    proj_theirs = swap_cores(proj_mine)
    normed_two, half_down = lax.optimization_barrier((normed_two, half_down))

    fed, fed_other, grad_normed, grad_other, tall, grad_expand = feed(
        (normed_two, normed_two_other),
        (back_rows, swap_cores(back_rows)),
        expand_low,
        half_down,
    )
    grad_middle, grad_att, proj_kept, proj_sent, gain_grad_two = whole_call(
        turn_kernel,
        "turn",
        3 * 10**9,
        (
            jax.ShapeDtypeStruct(square, jnp.float32),
            jax.ShapeDtypeStruct((width, local), low),
            jax.ShapeDtypeStruct((groups, 64, width), low),
            jax.ShapeDtypeStruct((groups, 64, width), low),
            jax.ShapeDtypeStruct((1, width), jnp.float32),
        ),
        core_at,
        grad_normed,
        swap_cores(grad_other),
        middle,
        back_rows,
        full_gains,
        proj_mine,
        proj_theirs,
        attended,
    )
    output = whole_call(
        emit_kernel,
        "emit",
        1000,
        jax.ShapeDtypeStruct((width, local), low),
        middle,
        fed,
        swap_cores(fed_other),
    )

    expand_sum = lax.psum_scatter(grad_expand, "y", scatter_dimension=0, tiled=False)
    context = (span_order, order_own, rank_at, query, all_keys, grad_att, attended, lse)
    first_query, first_terms = attend_back(0, SPLIT, *context)
    first_terms, tall = lax.optimization_barrier((first_terms, tall))
    first_terms = exchange(first_terms, CTX)
    grad_query, key_terms = attend_back(SPLIT, KV_HEADS - SPLIT, *context)
    key_terms = exchange(key_terms, CTX)
    early = whole_call(
        pack_early_kernel,
        "pack_early",
        1000,
        jax.ShapeDtypeStruct((2 * groups, 64, FF // 4), low),
        expand_sum.reshape(groups, shard, FF // 4),
    )
    key_terms, first_terms, output, early = lax.optimization_barrier(
        (key_terms, first_terms, output, early)
    )
    early = exchange(early, CHIP_CTX)
    tall = stack(tall, proj_kept, swap_cores(proj_sent))
    tall = lax.psum_scatter(tall, "y", scatter_dimension=0, tiled=False)
    half = jax.ShapeDtypeStruct((local, PADDED), low)
    input_grad, near, away, late_gains = whole_call(
        late_kernel,
        "late",
        30 * 10**9,
        (
            jax.ShapeDtypeStruct((width, local), low),
            half,
            half,
            jax.ShapeDtypeStruct((2, width), jnp.float32),
        ),
        core_at,
        first_terms,
        key_terms,
        first_query,
        grad_query,
        cosine,
        sine,
        mine,
        theirs,
        tokens,
        grad_middle,
        full_gains,
        gain_grad_two,
    )
    late = whole_call(
        weight_kernel,
        "weight",
        1000,
        jax.ShapeDtypeStruct((groups, 128, PADDED), low),
        normed_one,
        normed_other,
        near,
        swap_cores(away),
        late_gains,
    )
    late = whole_call(
        pack_late_kernel,
        "pack_late",
        1000,
        jax.ShapeDtypeStruct((2 * groups, 64, LATE), low),
        late,
        tall.reshape(groups * TALL, width),
    )
    late, early = lax.optimization_barrier((late, early))
    late = exchange(late, CHIP_CTX)
    parts = whole_call(
        sum_kernel,
        "sum_parts",
        1000,
        jax.ShapeDtypeStruct((8, 64, FF // 4 + LATE), low),
        early,
        late,
        near=True,
    )
    wide, rest = whole_call(
        finish_kernel,
        "finish",
        1000,
        (
            jax.ShapeDtypeStruct((128, PADDED), low),
            jax.ShapeDtypeStruct((4, 128, FF // 4 + 512), low),
        ),
        exchange(parts, CHIPS),
        near=True,
    )
    wide_other = swap_cores(wide)
    rest_other = swap_cores(rest)
    news = update(
        core_at,
        wide,
        wide_other,
        rest,
        rest_other,
        [gains, gains_first, gains_second],
        [
            w_qkv,
            qkv_first,
            qkv_second,
            w_proj,
            proj_first,
            proj_second,
            w_expand,
            expand_first,
            expand_second,
            w_down,
            down_first,
            down_second,
        ],
    )
    return (
        output.T.reshape(batch, local, width),
        input_grad.T.reshape(batch, local, width),
        *news,
    )


def solution(mesh):
    parts = jax.sharding.Mesh(mesh.devices.reshape(2, 4, 2, 2, 4), AXES)
    dp, ctx = ("zh", "y", "core"), CTX
    rows = P(dp, ctx, None)
    owned = P(ctx, None)
    split = P(None, ctx)
    return jax.shard_map(
        on_device,
        mesh=parts,
        in_specs=(rows, rows, P()) + (owned,) * 12 + (split,) * 3,
        out_specs=(rows, rows) + (owned,) * 12 + (split,) * 3,
        check_vma=False,
    )
```
